32 devices in a mesh: wide: 8 (over y, x, core), narrow: 4 (over z).
Axes of the slice: x: 2, y: 2, z: 4, core: 2. Of those that a mesh axis runs over, the one named last changes fastest.
Arguments:
- patches: bfloat16 [32, 256, 16], P('wide'), may hold values from -6 to 6
- target_noise: float32 [32, 256, 16], P('wide'), may hold values from -6 to 6
- kept_slots: int32 [32, 160], P('wide'), may hold values from 0 to 255, as said below
- kept_count: int32 [32], P('wide'), may hold values from 80 to 160, as said below
- time_step: int32 [32], P('wide'), may hold values from 0 to 999
- labels: int32 [32], P('wide'), may hold values from 0 to 999
- teacher: float32 [32, 1152], P('wide'), may hold values from -6 to 6
- attend_in: float32 [2, 1152, 3, 1152], P(None, 'wide', None, 'narrow'), may hold values from -0.1875 to 0.1875
- attend_out: float32 [2, 1152, 1152], P(None, 'narrow', 'wide'), may hold values from -0.5 to 0.5
- expand: float32 [2, 1152, 4608], P(None, 'wide', 'narrow'), may hold values from -0.1875 to 0.1875
- contract: float32 [2, 4608, 1152], P(None, 'narrow', 'wide'), may hold values from -0.09375 to 0.09375
- modulation: float32 [2, 1152, 6, 1152], P(None, 'wide', None, 'narrow'), may hold values from -0.1875 to 0.1875
- patch_table: float32 [33, 1152], P(None, 'narrow'), may hold values from -0.1875 to 0.1875
- condition: float32 [1256, 1152], P(None, 'narrow'), may hold values from -0.375 to 0.375
- moment_attend_in: float32 [2, 1152, 3, 1152], P(None, 'wide', None, 'narrow'), may hold values from -3.33786e-06 to 3.33786e-06
- moment_attend_out: float32 [2, 1152, 1152], P(None, 'narrow', 'wide'), may hold values from -3.33786e-06 to 3.33786e-06
- moment_expand: float32 [2, 1152, 4608], P(None, 'wide', 'narrow'), may hold values from -1.9073486e-06 to 1.9073486e-06
- moment_contract: float32 [2, 4608, 1152], P(None, 'narrow', 'wide'), may hold values from -3.33786e-06 to 3.33786e-06
- moment_modulation: float32 [2, 1152, 6, 1152], P(None, 'wide', None, 'narrow'), may hold values from -3.33786e-06 to 3.33786e-06
- moment_patch: float32 [33, 1152], P(None, 'narrow'), may hold values from -4.7683716e-06 to 4.7683716e-06
- moment_condition: float32 [1256, 1152], P(None, 'narrow'), may hold values from -4.7683716e-06 to 4.7683716e-06
- second_attend_in: float32 [2, 1152, 3, 1152], P(None, 'wide', None, 'narrow'), may hold values from 2.5375211e-14 to 1.01500846e-13
- second_attend_out: float32 [2, 1152, 1152], P(None, 'narrow', 'wide'), may hold values from 2.5375211e-14 to 1.01500846e-13
- second_expand: float32 [2, 1152, 4608], P(None, 'wide', 'narrow'), may hold values from 1.0150085e-14 to 4.060034e-14
- second_contract: float32 [2, 4608, 1152], P(None, 'narrow', 'wide'), may hold values from 2.5375211e-14 to 1.01500846e-13
- second_modulation: float32 [2, 1152, 6, 1152], P(None, 'wide', None, 'narrow'), may hold values from 2.5375211e-14 to 1.01500846e-13
- second_patch: float32 [33, 1152], P(None, 'narrow'), may hold values from 5.0750423e-14 to 2.0300169e-13
- second_condition: float32 [1256, 1152], P(None, 'narrow'), may hold values from 5.0750423e-14 to 2.0300169e-13
- average_attend_in: float32 [2, 1152, 3, 1152], P(None, 'wide', None, 'narrow'), may hold values from -0.1875 to 0.1875
- average_attend_out: float32 [2, 1152, 1152], P(None, 'narrow', 'wide'), may hold values from -0.5 to 0.5
- average_expand: float32 [2, 1152, 4608], P(None, 'wide', 'narrow'), may hold values from -0.1875 to 0.1875
- average_contract: float32 [2, 4608, 1152], P(None, 'narrow', 'wide'), may hold values from -0.09375 to 0.09375
- average_modulation: float32 [2, 1152, 6, 1152], P(None, 'wide', None, 'narrow'), may hold values from -0.1875 to 0.1875
- average_patch: float32 [33, 1152], P(None, 'narrow'), may hold values from -0.1875 to 0.1875
- average_condition: float32 [1256, 1152], P(None, 'narrow'), may hold values from -0.375 to 0.375
Outputs:
- loss_parts: float32 [2], replicated
- grad_norm: float32 [], replicated
- new_attend_in: float32 [2, 1152, 3, 1152], P(None, 'wide', None, 'narrow')
- new_attend_out: float32 [2, 1152, 1152], P(None, 'narrow', 'wide')
- new_expand: float32 [2, 1152, 4608], P(None, 'wide', 'narrow')
- new_contract: float32 [2, 4608, 1152], P(None, 'narrow', 'wide')
- new_modulation: float32 [2, 1152, 6, 1152], P(None, 'wide', None, 'narrow')
- new_patch: float32 [33, 1152], P(None, 'narrow')
- new_condition: float32 [1256, 1152], P(None, 'narrow')
- next_moment_attend_in: float32 [2, 1152, 3, 1152], P(None, 'wide', None, 'narrow')
- next_moment_attend_out: float32 [2, 1152, 1152], P(None, 'narrow', 'wide')
- next_moment_expand: float32 [2, 1152, 4608], P(None, 'wide', 'narrow')
- next_moment_contract: float32 [2, 4608, 1152], P(None, 'narrow', 'wide')
- next_moment_modulation: float32 [2, 1152, 6, 1152], P(None, 'wide', None, 'narrow')
- next_moment_patch: float32 [33, 1152], P(None, 'narrow')
- next_moment_condition: float32 [1256, 1152], P(None, 'narrow')
- next_second_attend_in: float32 [2, 1152, 3, 1152], P(None, 'wide', None, 'narrow')
- next_second_attend_out: float32 [2, 1152, 1152], P(None, 'narrow', 'wide')
- next_second_expand: float32 [2, 1152, 4608], P(None, 'wide', 'narrow')
- next_second_contract: float32 [2, 4608, 1152], P(None, 'narrow', 'wide')
- next_second_modulation: float32 [2, 1152, 6, 1152], P(None, 'wide', None, 'narrow')
- next_second_patch: float32 [33, 1152], P(None, 'narrow')
- next_second_condition: float32 [1256, 1152], P(None, 'narrow')
- next_average_attend_in: float32 [2, 1152, 3, 1152], P(None, 'wide', None, 'narrow')
- next_average_attend_out: float32 [2, 1152, 1152], P(None, 'narrow', 'wide')
- next_average_expand: float32 [2, 1152, 4608], P(None, 'wide', 'narrow')
- next_average_contract: float32 [2, 4608, 1152], P(None, 'narrow', 'wide')
- next_average_modulation: float32 [2, 1152, 6, 1152], P(None, 'wide', None, 'narrow')
- next_average_patch: float32 [33, 1152], P(None, 'narrow')
- next_average_condition: float32 [1256, 1152], P(None, 'narrow')
The draws below stay inside these ranges and needn't reach their ends.
Inputs may be any that keep to these rules, and one draw needn't show every extreme that they name: `kept_slots`: within one image the 160 slots hold distinct positions. `kept_count`: some image holds exactly 160 kept tokens.
All inputs are finite; a program needn't handle non-finite values.
Results may differ from the reference program's by a relative error of at most 0.02.
Values may be sent and summed in bfloat16 or wider, within the bound.
A program may use at most 256 MiB of HBM per device.

```python
import math
import jax
import jax.numpy as jnp
from jax import lax

D = 1152
FF = 4608
HEAD_DIM = 72
CLASSES = 1000
FREQ = 256
PATCH_IN = 16
LEN = 256
CAP = 160
STEP = 10
IMAGES = 32
PARAMS = 49260672


def draw_kept_slots(key, part):
    key = jax.random.fold_in(key, 11)
    keys = jax.random.split(key, IMAGES)
    orders = jax.vmap(lambda single: jax.random.permutation(single, LEN))(keys)
    return orders[:, :CAP].astype(jnp.int32)


def draw_kept_count(key, part):
    key = jax.random.fold_in(key, 23)
    counts_key, fullest_key = jax.random.split(key)
    counts = jax.random.randint(counts_key, (IMAGES,), CAP // 2, CAP + 1)
    fullest = jax.random.randint(fullest_key, (), 0, IMAGES)
    return jnp.where(jnp.arange(IMAGES) == fullest, CAP, counts).astype(jnp.int32)


def set_ends(array, rng, smallest, high):
    index_at = [jax.random.randint(jax.random.fold_in(rng, axis), (), 0, length) for axis, length in enumerate(array.shape)]
    main_axis = array.shape.index(max(array.shape))
    next_to = index_at[:main_axis] + [(index_at[main_axis] + 1) % array.shape[main_axis]] + index_at[main_axis + 1:]
    return array.at[tuple(index_at)].set(smallest).at[tuple(next_to)].set(high)


def block_scale(stream_key, dims, cuts, least, high):
    factor_of = 1.0
    for dim, blocks in cuts:
        draws = jax.random.uniform(jax.random.fold_in(jax.random.fold_in(stream_key, 6), dim), (blocks,), jnp.float32, least / len(cuts), high / len(cuts))
        factor_of = factor_of * jnp.repeat(jnp.exp(draws), dims[dim] // blocks).reshape((-1,) + (1,) * (len(dims) - 1 - dim))
    return factor_of


def noise(rng, extent, deviation, reach, cuts=(), held_as=jnp.bfloat16):
    array = deviation * jax.random.normal(rng, extent, jnp.float32)
    if cuts:
        array = array * block_scale(rng, extent, cuts, -0.22, 0.18)
    return jnp.clip(array, -reach, reach).astype(held_as)


def setup_inputs(seed: int = 0) -> dict:
    key_of = jax.random.split(jax.random.key(seed), 36)
    return {
        "patches": noise(key_of[0], (IMAGES, LEN, PATCH_IN), 1.0, 6.0, ((0, 8),)),
        "target_noise": noise(key_of[1], (IMAGES, LEN, PATCH_IN), 1.0, 6.0, ((0, 8),), jnp.float32),
        "kept_slots": draw_kept_slots(jax.random.fold_in(key_of[35], 71), 0),
        "kept_count": draw_kept_count(jax.random.fold_in(key_of[35], 71), 0),
        "time_step": set_ends(jax.random.randint(key_of[4], (IMAGES,), 0, 1000), jax.random.fold_in(key_of[4], 1), 0, 999).astype(jnp.int32),
        "labels": set_ends(jax.random.randint(key_of[5], (IMAGES,), 0, CLASSES), jax.random.fold_in(key_of[5], 1), 0, CLASSES - 1).astype(jnp.int32),
        "teacher": noise(key_of[6], (IMAGES, D), 1.0, 6.0, ((0, 8),), jnp.float32),
        "attend_in": noise(key_of[7], (2, D, 3, D), D ** -0.5, 0.1875, ((1, 8), (3, 4)), jnp.float32),
        "attend_out": noise(key_of[8], (2, D, D), (D // 8) ** -0.5, 0.5, ((1, 4), (2, 8)), jnp.float32),
        "expand": noise(key_of[9], (2, D, FF), D ** -0.5, 0.1875, ((1, 8), (2, 4)), jnp.float32),
        "contract": noise(key_of[10], (2, FF, D), FF ** -0.5, 0.09375, ((1, 4), (2, 8)), jnp.float32),
        "modulation": noise(key_of[11], (2, D, 6, D), D ** -0.5, 0.1875, ((1, 8), (3, 4)), jnp.float32),
        "patch_table": noise(key_of[12], (2 * PATCH_IN + 1, D), D ** -0.5, 0.1875, ((1, 4),), jnp.float32),
        "condition": noise(key_of[13], (FREQ + CLASSES, D), FREQ ** -0.5, 0.375, ((1, 4),), jnp.float32),
        "moment_attend_in": noise(key_of[14], (2, D, 3, D), (0.11 * 0.05 * 0.7 / PARAMS ** 0.5), 3.337860107421875e-06, ((1, 8), (3, 4)), jnp.float32),
        "moment_attend_out": noise(key_of[15], (2, D, D), (0.11 * 0.05 * 0.7 / PARAMS ** 0.5), 3.337860107421875e-06, ((1, 4), (2, 8)), jnp.float32),
        "moment_expand": noise(key_of[16], (2, D, FF), (0.11 * 0.05 * 0.45 / PARAMS ** 0.5), 1.9073486328125e-06, ((1, 8), (2, 4)), jnp.float32),
        "moment_contract": noise(key_of[17], (2, FF, D), (0.11 * 0.05 * 0.7 / PARAMS ** 0.5), 3.337860107421875e-06, ((1, 4), (2, 8)), jnp.float32),
        "moment_modulation": noise(key_of[18], (2, D, 6, D), (0.11 * 0.05 * 0.7 / PARAMS ** 0.5), 3.337860107421875e-06, ((1, 8), (3, 4)), jnp.float32),
        "moment_patch": noise(key_of[19], (2 * PATCH_IN + 1, D), (0.11 * 0.05 / PARAMS ** 0.5), 4.76837158203125e-06, ((1, 4),), jnp.float32),
        "moment_condition": noise(key_of[20], (FREQ + CLASSES, D), (0.11 * 0.05 / PARAMS ** 0.5), 4.76837158203125e-06, ((1, 4),), jnp.float32),
        "second_attend_in": jnp.clip(jnp.exp(math.log(1.0150084576001153e-13) - 1.3862944 * jax.random.uniform(key_of[21], (2, D, 3, D), jnp.float32) ** block_scale(key_of[21], (2, D, 3, D), ((1, 8), (3, 4)), -0.2, 0.2)), 2.5375211440002883e-14, 1.0150084576001153e-13),
        "second_attend_out": jnp.clip(jnp.exp(math.log(1.0150084576001153e-13) - 1.3862944 * jax.random.uniform(key_of[22], (2, D, D), jnp.float32) ** block_scale(key_of[22], (2, D, D), ((1, 4), (2, 8)), -0.2, 0.2)), 2.5375211440002883e-14, 1.0150084576001153e-13),
        "second_expand": jnp.clip(jnp.exp(math.log(4.060033898163097e-14) - 1.3862944 * jax.random.uniform(key_of[23], (2, D, FF), jnp.float32) ** block_scale(key_of[23], (2, D, FF), ((1, 8), (2, 4)), -0.2, 0.2)), 1.0150084745407743e-14, 4.060033898163097e-14),
        "second_contract": jnp.clip(jnp.exp(math.log(1.0150084576001153e-13) - 1.3862944 * jax.random.uniform(key_of[24], (2, FF, D), jnp.float32) ** block_scale(key_of[24], (2, FF, D), ((1, 4), (2, 8)), -0.2, 0.2)), 2.5375211440002883e-14, 1.0150084576001153e-13),
        "second_modulation": jnp.clip(jnp.exp(math.log(1.0150084576001153e-13) - 1.3862944 * jax.random.uniform(key_of[25], (2, D, 6, D), jnp.float32) ** block_scale(key_of[25], (2, D, 6, D), ((1, 8), (3, 4)), -0.2, 0.2)), 2.5375211440002883e-14, 1.0150084576001153e-13),
        "second_patch": jnp.clip(jnp.exp(math.log(2.0300169152002306e-13) - 1.3862944 * jax.random.uniform(key_of[26], (2 * PATCH_IN + 1, D), jnp.float32) ** block_scale(key_of[26], (2 * PATCH_IN + 1, D), ((1, 4),), -0.2, 0.2)), 5.0750422880005766e-14, 2.0300169152002306e-13),
        "second_condition": jnp.clip(jnp.exp(math.log(2.0300169152002306e-13) - 1.3862944 * jax.random.uniform(key_of[27], (FREQ + CLASSES, D), jnp.float32) ** block_scale(key_of[27], (FREQ + CLASSES, D), ((1, 4),), -0.2, 0.2)), 5.0750422880005766e-14, 2.0300169152002306e-13),
        "average_attend_in": noise(key_of[28], (2, D, 3, D), D ** -0.5, 0.1875, ((1, 8), (3, 4)), jnp.float32),
        "average_attend_out": noise(key_of[29], (2, D, D), (D // 8) ** -0.5, 0.5, ((1, 4), (2, 8)), jnp.float32),
        "average_expand": noise(key_of[30], (2, D, FF), D ** -0.5, 0.1875, ((1, 8), (2, 4)), jnp.float32),
        "average_contract": noise(key_of[31], (2, FF, D), FF ** -0.5, 0.09375, ((1, 4), (2, 8)), jnp.float32),
        "average_modulation": noise(key_of[32], (2, D, 6, D), D ** -0.5, 0.1875, ((1, 8), (3, 4)), jnp.float32),
        "average_patch": noise(key_of[33], (2 * PATCH_IN + 1, D), D ** -0.5, 0.1875, ((1, 4),), jnp.float32),
        "average_condition": noise(key_of[34], (FREQ + CLASSES, D), FREQ ** -0.5, 0.375, ((1, 4),), jnp.float32),
    }


highest_float_accuracy = lax.Precision.HIGHEST
norm_eps = 1e-06
contrast_sharpness_divisor = 0.02
nce_weight = 0.5
learn_rate = 0.05
beta_first = 0.9
beta_second = 0.999
adam_eps = 1e-08
weight_decay = 0.05
clip_norm = 0.05
ema_decay = 0.9999

@jax.custom_vjp
def low(v):
    return lax.optimization_barrier(v.astype(jnp.bfloat16)).astype(jnp.float32)

@jax.custom_vjp
def low_back(v):
    return v

def low_keep(v):
    return (low(v), None)

def low_pass(kept, grad):
    return (grad,)

def back_keep(v):
    return (v, None)

def back_low(kept, grad):
    return (low(grad),)
low.defvjp(low_keep, low_pass)
low_back.defvjp(back_keep, back_low)

def layer_norm(values):
    center = values - lax.optimization_barrier(jnp.mean(values, -1, keepdims=True))
    return center * lax.rsqrt(lax.optimization_barrier(jnp.mean(center * center, -1, keepdims=True)) + norm_eps)

def modulate(values, shift, scale):
    return layer_norm(values) * (1.0 + scale[:, None, :]) + shift[:, None, :]

def sinusoid(places, width):
    half = width // 2
    freqs = jnp.exp(-math.log(10000.0) * jnp.arange(half, dtype=jnp.float32) / half)
    angle = places.astype(jnp.float32)[:, None] * freqs[None, :]
    return jnp.concatenate([jnp.cos(angle), jnp.sin(angle)], -1)

def block(values, mod, key_valid, attend_in, attend_out, expand, contract):
    shift_a, scale_a, gate_a, shift_m, scale_m, gate_m = [mod[:, lookup_index] for lookup_index in range(6)]
    batch, length, width = values.shape
    heads = width // HEAD_DIM
    normed = low(modulate(values, shift_a, scale_a))
    triple = jnp.einsum('bld,dce->blce', normed, attend_in, precision=highest_float_accuracy)
    query, key, value = [low(low_back(triple[:, :, lookup_index])).reshape(batch, length, heads, HEAD_DIM) for lookup_index in range(3)]
    scores = low_back(jnp.einsum('bqhe,bkhe->bhqk', query, key, precision=highest_float_accuracy) / math.sqrt(HEAD_DIM))
    scores = jnp.where(key_valid[:, None, None, :] > 0, scores, -1e+30)
    probs = low(jax.nn.softmax(scores, -1))
    context = low(low_back(jnp.einsum('bhqk,bkhe->bqhe', probs, value, precision=highest_float_accuracy))).reshape(batch, length, width)
    attn = low_back(jnp.einsum('bld,de->ble', context, attend_out, precision=highest_float_accuracy))
    middle = values + gate_a[:, None, :] * attn
    normed_m = low(modulate(middle, shift_m, scale_m))
    inner = low_back(jnp.einsum('bld,df->blf', normed_m, expand, precision=highest_float_accuracy))
    active = low(jax.nn.gelu(inner, approximate=True))
    branch = low_back(jnp.einsum('blf,fd->bld', active, contract, precision=highest_float_accuracy))
    return middle + gate_m[:, None, :] * branch

def forward(params, patches, target_noise, kept_slots, kept_count, time_step, labels, teacher):
    attend_in, attend_out, expand, contract, modulation, patch_table, condition = [low(p) for p in params]
    images, length = (patches.shape[0], patches.shape[1])
    capacity = kept_slots.shape[1]
    width = attend_out.shape[-1]
    slot_valid = (jnp.arange(capacity)[None, :] < kept_count[:, None]).astype(jnp.float32)
    select = (kept_slots[:, :, None] == jnp.arange(length)[None, None, :]).astype(jnp.float32) * slot_valid[:, :, None]
    kept_place = lax.optimization_barrier(jnp.sum(select, 1))
    places = sinusoid(jnp.arange(length), width)
    features = sinusoid(time_step, FREQ)
    onehot = (labels[:, None] == jnp.arange(CLASSES)[None, :]).astype(jnp.float32)
    cond_sum = jnp.dot(features, condition[:FREQ], precision=highest_float_accuracy) + jnp.dot(onehot, condition[FREQ:], precision=highest_float_accuracy)
    sigmoid_linear_narrow = low(jax.nn.silu(cond_sum))
    shift_scale_gate_factors = jnp.einsum('bd,ndse->nbse', sigmoid_linear_narrow, modulation, precision=highest_float_accuracy)
    kept_patches = jnp.einsum('bcl,blp->bcp', select, patches, precision=highest_float_accuracy)
    embed = jnp.einsum('bcp,pd->bcd', kept_patches, patch_table[:PATCH_IN], precision=highest_float_accuracy)
    embed = embed + jnp.einsum('bcl,ld->bcd', select, places, precision=highest_float_accuracy)
    encoded = block(embed, shift_scale_gate_factors[0], slot_valid, attend_in[0], attend_out[0], expand[0], contract[0])
    pooled = lax.optimization_barrier(jnp.sum(encoded * slot_valid[:, :, None], 1)) / kept_count.astype(jnp.float32)[:, None]
    normalised_direction = pooled * lax.rsqrt(lax.optimization_barrier(jnp.sum(pooled * pooled, -1, keepdims=True)) + 1e-06)
    frozen_target_direction = teacher * lax.rsqrt(lax.optimization_barrier(jnp.sum(teacher * teacher, -1, keepdims=True)) + 1e-06)
    cosine_match_scores = jnp.dot(normalised_direction, frozen_target_direction.T, precision=highest_float_accuracy) / contrast_sharpness_divisor
    nce = jnp.mean(jax.nn.logsumexp(cosine_match_scores, -1) - jnp.diagonal(cosine_match_scores))
    decode_in = jnp.einsum('bcl,bcd->bld', select, encoded, precision=highest_float_accuracy)
    decode_in = decode_in + (1.0 - kept_place)[:, :, None] * patch_table[2 * PATCH_IN] + places[None]
    decoded = block(decode_in, shift_scale_gate_factors[1], jnp.ones((images, length), jnp.float32), attend_in[1], attend_out[1], expand[1], contract[1])
    predict = low_back(jnp.einsum('bld,pd->blp', low(layer_norm(decoded)), patch_table[PATCH_IN:2 * PATCH_IN], precision=highest_float_accuracy))
    error_map = predict - target_noise
    mse = jnp.mean(error_map * error_map)
    return (mse + nce_weight * nce, (mse, nce))

def adam(weight, grad, moment, second, average, factor):
    grad = grad * factor
    moment = beta_first * moment + (1.0 - beta_first) * grad
    second = beta_second * second + (1.0 - beta_second) * grad * grad
    update = moment / (1.0 - beta_first ** STEP) / (jnp.sqrt(second / (1.0 - beta_second ** STEP)) + adam_eps)
    fresh = weight - learn_rate * (update + weight_decay * weight)
    average_decay = min(ema_decay, (1.0 + STEP) / (10.0 + STEP))
    average = average_decay * average + (1.0 - average_decay) * fresh
    return (fresh, moment, second, average)

def reference(patches, target_noise, kept_slots, kept_count, time_step, labels, teacher, attend_in, attend_out, expand, contract, modulation, patch_table, condition, moment_attend_in, moment_attend_out, moment_expand, moment_contract, moment_modulation, moment_patch, moment_condition, second_attend_in, second_attend_out, second_expand, second_contract, second_modulation, second_patch, second_condition, average_attend_in, average_attend_out, average_expand, average_contract, average_modulation, average_patch, average_condition):
    params = (attend_in, attend_out, expand, contract, modulation, patch_table, condition)
    moments = (moment_attend_in, moment_attend_out, moment_expand, moment_contract, moment_modulation, moment_patch, moment_condition)
    seconds = (second_attend_in, second_attend_out, second_expand, second_contract, second_modulation, second_patch, second_condition)
    averages = (average_attend_in, average_attend_out, average_expand, average_contract, average_modulation, average_patch, average_condition)
    wide_patches = patches.astype(jnp.float32)

    def total(weight_tensors):
        return forward(weight_tensors, wide_patches, target_noise, kept_slots, kept_count, time_step, labels, teacher)
    loss, back, parts = jax.vjp(total, params, has_aux=True)
    grads = back(jnp.ones_like(loss))[0]
    squares = jnp.float32(0.0)
    for grad in grads:
        squares = squares + jnp.sum(grad * grad)
    grad_norm = jnp.sqrt(squares)
    factor = clip_norm / jnp.maximum(grad_norm, clip_norm)
    fresh = [adam(params[lookup_index], grads[lookup_index], moments[lookup_index], seconds[lookup_index], averages[lookup_index], factor) for lookup_index in range(7)]
    return (jnp.stack([parts[0], parts[1]]), grad_norm, fresh[0][0], fresh[1][0], fresh[2][0], fresh[3][0], fresh[4][0], fresh[5][0], fresh[6][0], fresh[0][1], fresh[1][1], fresh[2][1], fresh[3][1], fresh[4][1], fresh[5][1], fresh[6][1], fresh[0][2], fresh[1][2], fresh[2][2], fresh[3][2], fresh[4][2], fresh[5][2], fresh[6][2], fresh[0][3], fresh[1][3], fresh[2][3], fresh[3][3], fresh[4][3], fresh[5][3], fresh[6][3])
```

```python
from functools import partial
import math

import jax
import jax.numpy as jnp
from jax import lax
from jax.experimental import pallas as pl
from jax.experimental.pallas import tpu as pltpu
from jax.sharding import Mesh
from jax.sharding import PartitionSpec as P

HEAD_DIM = 72
CLASSES = 1000
FREQ = 256
PATCH_IN = 16
STEP = 10

MESH = pl.DeviceIdType.MESH
WIDE = ("plane", "core")
NARROW = ("zh", "zl")
ALL = WIDE + NARROW

highest_float_accuracy = lax.Precision.HIGHEST
norm_eps = 1e-06
contrast_sharpness_divisor = 0.02
nce_weight = 0.5
learn_rate = 0.05
beta_first = 0.9
beta_second = 0.999
adam_eps = 1e-08
weight_decay = 0.05
clip_norm = 0.05
ema_decay = 0.9999


def layer_norm(values):
    center = values - jnp.mean(values, -1, keepdims=True)
    return center * lax.rsqrt(jnp.mean(center * center, -1, keepdims=True) + norm_eps)


def modulate(values, shift, scale):
    return layer_norm(values) * (1.0 + scale[None, :]) + shift[None, :]


def sinusoid(places, width):
    half = width // 2
    freqs = jnp.exp(-math.log(10000.0) * jnp.arange(half, dtype=jnp.float32) / half)
    angle = places.astype(jnp.float32)[:, None] * freqs[None, :]
    return jnp.concatenate([jnp.cos(angle), jnp.sin(angle)], -1)


def flat_place(axes):
    place = 0
    for axis in axes:
        place = place * lax.axis_size(axis) + lax.axis_index(axis)
    return place


def group_size(axes):
    size = 1
    for axis in axes:
        size = size * lax.axis_size(axis)
    return size


def device_at(axes, place):
    where = {}
    for axis in reversed(axes):
        where[axis] = lax.rem(place, lax.axis_size(axis))
        place = place // lax.axis_size(axis)
    return where


def exchange_kernel(specs, *refs):
    count = len(specs)
    sources, results, sems = refs[:count], refs[count : 2 * count], refs[2 * count :]
    barrier = pltpu.get_barrier_semaphore()
    greeted = 0
    for axes, _ in specs:
        size, me = group_size(axes), flat_place(axes)
        greeted += size - 1

        def greet(offset, carry, axes=axes, size=size, me=me):
            target = lax.rem(me + offset, size)
            pl.semaphore_signal(
                barrier, inc=1, device_id=device_at(axes, target), device_id_type=MESH
            )
            return carry

        lax.fori_loop(1, size, greet, 0)
    pl.semaphore_wait(barrier, greeted)

    def copy_to(index, offset, arriving):
        axes, mode = specs[index]
        size, me = group_size(axes), flat_place(axes)
        target = lax.rem(me + offset, size)
        source = sources[index].at[target] if mode == "each" else sources[index]
        return pltpu.make_async_remote_copy(
            src_ref=source,
            dst_ref=results[index].at[target if arriving else me],
            send_sem=sems[2 * index].at[target],
            recv_sem=sems[2 * index + 1].at[target if arriving else me],
            device_id=device_at(axes, target),
            device_id_type=MESH,
        )

    for index, (axes, mode) in enumerate(specs):

        def start(offset, carry, index=index):
            copy_to(index, offset, False).start()
            return carry

        lax.fori_loop(1, group_size(axes), start, 0)
    for index, (axes, mode) in enumerate(specs):
        me = flat_place(axes)
        own = sources[index][me] if mode == "each" else sources[index][...]
        results[index][me] = own
    for index, (axes, mode) in enumerate(specs):

        def finish(offset, carry, index=index):
            copy_to(index, offset, True).wait_recv()
            copy_to(index, offset, False).wait_send()
            return carry

        lax.fori_loop(1, group_size(axes), finish, 0)


def exchange(arrays, specs, collective_id):
    shapes, scratch = [], []
    for array, (axes, mode) in zip(arrays, specs):
        size = group_size(axes)
        piece = array.shape[1:] if mode == "each" else array.shape
        shapes.append(jax.ShapeDtypeStruct((size,) + piece, array.dtype))
        scratch += [pltpu.SemaphoreType.DMA((size,)), pltpu.SemaphoreType.DMA((size,))]
    return pl.pallas_call(
        partial(exchange_kernel, specs),
        out_shape=shapes,
        in_specs=[pl.BlockSpec(memory_space=pltpu.VMEM)] * len(arrays),
        out_specs=[pl.BlockSpec(memory_space=pltpu.VMEM)] * len(arrays),
        scratch_shapes=scratch,
        compiler_params=pltpu.CompilerParams(
            collective_id=collective_id, has_side_effects=True, vmem_limit_bytes=40 * 2**20
        ),
        cost_estimate=pl.CostEstimate(flops=0, bytes_accessed=16 * 2**20, transcendentals=0),
    )(*arrays)


def group_places():
    core, low = lax.axis_index("core"), lax.axis_index("zl")
    return {
        "me": core * 2 + low,
        "mate": (1 - core) * 2 + low,
        "far": core * 2 + (1 - low),
        "far_mate": (1 - core) * 2 + (1 - low),
        "mate_id": {"core": 1 - core},
        "far_id": {"zl": 1 - low},
    }


def greet_group(at):
    barrier = pltpu.get_barrier_semaphore()
    for name in ("mate_id", "far_id"):
        pl.semaphore_signal(barrier, inc=1, device_id=at[name], device_id_type=MESH)
    pl.semaphore_wait(barrier, 2)


def own_sum_kernel(chunk, part_ref, sum_ref, near, home, stage, far, sends, recvs):
    length = part_ref.shape[1]
    steps = length // chunk
    at = group_places()
    greet_group(at)

    def copy(source, target, kind, step, to):
        return pltpu.make_async_remote_copy(
            src_ref=source,
            dst_ref=target,
            send_sem=sends.at[kind, step],
            recv_sem=recvs.at[kind, step],
            device_id=at[to],
            device_id_type=MESH,
        )

    rows = [pl.ds(step * chunk, chunk) for step in range(steps)]
    to_near = [
        copy(part_ref.at[at["far_mate"], rows[s]], near.at[rows[s]], 0, s, "mate_id")
        for s in range(steps)
    ]
    to_home = [
        copy(part_ref.at[at["mate"], rows[s]], home.at[rows[s]], 1, s, "mate_id")
        for s in range(steps)
    ]
    to_far = [copy(stage.at[rows[s]], far.at[rows[s]], 2, s, "far_id") for s in range(steps)]
    for s in range(steps):
        to_near[s].start()
    for s in range(steps):
        to_home[s].start()
    for s in range(steps):
        to_near[s].wait_recv()
        both = part_ref[at["far"], rows[s]].astype(jnp.float32) + near[rows[s]].astype(jnp.float32)
        stage[rows[s]] = both.astype(jnp.bfloat16)
        to_far[s].start()
    for s in range(steps):
        to_home[s].wait_recv()
        sum_ref[rows[s]] = part_ref[at["me"], rows[s]].astype(jnp.float32) + home[rows[s]].astype(
            jnp.float32
        )
    for s in range(steps):
        to_far[s].wait_recv()
        sum_ref[rows[s]] = sum_ref[rows[s]] + far[rows[s]].astype(jnp.float32)
    for s in range(steps):
        to_near[s].wait_send()
        to_home[s].wait_send()
        to_far[s].wait_send()


def chunk_of(length):
    return 64 if length % 64 == 0 else 32


def own_sum(parts, collective_id):
    _, length, width = parts.shape
    chunk = chunk_of(length)
    steps = length // chunk
    buffer = pltpu.VMEM((length, width), jnp.bfloat16)
    return pl.pallas_call(
        partial(own_sum_kernel, chunk),
        out_shape=jax.ShapeDtypeStruct((length, width), jnp.float32),
        in_specs=[pl.BlockSpec(memory_space=pltpu.VMEM)],
        out_specs=pl.BlockSpec(memory_space=pltpu.VMEM),
        scratch_shapes=[buffer] * 4
        + [pltpu.SemaphoreType.DMA((3, steps)), pltpu.SemaphoreType.DMA((3, steps))],
        compiler_params=pltpu.CompilerParams(
            collective_id=collective_id, has_side_effects=True, vmem_limit_bytes=40 * 2**20
        ),
        cost_estimate=pl.CostEstimate(
            flops=0, bytes_accessed=length * 256 * 1024, transcendentals=0
        ),
    )(parts)


def group_copy_kernel(chunk, own_ref, all_ref, sends, recvs):
    length = own_ref.shape[0]
    steps = length // chunk
    at = group_places()
    greet_group(at)

    def copy(source, target, kind, step, to):
        return pltpu.make_async_remote_copy(
            src_ref=source,
            dst_ref=target,
            send_sem=sends.at[kind, step],
            recv_sem=recvs.at[kind, step],
            device_id=at[to],
            device_id_type=MESH,
        )

    rows = [pl.ds(step * chunk, chunk) for step in range(steps)]
    out = [copy(own_ref.at[rows[s]], all_ref.at[at["me"], rows[s]], 0, s, "far_id") for s in range(steps)]
    arrive = [copy(own_ref.at[rows[s]], all_ref.at[at["far"], rows[s]], 0, s, "far_id") for s in range(steps)]
    mate_out = [copy(own_ref.at[rows[s]], all_ref.at[at["me"], rows[s]], 1, s, "mate_id") for s in range(steps)]
    mate_in = [copy(own_ref.at[rows[s]], all_ref.at[at["mate"], rows[s]], 1, s, "mate_id") for s in range(steps)]
    pass_out = [
        copy(all_ref.at[at["far"], rows[s]], all_ref.at[at["far"], rows[s]], 2, s, "mate_id")
        for s in range(steps)
    ]
    pass_in = [
        copy(all_ref.at[at["far"], rows[s]], all_ref.at[at["far_mate"], rows[s]], 2, s, "mate_id")
        for s in range(steps)
    ]
    for s in range(steps):
        out[s].start()
    for s in range(steps):
        mate_out[s].start()
    all_ref[at["me"]] = own_ref[...]
    for s in range(steps):
        arrive[s].wait_recv()
        pass_out[s].start()
    for s in range(steps):
        mate_in[s].wait_recv()
        pass_in[s].wait_recv()
    for s in range(steps):
        out[s].wait_send()
        mate_out[s].wait_send()
        pass_out[s].wait_send()


def group_copy(own, collective_id):
    length, width = own.shape
    chunk = chunk_of(length)
    steps = length // chunk
    return pl.pallas_call(
        partial(group_copy_kernel, chunk),
        out_shape=jax.ShapeDtypeStruct((4, length, width), jnp.bfloat16),
        in_specs=[pl.BlockSpec(memory_space=pltpu.VMEM)],
        out_specs=pl.BlockSpec(memory_space=pltpu.VMEM),
        scratch_shapes=[pltpu.SemaphoreType.DMA((3, steps)), pltpu.SemaphoreType.DMA((3, steps))],
        compiler_params=pltpu.CompilerParams(
            collective_id=collective_id, has_side_effects=True, vmem_limit_bytes=40 * 2**20
        ),
        cost_estimate=pl.CostEstimate(
            flops=0, bytes_accessed=length * 256 * 1024, transcendentals=0
        ),
    )(own)


def swap_pairs():
    forth, straight = [], []
    half, low = lax.axis_size("zh"), lax.axis_size("zl")
    for h in range(half):
        for z in range(low):
            zero, one = h * low + z, half * low + h * low + z
            other_one = half * low + (half - 1 - h) * low + z
            forth += [(zero, other_one), (one, zero)]
            straight += [(one, other_one)]
    return forth, straight


SWAP = ("core", "zh", "zl")


def gather_rows(shard):
    forth, straight = swap_pairs()
    first = lax.ppermute(shard, SWAP, forth)
    second = lax.ppermute(shard, SWAP, straight)
    on_zero = lax.axis_index("core") == 0
    pair = jnp.stack([jnp.where(on_zero, shard, first), jnp.where(on_zero, first, second)])
    full = lax.all_gather(pair, "plane", axis=0, tiled=True)
    return full.reshape(full.shape[0] * full.shape[1], full.shape[2])


def scatter_rows(grad):
    planes = lax.axis_size("plane")
    rows = grad.shape[0] // planes
    mine = lax.psum_scatter(grad, "plane", scatter_dimension=0, tiled=True)
    low, high = mine[: rows // 2], mine[rows // 2 :]
    forth, straight = swap_pairs()
    back = [(to, at) for at, to in forth]
    onward = [(to, at) for at, to in straight]
    on_zero = lax.axis_index("core") == 0
    first = lax.ppermute(jnp.where(on_zero, high, low), SWAP, back)
    second = lax.ppermute(high, SWAP, onward)
    return jnp.where(on_zero, low, second).astype(jnp.float32) + first.astype(jnp.float32)


def scores_of(query, key, key_valid):
    scale = 1.0 / math.sqrt(HEAD_DIM)
    scores = jnp.einsum("bqhe,bkhe->bhqk", query, key, preferred_element_type=jnp.float32) * scale
    if key_valid is None:
        return scores
    return jnp.where(key_valid[:, None, None, :] > 0, scores, -1e30)


def attend_forward(query, key, value, key_valid):
    scores = scores_of(query, key, key_valid)
    peak = jnp.max(scores, -1, keepdims=True)
    expo = jnp.exp(scores - peak)
    total = jnp.sum(expo, -1, keepdims=True)
    probs = (expo / total).astype(jnp.bfloat16)
    context = jnp.einsum(
        "bhqk,bkhe->bqhe", probs, value, preferred_element_type=jnp.float32
    ).astype(jnp.bfloat16)
    return (context, peak + jnp.log(total))


def attend_backward(query, key, value, log_total, grad_context, key_valid):
    scale = 1.0 / math.sqrt(HEAD_DIM)
    probs = jnp.exp(scores_of(query, key, key_valid) - log_total)
    grad_value = jnp.einsum(
        "bhqk,bqhe->bkhe",
        probs.astype(jnp.bfloat16),
        grad_context,
        preferred_element_type=jnp.float32,
    ).astype(jnp.bfloat16)
    grad_probs = jnp.einsum(
        "bqhe,bkhe->bhqk", grad_context, value, preferred_element_type=jnp.float32
    )
    grad_scores = (probs * (grad_probs - jnp.sum(grad_probs * probs, -1, keepdims=True))).astype(
        jnp.bfloat16
    )
    grad_query = (
        jnp.einsum("bhqk,bkhe->bqhe", grad_scores, key, preferred_element_type=jnp.float32) * scale
    ).astype(jnp.bfloat16)
    grad_key = (
        jnp.einsum("bhqk,bqhe->bkhe", grad_scores, query, preferred_element_type=jnp.float32)
        * scale
    ).astype(jnp.bfloat16)
    return (grad_query, grad_key, grad_value)


def split_heads(triple):
    batch, length, three = triple.shape
    local = three // 3
    return [
        triple[:, :, i * local : (i + 1) * local].reshape(
            batch, length, local // HEAD_DIM, HEAD_DIM
        )
        for i in range(3)
    ]


def weight_parts(attend, feed):
    local = attend.shape[1] // 4
    hidden = feed.shape[1] // 2
    return attend[:, : 3 * local], attend[:, 3 * local :], feed[:, :hidden], feed[:, hidden:]


def low_dot(spec, left, right):
    return jnp.einsum(spec, left, right, preferred_element_type=jnp.float32)


def block_forward(values, mod, key_valid, weight_tensors, ids):
    attend_in, attend_out, expand, contract = weight_tensors
    shift_a, scale_a, gate_a, shift_m, scale_m, gate_m = [mod[i] for i in range(6)]
    sum_id, copy_id = ids
    normed = group_copy(modulate(values, shift_a, scale_a).astype(jnp.bfloat16), copy_id)
    triple = low_dot("bld,dc->blc", normed, attend_in).astype(jnp.bfloat16)
    context, log_total = attend_forward(*split_heads(triple), key_valid)
    flat_context = context.reshape(triple.shape[0], triple.shape[1], triple.shape[2] // 3)
    attn = own_sum(low_dot("ble,de->bld", flat_context, attend_out).astype(jnp.bfloat16), sum_id)
    middle = values + gate_a[None, :] * attn
    normed_m = group_copy(modulate(middle, shift_m, scale_m).astype(jnp.bfloat16), copy_id)
    inner = low_dot("bld,df->blf", normed_m, expand)
    active = jax.nn.gelu(inner, approximate=True).astype(jnp.bfloat16)
    branch = own_sum(low_dot("blf,df->bld", active, contract).astype(jnp.bfloat16), sum_id)
    result = middle + gate_m[None, :] * branch
    saved = (values, middle, normed, normed_m, triple, flat_context, log_total, attn, inner, active, branch)
    return (result, saved)


def block_backward(grad, mod, key_valid, weight_tensors, saved, ids):
    attend_in, attend_out, expand, contract = weight_tensors
    values, middle, normed, normed_m, triple, flat_context, log_total, attn, inner, active, branch = saved
    shift_a, scale_a, gate_a, shift_m, scale_m, gate_m = [mod[i] for i in range(6)]
    sum_id, copy_id = ids
    grad_branch = group_copy((gate_m[None, :] * grad).astype(jnp.bfloat16), copy_id)
    grad_gate_m = jnp.sum(grad * branch, 0)
    grad_active = low_dot("bld,df->blf", grad_branch, contract)
    gelu_back = jax.vjp(partial(jax.nn.gelu, approximate=True), inner)[1]
    grad_inner = gelu_back(grad_active)[0].astype(jnp.bfloat16)
    grad_normed = own_sum(
        low_dot("blf,df->bld", grad_inner, expand).astype(jnp.bfloat16), sum_id
    )
    grad_contract = low_dot("bld,blf->df", grad_branch, active)
    grad_expand = low_dot("bld,blf->df", normed_m, grad_inner)
    grad_feed = jnp.concatenate([grad_expand, grad_contract], 1).astype(jnp.bfloat16)
    _, modulate_back = jax.vjp(modulate, middle, shift_m, scale_m)
    grad_mid, grad_shift_m, grad_scale_m = modulate_back(grad_normed)
    grad_mid = grad + grad_mid
    grad_attn = group_copy((gate_a[None, :] * grad_mid).astype(jnp.bfloat16), copy_id)
    grad_gate_a = jnp.sum(grad_mid * attn, 0)
    grad_flat = low_dot("bld,de->ble", grad_attn, attend_out).astype(jnp.bfloat16)
    grad_attend_out = low_dot("bld,ble->de", grad_attn, flat_context)
    query, key, value = split_heads(triple)
    grad_context = grad_flat.reshape(query.shape)
    grad_parts = attend_backward(query, key, value, log_total, grad_context, key_valid)
    grad_triple = jnp.concatenate([g.reshape(flat_context.shape) for g in grad_parts], 2)
    grad_normed = own_sum(
        low_dot("blc,dc->bld", grad_triple, attend_in).astype(jnp.bfloat16), sum_id
    )
    grad_attend_in = low_dot("bld,blc->dc", normed, grad_triple)
    grad_attend = jnp.concatenate([grad_attend_in, grad_attend_out], 1).astype(jnp.bfloat16)
    _, modulate_back = jax.vjp(modulate, values, shift_a, scale_a)
    grad_values, grad_shift_a, grad_scale_a = modulate_back(grad_normed)
    grad_mod = jnp.stack(
        [grad_shift_a, grad_scale_a, grad_gate_a, grad_shift_m, grad_scale_m, grad_gate_m], 0
    )
    return (grad_mid + grad_values, grad_mod, grad_attend, grad_feed)


def adam(weight, grad, moment, second, average, factor):
    grad = grad * factor
    moment = beta_first * moment + (1.0 - beta_first) * grad
    second = beta_second * second + (1.0 - beta_second) * grad * grad
    update = (
        moment
        / (1.0 - beta_first**STEP)
        / (jnp.sqrt(second / (1.0 - beta_second**STEP)) + adam_eps)
    )
    fresh = weight - learn_rate * (update + weight_decay * weight)
    average_decay = min(ema_decay, (1.0 + STEP) / (10.0 + STEP))
    average = average_decay * average + (1.0 - average_decay) * fresh
    return (fresh, moment, second, average)


def shards(
    patches,
    target_noise,
    kept_slots,
    kept_count,
    time_step,
    labels,
    teacher,
    *tables,
):
    params, moments, seconds, averages = tables[:7], tables[7:14], tables[14:21], tables[21:]
    attend_in, attend_out, expand, contract, modulation, patch_table, condition = params
    batch, length = (patches.shape[0], patches.shape[1])
    capacity = kept_slots.shape[1]
    rows, local = (attend_in.shape[1], attend_in.shape[3])
    wides, narrows = (group_size(WIDE), group_size(NARROW))
    wide_index, narrow_index = (flat_place(WIDE), flat_place(NARROW))
    images = batch * wides
    width = local * narrows
    assert batch == narrows

    attend_rows, feed_rows = [], []
    for i in range(2):
        attend_shard = jnp.concatenate(
            [attend_in[i].reshape(rows, 3 * local), attend_out[i].T], 1
        ).astype(jnp.bfloat16)
        feed_shard = jnp.concatenate([expand[i], contract[i].T], 1).astype(jnp.bfloat16)
        attend_rows.append(gather_rows(attend_shard))
        feed_rows.append(gather_rows(feed_shard))
    weights = [weight_parts(attend_rows[i], feed_rows[i]) for i in range(2)]

    def own(array):
        return lax.dynamic_index_in_dim(array, narrow_index, 0, keepdims=False)

    condition_low = condition.astype(jnp.bfloat16)
    features = sinusoid(time_step, FREQ)
    onehot = (labels[:, None] == jnp.arange(CLASSES)[None, :]).astype(jnp.bfloat16)
    cond_part = jnp.dot(
        features, condition_low[:FREQ].astype(jnp.float32), precision=highest_float_accuracy
    ) + low_dot("bc,cd->bd", onehot, condition_low[FREQ:])
    facts = jnp.stack([kept_count, time_step, labels], 1).astype(jnp.float32)
    facts = jnp.pad(own(facts)[None, :], ((0, 7), (0, local - 3)))
    payload = jnp.concatenate([cond_part, own(teacher).reshape(narrows, local), facts], 0)
    table_pad = jnp.pad(patch_table.astype(jnp.bfloat16), ((0, 15), (0, 0)))
    everyone, tables_near = exchange(
        [payload, table_pad], [(ALL, "same"), (NARROW, "same")], 0
    )
    everyone = everyone.reshape(wides, narrows, batch + narrows + 8, local)
    cond_sum = jnp.transpose(everyone[:, :, :batch], (0, 2, 1, 3)).reshape(images, width)
    negatives = everyone[:, :, batch : batch + narrows].reshape(images, width)
    facts_all = everyone[:, :, batch + narrows, :3]
    time_all = facts_all[:, :, 1].reshape(images).astype(jnp.int32)
    labels_all = facts_all[:, :, 2].reshape(images).astype(jnp.int32)
    patch_full = jnp.transpose(tables_near, (1, 0, 2)).reshape(48, width)[:33]
    silu_low = jax.nn.silu(cond_sum).astype(jnp.bfloat16)
    silu_rows = lax.dynamic_slice_in_dim(silu_low, wide_index * rows, rows, 1)
    modulation_low = modulation.astype(jnp.bfloat16)
    mod_part = low_dot("ip,npkc->inkc", silu_rows, modulation_low)
    mod_part = mod_part.reshape(wides, batch, 12, local)
    (mod_wide,) = exchange([mod_part], [(WIDE, "each")], 1)
    (mod_near,) = exchange([jnp.sum(mod_wide, 0)], [(NARROW, "each")], 2)
    mods = jnp.transpose(mod_near, (1, 0, 2)).reshape(2, 6, width)

    count_own = own(kept_count).astype(jnp.float32)
    slot_valid = (jnp.arange(capacity) < own(kept_count)).astype(jnp.float32)
    select = (own(kept_slots)[:, None] == jnp.arange(length)[None, :]).astype(
        jnp.float32
    ) * slot_valid[:, None]
    kept_place = jnp.sum(select, 0)
    places = sinusoid(jnp.arange(length), width)
    group_counts = lax.dynamic_slice(
        facts_all[:, :, 0],
        (lax.axis_index("plane") * 2, lax.axis_index("zh") * 2),
        (2, 2),
    ).reshape(4)
    group_valid = (jnp.arange(capacity)[None, :] < group_counts[:, None]).astype(jnp.float32)
    kept_patches = low_dot("cl,lp->cp", select.astype(jnp.bfloat16), own(patches))
    embed = low_dot("cp,pd->cd", kept_patches.astype(jnp.bfloat16), patch_full[:PATCH_IN])
    embed = embed + jnp.dot(select, places, precision=highest_float_accuracy)
    encoded, saved_enc = block_forward(embed, mods[0], group_valid, weights[0], (3, 4))

    def pool_unit(values):
        pooled = jnp.sum(values * slot_valid[:, None], 0) / count_own
        return pooled * lax.rsqrt(jnp.sum(pooled * pooled, -1, keepdims=True) + 1e-06)

    normalised_direction, pool_back = jax.vjp(pool_unit, encoded)
    frozen_target_direction = negatives * lax.rsqrt(
        jnp.sum(negatives * negatives, -1, keepdims=True) + 1e-06
    )
    cosine_match_scores = (
        jnp.sum(normalised_direction[None, :] * frozen_target_direction, -1)
        / contrast_sharpness_divisor
    )
    peak = jnp.max(cosine_match_scores)
    expo = jnp.exp(cosine_match_scores - peak)
    total = jnp.sum(expo)
    positive = ((wide_index * batch + narrow_index) == jnp.arange(images)).astype(jnp.float32)
    nce_local = peak + jnp.log(total) - jnp.sum(cosine_match_scores * positive)
    derivative_of_raw_scores = (expo / total - positive) * (nce_weight / images)
    unit_vector_gradient = (
        jnp.sum(derivative_of_raw_scores[:, None] * frozen_target_direction, 0)
        / contrast_sharpness_divisor
    )
    grad_pool = pool_back(unit_vector_gradient)[0]
    mask_token = patch_full[2 * PATCH_IN].astype(jnp.float32)
    decode_in = jnp.einsum("cl,cd->ld", select, encoded, precision=highest_float_accuracy)
    decode_in = decode_in + (1.0 - kept_place)[:, None] * mask_token + places
    decoded, saved_dec = block_forward(decode_in, mods[1], None, weights[1], (5, 6))
    final, final_back = jax.vjp(layer_norm, decoded)
    final_low = final.astype(jnp.bfloat16)
    head = patch_full[PATCH_IN : 2 * PATCH_IN]
    predict = low_dot("ld,pd->lp", final_low, head)
    error_map = predict - own(target_noise)
    count_all = images * length * PATCH_IN
    mse_local = jnp.sum(error_map * error_map)
    grad_predict = (error_map * (2.0 / count_all)).astype(jnp.bfloat16)
    grad_head = low_dot("lp,ld->pd", grad_predict, final_low)
    grad_final = low_dot("lp,pd->ld", grad_predict, head)
    grad_decoded = final_back(grad_final)[0]
    grad_dec_in, grad_mod_dec, attend_dec, feed_dec = block_backward(
        grad_decoded, mods[1], None, weights[1], saved_dec, (5, 6)
    )
    grad_mask = jnp.sum((1.0 - kept_place)[:, None] * grad_dec_in, 0)
    grad_encoded = jnp.dot(select, grad_dec_in, precision=highest_float_accuracy) + grad_pool
    grad_embed, grad_mod_enc, attend_enc, feed_enc = block_backward(
        grad_encoded, mods[0], group_valid, weights[0], saved_enc, (3, 4)
    )
    grad_patch = jnp.einsum(
        "cp,cd->pd", kept_patches, grad_embed, precision=highest_float_accuracy
    )

    attend_sums = [scatter_rows(g) for g in (attend_enc, attend_dec)]
    feed_sums = [scatter_rows(g) for g in (feed_enc, feed_dec)]

    grad_mods = jnp.stack([grad_mod_enc, grad_mod_dec]).reshape(12, narrows, local)
    grad_mods = jnp.transpose(grad_mods, (1, 0, 2))
    grad_table = jnp.concatenate([grad_patch, grad_head, grad_mask[None, :]], 0)
    grad_table = jnp.transpose(grad_table.reshape(33, narrows, local), (1, 0, 2))
    mods_near, table_near = exchange(
        [grad_mods, jnp.pad(grad_table, ((0, 0), (0, 7), (0, 0)))],
        [(NARROW, "each"), (NARROW, "each")],
        7,
    )
    table_sum = jnp.pad(jnp.sum(table_near, 0), ((0, 8), (0, 0))).astype(jnp.bfloat16)
    mods_all, table_all = exchange(
        [mods_near, table_sum], [(WIDE, "same"), (WIDE, "same")], 8
    )
    grad_patch_table = jnp.sum(table_all.astype(jnp.float32), 0)[:33]
    mods_all = mods_all.reshape(images, 2, 6, local)
    silu_broad = silu_rows.astype(jnp.float32)
    grad_modulation = jnp.einsum(
        "ip,inkc->npkc", silu_broad, mods_all, precision=highest_float_accuracy
    )
    grad_silu = jnp.einsum(
        "inkc,npkc->ip",
        mods_all,
        modulation_low.astype(jnp.float32),
        precision=highest_float_accuracy,
    )
    (silu_near,) = exchange([grad_silu], [(NARROW, "same")], 9)
    (silu_wide,) = exchange([jnp.sum(silu_near, 0)], [(WIDE, "same")], 10)
    grad_silu = jnp.transpose(silu_wide, (1, 0, 2)).reshape(images, width)
    grad_silu = lax.dynamic_slice_in_dim(grad_silu, narrow_index * local, local, 1)
    cond_cols = lax.dynamic_slice_in_dim(cond_sum, narrow_index * local, local, 1)
    grad_cond = jax.vjp(jax.nn.silu, cond_cols)[1](grad_silu)[0]
    features_all = sinusoid(time_all, FREQ)
    onehot_all = (labels_all[:, None] == jnp.arange(CLASSES)[None, :]).astype(jnp.float32)
    grad_condition = jnp.dot(
        jnp.concatenate([features_all, onehot_all], 1).T, grad_cond, precision=highest_float_accuracy
    )

    grads = [
        jnp.stack([g[:, : 3 * local].reshape(rows, 3, local) for g in attend_sums]),
        jnp.stack([g[:, 3 * local :].T for g in attend_sums]),
        jnp.stack([g[:, : expand.shape[2]] for g in feed_sums]),
        jnp.stack([g[:, expand.shape[2] :].T for g in feed_sums]),
        grad_modulation,
        grad_patch_table,
        grad_condition,
    ]
    square_big = jnp.sum(grad_modulation * grad_modulation)
    for g in attend_sums + feed_sums:
        square_big = square_big + jnp.sum(g * g)
    square_small = jnp.sum(grad_patch_table * grad_patch_table) + jnp.sum(
        grad_condition * grad_condition
    )
    square_local = square_big + (wide_index == 0).astype(jnp.float32) * square_small
    scalars = jnp.stack([mse_local, nce_local, square_local])
    scalars = jnp.pad(scalars[None, :], ((0, 7), (0, 125)))
    (scalars_all,) = exchange([scalars], [(ALL, "same")], 11)
    sums = jnp.sum(scalars_all[:, 0], 0)
    grad_norm = jnp.sqrt(sums[2])
    factor = clip_norm / jnp.maximum(grad_norm, clip_norm)
    fresh = [
        adam(params[i], grads[i], moments[i], seconds[i], averages[i], factor) for i in range(7)
    ]
    loss_parts = jnp.stack([sums[0] / count_all, sums[1] / images])
    return (loss_parts, grad_norm) + tuple(fresh[i][k] for k in range(4) for i in range(7))


def solution(mesh):
    wide, narrow = mesh.devices.shape
    grid = Mesh(mesh.devices.reshape(wide // 2, 2, narrow // 2, 2), ALL)
    image_specs = (
        P(WIDE, None, None),
        P(WIDE, None, None),
        P(WIDE, None),
        P(WIDE),
        P(WIDE),
        P(WIDE),
        P(WIDE, None),
    )
    table_specs = (
        P(None, WIDE, None, NARROW),
        P(None, NARROW, WIDE),
        P(None, WIDE, NARROW),
        P(None, NARROW, WIDE),
        P(None, WIDE, None, NARROW),
        P(None, NARROW),
        P(None, NARROW),
    )
    return jax.shard_map(
        shards,
        mesh=grid,
        in_specs=image_specs + table_specs * 4,
        out_specs=(P(), P()) + table_specs * 4,
        check_vma=False,
    )
```

```python
from functools import partial
import math

import jax
import jax.numpy as jnp
from jax import lax
from jax.experimental import pallas as pl
from jax.experimental.pallas import tpu as pltpu
from jax.sharding import Mesh
from jax.sharding import PartitionSpec as P

HEAD_DIM = 72
CLASSES = 1000
FREQ = 256
PATCH_IN = 16
STEP = 10

MESH = pl.DeviceIdType.MESH
WIDE = ("py", "px", "core")
NARROW = ("zh", "zl")
ALL = WIDE + NARROW

highest_float_accuracy = lax.Precision.HIGHEST
norm_eps = 1e-06
contrast_sharpness_divisor = 0.02
nce_weight = 0.5
learn_rate = 0.05
beta_first = 0.9
beta_second = 0.999
adam_eps = 1e-08
weight_decay = 0.05
clip_norm = 0.05
ema_decay = 0.9999


def layer_norm(values):
    center = values - jnp.mean(values, -1, keepdims=True)
    return center * lax.rsqrt(jnp.mean(center * center, -1, keepdims=True) + norm_eps)


def modulate(values, shift, scale):
    return layer_norm(values) * (1.0 + scale[None, :]) + shift[None, :]


def sinusoid(places, width):
    half = width // 2
    freqs = jnp.exp(-math.log(10000.0) * jnp.arange(half, dtype=jnp.float32) / half)
    angle = places.astype(jnp.float32)[:, None] * freqs[None, :]
    return jnp.concatenate([jnp.cos(angle), jnp.sin(angle)], -1)


def flat_place(axes):
    place = 0
    for axis in axes:
        place = place * lax.axis_size(axis) + lax.axis_index(axis)
    return place


def group_size(axes):
    size = 1
    for axis in axes:
        size = size * lax.axis_size(axis)
    return size


def device_at(axes, place):
    where = {}
    for axis in reversed(axes):
        where[axis] = lax.rem(place, lax.axis_size(axis))
        place = place // lax.axis_size(axis)
    return where


def turned(axis, offset):
    size = lax.axis_size(axis)
    return lax.rem(lax.axis_index(axis) + (offset % size), size)


def other(axis):
    return 1 - lax.axis_index(axis)


class Part:
    def __init__(self):
        self.arrays, self.in_spaces = [], []
        self.shapes, self.out_spaces = [], []
        self.aliases = {}
        self.scratch = []
        self.peers = []

    def take(self, array, space=pltpu.HBM):
        self.arrays.append(array)
        self.in_spaces.append(space)
        return len(self.arrays) - 1

    def give(self, shape, dtype=jnp.bfloat16, space=pltpu.HBM, source=None):
        self.shapes.append(jax.ShapeDtypeStruct(shape, dtype))
        self.out_spaces.append(space)
        if source is not None:
            self.aliases[source] = len(self.shapes) - 1
        return len(self.shapes) - 1

    def greet(self, barrier):
        for peer in self.peers:
            pl.semaphore_signal(barrier, inc=1, device_id=peer(), device_id_type=MESH)
        return len(self.peers)

    def begin(self, ins, outs, scratch):
        pass

    def finish(self, ins, outs, scratch):
        pass


class Exchange(Part):
    def __init__(self, arrays, specs):
        super().__init__()
        self.specs = specs
        for array, (axes, mode) in zip(arrays, specs):
            size = group_size(axes)
            piece = array.shape[1:] if mode == "each" else array.shape
            self.take(array, pltpu.VMEM)
            self.give((size,) + piece, array.dtype, pltpu.VMEM)
            self.scratch += [pltpu.SemaphoreType.DMA((size,)), pltpu.SemaphoreType.DMA((size,))]

    def greet(self, barrier):
        greeted = 0
        for axes, _ in self.specs:
            size, me = group_size(axes), flat_place(axes)
            greeted += size - 1

            def signal(offset, carry, axes=axes, size=size, me=me):
                target = lax.rem(me + offset, size)
                pl.semaphore_signal(
                    barrier, inc=1, device_id=device_at(axes, target), device_id_type=MESH
                )
                return carry

            lax.fori_loop(1, size, signal, 0)
        return greeted

    def begin(self, ins, outs, scratch):
        def copy_to(index, offset, arriving):
            axes, mode = self.specs[index]
            size, me = group_size(axes), flat_place(axes)
            target = lax.rem(me + offset, size)
            return pltpu.make_async_remote_copy(
                src_ref=ins[index].at[target] if mode == "each" else ins[index],
                dst_ref=outs[index].at[target if arriving else me],
                send_sem=scratch[2 * index].at[target],
                recv_sem=scratch[2 * index + 1].at[target if arriving else me],
                device_id=device_at(axes, target),
                device_id_type=MESH,
            )

        for index, (axes, mode) in enumerate(self.specs):

            def start(offset, carry, index=index):
                copy_to(index, offset, False).start()
                return carry

            lax.fori_loop(1, group_size(axes), start, 0)
        for index, (axes, mode) in enumerate(self.specs):
            me = flat_place(axes)
            outs[index][me] = ins[index][me] if mode == "each" else ins[index][...]
        for index, (axes, mode) in enumerate(self.specs):

            def end(offset, carry, index=index):
                copy_to(index, offset, True).wait_recv()
                copy_to(index, offset, False).wait_send()
                return carry

            lax.fori_loop(1, group_size(axes), end, 0)


def chunk_of(length):
    return 64 if length % 64 == 0 else 32


class GroupPart(Part):
    def __init__(self, length):
        super().__init__()
        self.chunk = chunk_of(length)
        self.steps = length // self.chunk
        self.peers = [lambda: {"core": other("core")}, lambda: {"zl": other("zl")}]

    def ranks(self):
        core, low = lax.axis_index("core"), lax.axis_index("zl")
        return core * 2 + low, (1 - core) * 2 + low, core * 2 + 1 - low, (1 - core) * 2 + 1 - low

    def copy(self, source, target, sems, kind, step):
        peer = {"zl": other("zl")} if kind == "far" else {"core": other("core")}
        row = {"far": 0, "mate": 1, "relay": 2}[kind]
        return pltpu.make_async_remote_copy(
            src_ref=source,
            dst_ref=target,
            send_sem=sems[0].at[row, step],
            recv_sem=sems[1].at[row, step],
            device_id=peer,
            device_id_type=MESH,
        )

    def sems(self):
        return [pltpu.SemaphoreType.DMA((3, self.steps)), pltpu.SemaphoreType.DMA((3, self.steps))]


class OwnSum(GroupPart):
    def __init__(self, parts):
        _, length, width = parts.shape
        super().__init__(length)
        self.take(parts, pltpu.VMEM)
        self.give((length, width), jnp.float32, pltpu.VMEM)
        self.scratch = [pltpu.VMEM((length, width), jnp.bfloat16)] * 4 + self.sems()

    def begin(self, ins, outs, scratch):
        (part_ref,), (sum_ref,) = ins, outs
        near, home, stage, far = scratch[:4]
        sems = scratch[4:]
        me, mate, away, away_mate = self.ranks()
        rows = [pl.ds(s * self.chunk, self.chunk) for s in range(self.steps)]
        every = range(self.steps)
        to_near = [self.copy(part_ref.at[away_mate, rows[s]], near.at[rows[s]], sems, "mate", s) for s in every]
        to_home = [self.copy(part_ref.at[mate, rows[s]], home.at[rows[s]], sems, "relay", s) for s in every]
        to_far = [self.copy(stage.at[rows[s]], far.at[rows[s]], sems, "far", s) for s in every]
        for s in every:
            to_near[s].start()
        for s in every:
            to_home[s].start()
        for s in every:
            to_near[s].wait_recv()
            both = part_ref[away, rows[s]].astype(jnp.float32) + near[rows[s]].astype(jnp.float32)
            stage[rows[s]] = both.astype(jnp.bfloat16)
            to_far[s].start()
        for s in every:
            to_home[s].wait_recv()
            sum_ref[rows[s]] = part_ref[me, rows[s]].astype(jnp.float32) + home[rows[s]].astype(
                jnp.float32
            )
        for s in every:
            to_far[s].wait_recv()
            sum_ref[rows[s]] = sum_ref[rows[s]] + far[rows[s]].astype(jnp.float32)
        for s in every:
            to_near[s].wait_send()
            to_home[s].wait_send()
            to_far[s].wait_send()


class GroupCopy(GroupPart):
    def __init__(self, own):
        length, width = own.shape
        super().__init__(length)
        self.take(own, pltpu.VMEM)
        self.give((4, length, width), jnp.bfloat16, pltpu.VMEM)
        self.scratch = self.sems()

    def begin(self, ins, outs, scratch):
        (own_ref,), (all_ref,) = ins, outs
        me, mate, away, away_mate = self.ranks()
        rows = [pl.ds(s * self.chunk, self.chunk) for s in range(self.steps)]
        every = range(self.steps)

        def move(kind, source, slot, s):
            return self.copy(source.at[rows[s]], all_ref.at[slot, rows[s]], scratch, kind, s)

        out = [move("far", own_ref, me, s) for s in every]
        arrive = [move("far", own_ref, away, s) for s in every]
        mate_out = [move("mate", own_ref, me, s) for s in every]
        mate_in = [move("mate", own_ref, mate, s) for s in every]
        relay_out = [move("relay", all_ref.at[away], away, s) for s in every]
        relay_in = [move("relay", all_ref.at[away], away_mate, s) for s in every]
        for s in every:
            out[s].start()
        for s in every:
            mate_out[s].start()
        all_ref[me] = own_ref[...]
        for s in every:
            arrive[s].wait_recv()
            relay_out[s].start()
        for s in every:
            mate_in[s].wait_recv()
            relay_in[s].wait_recv()
        for s in every:
            out[s].wait_send()
            mate_out[s].wait_send()
            relay_out[s].wait_send()


class Errand(Part):
    def plan(self, ins, outs):
        raise NotImplementedError

    def local(self, ins, outs):
        return []

    def reserve(self, count, local=0):
        self.scratch = [pltpu.SemaphoreType.DMA((count,)), pltpu.SemaphoreType.DMA((count,))]
        if local:
            self.scratch.append(pltpu.SemaphoreType.DMA((local,)))

    def run(self, ins, outs, scratch, ending):
        for i, (source, target, landing, device, when) in enumerate(self.plan(ins, outs)):

            def remote(place, i=i, source=source, device=device):
                return pltpu.make_async_remote_copy(
                    src_ref=source,
                    dst_ref=place,
                    send_sem=scratch[0].at[i],
                    recv_sem=scratch[1].at[i],
                    device_id=device,
                    device_id_type=MESH,
                )

            def act(remote=remote, target=target, landing=landing):
                if ending:
                    remote(landing).wait_recv()
                    remote(target).wait_send()
                else:
                    remote(target).start()

            if when is None:
                act()
            else:
                pl.when(when)(act)
        for i, (source, target, when) in enumerate(self.local(ins, outs)):

            def act_local(i=i, source=source, target=target):
                copy = pltpu.make_async_copy(source, target, scratch[2].at[i])
                if ending:
                    copy.wait()
                else:
                    copy.start()

            pl.when(when)(act_local)

    def begin(self, ins, outs, scratch):
        self.run(ins, outs, scratch, False)

    def finish(self, ins, outs, scratch):
        self.run(ins, outs, scratch, True)


def plane_peers():
    peers = []
    for axis in ("py", "px"):
        for offset in range(1, lax.axis_size(axis)):
            peers.append(lambda axis=axis, offset=offset: {axis: turned(axis, offset)})
    return peers


SWAP_PEERS = [
    lambda: {"core": other("core")},
    lambda: {"zh": other("zh")},
    lambda: {"core": other("core"), "zh": other("zh")},
]


class SwapIn(Errand):
    def __init__(self, shard):
        super().__init__()
        self.take(shard)
        self.give((lax.axis_size("py"), lax.axis_size("px"), 2) + shard.shape)
        self.peers = SWAP_PEERS
        self.reserve(2, 1)

    def plan(self, ins, outs):
        core, half = lax.axis_index("core"), lax.axis_index("zh")
        home = outs[0].at[lax.axis_index("py"), lax.axis_index("px")]
        crossed = jnp.where(core == 0, 1 - half, half)
        return [
            (ins[0], home.at[core], home.at[1 - core], {"core": 1 - core, "zh": crossed}, None),
            (ins[0], home.at[1], home.at[1], {"zh": 1 - half}, core == 1),
        ]

    def local(self, ins, outs):
        home = outs[0].at[lax.axis_index("py"), lax.axis_index("px")]
        return [(ins[0], home.at[0], lax.axis_index("core") == 0)]


class Spread(Errand):
    def __init__(self, rows, stages):
        super().__init__()
        self.stages = stages
        self.give(rows.shape, rows.dtype, pltpu.HBM, self.take(rows))
        self.peers = plane_peers()
        ny, nx = rows.shape[:2]
        straight = nx + ny - 2
        self.reserve(
            sum({"a": straight, "b": straight, "c": 2 * (nx - 1) * (ny - 1)}[s] for s in stages)
        )

    def plan(self, ins, outs):
        rows = outs[0]
        ny, nx = rows.shape[:2]
        y, x = lax.axis_index("py"), lax.axis_index("px")
        moves = []

        def along(axis, offset, at, core):
            to = {axis: turned(axis, offset)}
            back = turned(axis, -offset)
            here = rows.at[at["py"], at["px"], core]
            land = dict(at)
            land[axis] = back
            moves.append((here, here, rows.at[land["py"], land["px"], core], to, None))

        own = {"py": y, "px": x}
        sides = [("px", nx), ("py", ny)]
        for stage in self.stages:
            if stage in "ab":
                for core, (axis, size) in enumerate(sides if stage == "a" else sides[::-1]):
                    for offset in range(1, size):
                        along(axis, offset, own, core)
            else:
                for e in range(1, nx):
                    for offset in range(1, ny):
                        along("py", offset, {"py": y, "px": turned("px", e)}, 0)
                for e in range(1, ny):
                    for offset in range(1, nx):
                        along("px", offset, {"py": turned("py", e), "px": x}, 1)
        return moves


class FoldFar(Errand):
    def __init__(self, grad):
        super().__init__()
        self.take(grad)
        ny, nx, _, rows, columns = grad.shape
        self.give((ny - 1, nx - 1, rows, columns))
        self.give((nx - 1, ny - 1, rows, columns))
        self.peers = plane_peers()
        self.reserve(2 * (nx - 1) * (ny - 1))

    def plan(self, ins, outs):
        grad = ins[0]
        ny, nx = grad.shape[:2]
        moves = []
        for e in range(1, nx):
            for d in range(1, ny):
                slot = outs[0].at[d - 1, e - 1]
                to = turned("py", d)
                moves.append((grad.at[to, turned("px", e), 0], slot, slot, {"py": to}, None))
        for e in range(1, ny):
            for d in range(1, nx):
                slot = outs[1].at[d - 1, e - 1]
                to = turned("px", d)
                moves.append((grad.at[turned("py", e), to, 1], slot, slot, {"px": to}, None))
        return moves


class FoldNear(Errand):
    def __init__(self, grad):
        super().__init__()
        self.take(grad)
        ny, nx, _, rows, columns = grad.shape
        self.give((ny - 1, rows, columns))
        self.give((nx - 1, rows, columns))
        self.peers = plane_peers()
        self.reserve(nx + ny - 2)

    def plan(self, ins, outs):
        grad = ins[0]
        ny, nx = grad.shape[:2]
        y, x = lax.axis_index("py"), lax.axis_index("px")
        moves = []
        for d in range(1, ny):
            to, slot = turned("py", d), outs[0].at[d - 1]
            moves.append((grad.at[to, x, 0], slot, slot, {"py": to}, None))
        for d in range(1, nx):
            to, slot = turned("px", d), outs[1].at[d - 1]
            moves.append((grad.at[y, to, 1], slot, slot, {"px": to}, None))
        return moves


class FoldRelay(Errand):
    def __init__(self, sums):
        super().__init__()
        for each in sums:
            self.take(each)
            self.give(each.shape)
        self.peers = plane_peers()
        self.reserve(sums[0].shape[0] + sums[1].shape[0])

    def plan(self, ins, outs):
        moves = []
        for i, axis in enumerate(("px", "py")):
            for e in range(1, lax.axis_size(axis)):
                slot = outs[i].at[e - 1]
                moves.append((ins[i].at[e - 1], slot, slot, {axis: turned(axis, e)}, None))
        return moves


class SwapOut(Errand):
    def __init__(self, pair):
        super().__init__()
        self.take(pair)
        self.give(pair.shape)
        self.peers = SWAP_PEERS
        self.reserve(2, 1)

    def plan(self, ins, outs):
        core, half = lax.axis_index("core"), lax.axis_index("zh")
        crossed = jnp.where(core == 0, half, 1 - half)
        pair, met = ins[0], outs[0]
        return [
            (pair.at[1 - core], met.at[0], met.at[0], {"core": 1 - core, "zh": crossed}, None),
            (pair.at[1], met.at[1], met.at[1], {"zh": 1 - half}, core == 1),
        ]

    def local(self, ins, outs):
        return [(ins[0].at[0], outs[0].at[1], lax.axis_index("core") == 0)]


def take_counts(refs, parts, name):
    taken, rest = [], list(refs)
    for part in parts:
        size = len(getattr(part, name))
        taken.append(rest[:size])
        rest = rest[size:]
    return taken, rest


def kernel(parts, *refs):
    ins, refs = take_counts(refs, parts, "arrays")
    outs, refs = take_counts(refs, parts, "shapes")
    scratch, _ = take_counts(refs, parts, "scratch")
    barrier = pltpu.get_barrier_semaphore()
    greeted = sum(part.greet(barrier) for part in parts)
    pl.semaphore_wait(barrier, greeted)
    for i in range(1, len(parts)):
        parts[i].begin(ins[i], outs[i], scratch[i])
    parts[0].begin(ins[0], outs[0], scratch[0])
    for i in range(1, len(parts)):
        parts[i].finish(ins[i], outs[i], scratch[i])


def travel(collective_id, *parts):
    aliases, first_in, first_out = {}, 0, 0
    for part in parts:
        for source, result in part.aliases.items():
            aliases[first_in + source] = first_out + result
        first_in += len(part.arrays)
        first_out += len(part.shapes)
    results = pl.pallas_call(
        partial(kernel, parts),
        out_shape=[shape for part in parts for shape in part.shapes],
        in_specs=[pl.BlockSpec(memory_space=space) for part in parts for space in part.in_spaces],
        out_specs=[pl.BlockSpec(memory_space=space) for part in parts for space in part.out_spaces],
        scratch_shapes=[each for part in parts for each in part.scratch],
        input_output_aliases=aliases,
        compiler_params=pltpu.CompilerParams(
            collective_id=collective_id, has_side_effects=True, vmem_limit_bytes=40 * 2**20
        ),
        cost_estimate=pl.CostEstimate(flops=0, bytes_accessed=16 * 2**20, transcendentals=0),
    )(*[array for part in parts for array in part.arrays])
    split, _ = take_counts(results, parts, "shapes")
    return split


class Route:
    def __init__(self, shards, errands):
        self.shards = shards
        self.errands = iter(errands)
        self.rows, self.grads, self.far, self.near = {}, {}, {}, {}
        self.relayed, self.met = {}, {}
        self.count = 0

    def step(self, main):
        errands, parts = next(self.errands), [main]
        for name, what in errands:
            if what == "in":
                parts.append(SwapIn(self.shards[name]))
            elif what in ("a", "b", "c", "ab", "bc"):
                parts.append(Spread(self.rows[name], what))
            elif what == "far":
                parts.append(FoldFar(self.grads[name]))
            elif what == "near":
                parts.append(FoldNear(self.grads[name]))
            elif what == "relay":
                parts.append(FoldRelay(self.far_sums(name)))
            elif what == "out":
                parts.append(SwapOut(self.pair(name)))
        results = travel(self.count, *parts)
        self.count += 1
        for (name, what), got in zip(errands, results[1:]):
            if what in ("in", "a", "b", "c", "ab", "bc"):
                self.rows[name] = got[0]
            else:
                {"far": self.far, "near": self.near, "relay": self.relayed, "out": self.met}[what][
                    name
                ] = got
        return results[0]

    def weight(self, name):
        rows = self.rows[name]
        return rows.reshape(-1, rows.shape[-1])

    def give_grad(self, name, grad):
        self.grads[name] = grad.astype(jnp.bfloat16).reshape(self.rows[name].shape)

    def own_rows(self, name, py, px, core):
        grad = self.grads[name]
        at = lax.dynamic_slice(grad, (py, px, core, 0, 0), (1, 1, 1) + grad.shape[3:])
        return at[0, 0, 0].astype(jnp.float32)

    def far_sums(self, name):
        y, x = lax.axis_index("py"), lax.axis_index("px")
        along_y, along_x = self.far[name]
        first = [
            self.own_rows(name, y, turned("px", e), 0) + jnp.sum(along_y[:, e - 1].astype(jnp.float32), 0)
            for e in range(1, lax.axis_size("px"))
        ]
        last = [
            self.own_rows(name, turned("py", e), x, 1) + jnp.sum(along_x[:, e - 1].astype(jnp.float32), 0)
            for e in range(1, lax.axis_size("py"))
        ]
        return jnp.stack(first).astype(jnp.bfloat16), jnp.stack(last).astype(jnp.bfloat16)

    def pair(self, name):
        y, x = lax.axis_index("py"), lax.axis_index("px")
        halves = []
        for core in range(2):
            near = jnp.sum(self.near[name][core].astype(jnp.float32), 0)
            relayed = jnp.sum(self.relayed[name][core].astype(jnp.float32), 0)
            halves.append(self.own_rows(name, y, x, core) + near + relayed)
        return jnp.stack(halves).astype(jnp.bfloat16)

    def total(self, name):
        met = self.met[name][0].astype(jnp.float32)
        return met[0] + met[1]


def scores_of(query, key, key_valid):
    scale = 1.0 / math.sqrt(HEAD_DIM)
    scores = jnp.einsum("bqhe,bkhe->bhqk", query, key, preferred_element_type=jnp.float32) * scale
    if key_valid is None:
        return scores
    return jnp.where(key_valid[:, None, None, :] > 0, scores, -1e30)


def attend_forward(query, key, value, key_valid):
    scores = scores_of(query, key, key_valid)
    peak = jnp.max(scores, -1, keepdims=True)
    expo = jnp.exp(scores - peak)
    total = jnp.sum(expo, -1, keepdims=True)
    probs = (expo / total).astype(jnp.bfloat16)
    context = jnp.einsum(
        "bhqk,bkhe->bqhe", probs, value, preferred_element_type=jnp.float32
    ).astype(jnp.bfloat16)
    return (context, peak + jnp.log(total))


def attend_backward(query, key, value, log_total, grad_context, key_valid):
    scale = 1.0 / math.sqrt(HEAD_DIM)
    probs = jnp.exp(scores_of(query, key, key_valid) - log_total)
    grad_value = jnp.einsum(
        "bhqk,bqhe->bkhe",
        probs.astype(jnp.bfloat16),
        grad_context,
        preferred_element_type=jnp.float32,
    ).astype(jnp.bfloat16)
    grad_probs = jnp.einsum(
        "bqhe,bkhe->bhqk", grad_context, value, preferred_element_type=jnp.float32
    )
    grad_scores = (probs * (grad_probs - jnp.sum(grad_probs * probs, -1, keepdims=True))).astype(
        jnp.bfloat16
    )
    grad_query = (
        jnp.einsum("bhqk,bkhe->bqhe", grad_scores, key, preferred_element_type=jnp.float32) * scale
    ).astype(jnp.bfloat16)
    grad_key = (
        jnp.einsum("bhqk,bqhe->bkhe", grad_scores, query, preferred_element_type=jnp.float32)
        * scale
    ).astype(jnp.bfloat16)
    return (grad_query, grad_key, grad_value)


def split_heads(triple):
    batch, length, three = triple.shape
    local = three // 3
    return [
        triple[:, :, i * local : (i + 1) * local].reshape(
            batch, length, local // HEAD_DIM, HEAD_DIM
        )
        for i in range(3)
    ]


def low_dot(spec, left, right):
    return jnp.einsum(spec, left, right, preferred_element_type=jnp.float32)


def block_forward(values, mod, key_valid, block, route):
    shift_a, scale_a, gate_a, shift_m, scale_m, gate_m = [mod[i] for i in range(6)]
    (normed,) = route.step(GroupCopy(modulate(values, shift_a, scale_a).astype(jnp.bfloat16)))
    triple = low_dot("bld,dc->blc", normed, route.weight(f"in{block}")).astype(jnp.bfloat16)
    context, log_total = attend_forward(*split_heads(triple), key_valid)
    flat_context = context.reshape(triple.shape[0], triple.shape[1], triple.shape[2] // 3)
    partial_attn = low_dot("ble,de->bld", flat_context, route.weight(f"out{block}"))
    (attn,) = route.step(OwnSum(partial_attn.astype(jnp.bfloat16)))
    middle = values + gate_a[None, :] * attn
    (normed_m,) = route.step(GroupCopy(modulate(middle, shift_m, scale_m).astype(jnp.bfloat16)))
    inner = low_dot("bld,df->blf", normed_m, route.weight(f"expand{block}"))
    active = jax.nn.gelu(inner, approximate=True).astype(jnp.bfloat16)
    partial_branch = low_dot("blf,df->bld", active, route.weight(f"contract{block}"))
    (branch,) = route.step(OwnSum(partial_branch.astype(jnp.bfloat16)))
    result = middle + gate_m[None, :] * branch
    saved = (values, middle, normed, normed_m, triple, flat_context)
    return (result, saved + (log_total, attn, inner, active, branch))


def block_backward(grad, mod, key_valid, block, saved, route):
    values, middle, normed, normed_m, triple, flat_context = saved[:6]
    log_total, attn, inner, active, branch = saved[6:]
    shift_a, scale_a, gate_a, shift_m, scale_m, gate_m = [mod[i] for i in range(6)]
    (grad_branch,) = route.step(GroupCopy((gate_m[None, :] * grad).astype(jnp.bfloat16)))
    grad_gate_m = jnp.sum(grad * branch, 0)
    grad_active = low_dot("bld,df->blf", grad_branch, route.weight(f"contract{block}"))
    gelu_back = jax.vjp(partial(jax.nn.gelu, approximate=True), inner)[1]
    grad_inner = gelu_back(grad_active)[0].astype(jnp.bfloat16)
    partial_normed = low_dot("blf,df->bld", grad_inner, route.weight(f"expand{block}"))
    route.give_grad(f"contract{block}", low_dot("bld,blf->df", grad_branch, active))
    route.give_grad(f"expand{block}", low_dot("bld,blf->df", normed_m, grad_inner))
    (grad_normed,) = route.step(OwnSum(partial_normed.astype(jnp.bfloat16)))
    _, modulate_back = jax.vjp(modulate, middle, shift_m, scale_m)
    grad_mid, grad_shift_m, grad_scale_m = modulate_back(grad_normed)
    grad_mid = grad + grad_mid
    (grad_attn,) = route.step(GroupCopy((gate_a[None, :] * grad_mid).astype(jnp.bfloat16)))
    grad_gate_a = jnp.sum(grad_mid * attn, 0)
    grad_flat = low_dot("bld,de->ble", grad_attn, route.weight(f"out{block}")).astype(jnp.bfloat16)
    route.give_grad(f"out{block}", low_dot("bld,ble->de", grad_attn, flat_context))
    query, key, value = split_heads(triple)
    grad_context = grad_flat.reshape(query.shape)
    grad_parts = attend_backward(query, key, value, log_total, grad_context, key_valid)
    grad_triple = jnp.concatenate([g.reshape(flat_context.shape) for g in grad_parts], 2)
    partial_normed = low_dot("blc,dc->bld", grad_triple, route.weight(f"in{block}"))
    route.give_grad(f"in{block}", low_dot("bld,blc->dc", normed, grad_triple))
    (grad_normed,) = route.step(OwnSum(partial_normed.astype(jnp.bfloat16)))
    _, modulate_back = jax.vjp(modulate, values, shift_a, scale_a)
    grad_values, grad_shift_a, grad_scale_a = modulate_back(grad_normed)
    grad_mod = jnp.stack(
        [grad_shift_a, grad_scale_a, grad_gate_a, grad_shift_m, grad_scale_m, grad_gate_m], 0
    )
    return (grad_mid + grad_values, grad_mod)


def both(what, block):
    return [(f"in{block}", what), (f"out{block}", what)]


def errands_in_turn():
    return [
        both("in", 0),
        both("ab", 0) + [("expand0", "in")],
        both("c", 0) + [("contract0", "in")],
        [("expand0", "ab")] + both("in", 1),
        [("expand0", "c"), ("contract0", "a"), ("expand1", "in")],
        [("contract0", "bc"), ("contract1", "in")],
        both("ab", 1),
        both("c", 1) + [("expand1", "a")],
        [("expand1", "bc"), ("contract1", "a")],
        [("contract1", "bc")],
        [],
        [],
        [("expand1", "far"), ("contract1", "far")],
        [("expand1", "near"), ("expand1", "relay")],
        [("contract1", "near"), ("contract1", "relay")],
        both("far", 1) + both("near", 1),
        both("relay", 1) + [("expand0", "far"), ("expand1", "out")],
        [("contract0", "far"), ("expand0", "near"), ("contract1", "out")],
        [("contract0", "near"), ("expand0", "relay")] + both("out", 1),
        [("contract0", "relay"), ("expand0", "out")] + both("far", 0),
        both("near", 0) + both("relay", 0) + [("contract0", "out")],
        both("out", 0),
        [],
        [],
    ]


def adam(weight, grad, moment, second, average, factor):
    grad = grad * factor
    moment = beta_first * moment + (1.0 - beta_first) * grad
    second = beta_second * second + (1.0 - beta_second) * grad * grad
    update = (
        moment
        / (1.0 - beta_first**STEP)
        / (jnp.sqrt(second / (1.0 - beta_second**STEP)) + adam_eps)
    )
    fresh = weight - learn_rate * (update + weight_decay * weight)
    average_decay = min(ema_decay, (1.0 + STEP) / (10.0 + STEP))
    average = average_decay * average + (1.0 - average_decay) * fresh
    return (fresh, moment, second, average)


def shards(
    patches,
    target_noise,
    kept_slots,
    kept_count,
    time_step,
    labels,
    teacher,
    *tables,
):
    params, moments, seconds, averages = tables[:7], tables[7:14], tables[14:21], tables[21:]
    attend_in, attend_out, expand, contract, modulation, patch_table, condition = params
    batch, length = (patches.shape[0], patches.shape[1])
    capacity = kept_slots.shape[1]
    rows, local = (attend_in.shape[1], attend_in.shape[3])
    wides, narrows = (group_size(WIDE), group_size(NARROW))
    wide_index, narrow_index = (flat_place(WIDE), flat_place(NARROW))
    images = batch * wides
    width = local * narrows
    assert batch == narrows

    shards_low = {}
    for i in range(2):
        shards_low[f"in{i}"] = attend_in[i].reshape(rows, 3 * local).astype(jnp.bfloat16)
        shards_low[f"out{i}"] = attend_out[i].T.astype(jnp.bfloat16)
        shards_low[f"expand{i}"] = expand[i].astype(jnp.bfloat16)
        shards_low[f"contract{i}"] = contract[i].T.astype(jnp.bfloat16)
    route = Route(shards_low, errands_in_turn())

    def own(array):
        return lax.dynamic_index_in_dim(array, narrow_index, 0, keepdims=False)

    condition_low = condition.astype(jnp.bfloat16)
    features = sinusoid(time_step, FREQ)
    onehot = (labels[:, None] == jnp.arange(CLASSES)[None, :]).astype(jnp.bfloat16)
    cond_part = jnp.dot(
        features, condition_low[:FREQ].astype(jnp.float32), precision=highest_float_accuracy
    ) + low_dot("bc,cd->bd", onehot, condition_low[FREQ:])
    facts = jnp.stack([kept_count, time_step, labels], 1).astype(jnp.float32)
    facts = jnp.pad(own(facts)[None, :], ((0, 7), (0, local - 3)))
    payload = jnp.concatenate([cond_part, own(teacher).reshape(narrows, local), facts], 0)
    table_pad = jnp.pad(patch_table.astype(jnp.bfloat16), ((0, 15), (0, 0)))
    everyone, tables_near = route.step(
        Exchange([payload, table_pad], [(ALL, "same"), (NARROW, "same")])
    )
    everyone = everyone.reshape(wides, narrows, batch + narrows + 8, local)
    cond_sum = jnp.transpose(everyone[:, :, :batch], (0, 2, 1, 3)).reshape(images, width)
    negatives = everyone[:, :, batch : batch + narrows].reshape(images, width)
    facts_all = everyone[:, :, batch + narrows, :3]
    time_all = facts_all[:, :, 1].reshape(images).astype(jnp.int32)
    labels_all = facts_all[:, :, 2].reshape(images).astype(jnp.int32)
    patch_full = jnp.transpose(tables_near, (1, 0, 2)).reshape(48, width)[:33]
    silu_low = jax.nn.silu(cond_sum).astype(jnp.bfloat16)
    silu_rows = lax.dynamic_slice_in_dim(silu_low, wide_index * rows, rows, 1)
    modulation_low = modulation.astype(jnp.bfloat16)
    mod_part = low_dot("ip,npkc->inkc", silu_rows, modulation_low)
    mod_part = mod_part.reshape(wides, batch, 12, local)
    (mod_wide,) = route.step(Exchange([mod_part], [(WIDE, "each")]))
    (mod_near,) = route.step(Exchange([jnp.sum(mod_wide, 0)], [(NARROW, "each")]))
    mods = jnp.transpose(mod_near, (1, 0, 2)).reshape(2, 6, width)

    count_own = own(kept_count).astype(jnp.float32)
    slot_valid = (jnp.arange(capacity) < own(kept_count)).astype(jnp.float32)
    select = (own(kept_slots)[:, None] == jnp.arange(length)[None, :]).astype(
        jnp.float32
    ) * slot_valid[:, None]
    kept_place = jnp.sum(select, 0)
    places = sinusoid(jnp.arange(length), width)
    group_counts = lax.dynamic_slice(
        facts_all[:, :, 0],
        (flat_place(("py", "px")) * 2, lax.axis_index("zh") * 2),
        (2, 2),
    ).reshape(4)
    group_valid = (jnp.arange(capacity)[None, :] < group_counts[:, None]).astype(jnp.float32)
    kept_patches = low_dot("cl,lp->cp", select.astype(jnp.bfloat16), own(patches))
    embed = low_dot("cp,pd->cd", kept_patches.astype(jnp.bfloat16), patch_full[:PATCH_IN])
    embed = embed + jnp.dot(select, places, precision=highest_float_accuracy)
    encoded, saved_enc = block_forward(embed, mods[0], group_valid, 0, route)

    def pool_unit(values):
        pooled = jnp.sum(values * slot_valid[:, None], 0) / count_own
        return pooled * lax.rsqrt(jnp.sum(pooled * pooled, -1, keepdims=True) + 1e-06)

    normalised_direction, pool_back = jax.vjp(pool_unit, encoded)
    frozen_target_direction = negatives * lax.rsqrt(
        jnp.sum(negatives * negatives, -1, keepdims=True) + 1e-06
    )
    cosine_match_scores = (
        jnp.sum(normalised_direction[None, :] * frozen_target_direction, -1)
        / contrast_sharpness_divisor
    )
    peak = jnp.max(cosine_match_scores)
    expo = jnp.exp(cosine_match_scores - peak)
    total = jnp.sum(expo)
    positive = ((wide_index * batch + narrow_index) == jnp.arange(images)).astype(jnp.float32)
    nce_local = peak + jnp.log(total) - jnp.sum(cosine_match_scores * positive)
    derivative_of_raw_scores = (expo / total - positive) * (nce_weight / images)
    unit_vector_gradient = (
        jnp.sum(derivative_of_raw_scores[:, None] * frozen_target_direction, 0)
        / contrast_sharpness_divisor
    )
    grad_pool = pool_back(unit_vector_gradient)[0]
    mask_token = patch_full[2 * PATCH_IN].astype(jnp.float32)
    decode_in = jnp.einsum("cl,cd->ld", select, encoded, precision=highest_float_accuracy)
    decode_in = decode_in + (1.0 - kept_place)[:, None] * mask_token + places
    decoded, saved_dec = block_forward(decode_in, mods[1], None, 1, route)
    final, final_back = jax.vjp(layer_norm, decoded)
    final_low = final.astype(jnp.bfloat16)
    head = patch_full[PATCH_IN : 2 * PATCH_IN]
    predict = low_dot("ld,pd->lp", final_low, head)
    error_map = predict - own(target_noise)
    count_all = images * length * PATCH_IN
    mse_local = jnp.sum(error_map * error_map)
    grad_predict = (error_map * (2.0 / count_all)).astype(jnp.bfloat16)
    grad_head = low_dot("lp,ld->pd", grad_predict, final_low)
    grad_final = low_dot("lp,pd->ld", grad_predict, head)
    grad_decoded = final_back(grad_final)[0]
    grad_dec_in, grad_mod_dec = block_backward(grad_decoded, mods[1], None, 1, saved_dec, route)
    grad_mask = jnp.sum((1.0 - kept_place)[:, None] * grad_dec_in, 0)
    grad_encoded = jnp.dot(select, grad_dec_in, precision=highest_float_accuracy) + grad_pool
    grad_embed, grad_mod_enc = block_backward(
        grad_encoded, mods[0], group_valid, 0, saved_enc, route
    )
    grad_patch = jnp.einsum(
        "cp,cd->pd", kept_patches, grad_embed, precision=highest_float_accuracy
    )

    grad_mods = jnp.stack([grad_mod_enc, grad_mod_dec]).reshape(12, narrows, local)
    grad_mods = jnp.transpose(grad_mods, (1, 0, 2))
    grad_table = jnp.concatenate([grad_patch, grad_head, grad_mask[None, :]], 0)
    grad_table = jnp.transpose(grad_table.reshape(33, narrows, local), (1, 0, 2))
    grad_table = jnp.pad(grad_table, ((0, 0), (0, 7), (0, 0)))
    mods_near, table_near = route.step(
        Exchange([grad_mods, grad_table], [(NARROW, "each"), (NARROW, "each")])
    )
    table_sum = jnp.pad(jnp.sum(table_near, 0), ((0, 8), (0, 0))).astype(jnp.bfloat16)
    mods_all, table_all = route.step(
        Exchange([mods_near, table_sum], [(WIDE, "same"), (WIDE, "same")])
    )
    grad_patch_table = jnp.sum(table_all.astype(jnp.float32), 0)[:33]
    mods_all = mods_all.reshape(images, 2, 6, local)
    silu_broad = silu_rows.astype(jnp.float32)
    grad_modulation = jnp.einsum(
        "ip,inkc->npkc", silu_broad, mods_all, precision=highest_float_accuracy
    )
    grad_silu = jnp.einsum(
        "inkc,npkc->ip",
        mods_all,
        modulation_low.astype(jnp.float32),
        precision=highest_float_accuracy,
    )
    (silu_near,) = route.step(Exchange([grad_silu], [(NARROW, "same")]))
    (silu_wide,) = route.step(Exchange([jnp.sum(silu_near, 0)], [(WIDE, "same")]))
    grad_silu = jnp.transpose(silu_wide, (1, 0, 2)).reshape(images, width)
    grad_silu = lax.dynamic_slice_in_dim(grad_silu, narrow_index * local, local, 1)
    cond_cols = lax.dynamic_slice_in_dim(cond_sum, narrow_index * local, local, 1)
    grad_cond = jax.vjp(jax.nn.silu, cond_cols)[1](grad_silu)[0]
    features_all = sinusoid(time_all, FREQ)
    onehot_all = (labels_all[:, None] == jnp.arange(CLASSES)[None, :]).astype(jnp.float32)
    grad_condition = jnp.dot(
        jnp.concatenate([features_all, onehot_all], 1).T, grad_cond, precision=highest_float_accuracy
    )

    totals = {name: route.total(name) for name in shards_low}

    def stacked(name, shape):
        return jnp.stack([shape(totals[f"{name}{i}"]) for i in range(2)])

    grads = [
        stacked("in", lambda g: g.reshape(rows, 3, local)),
        stacked("out", lambda g: g.T),
        stacked("expand", lambda g: g),
        stacked("contract", lambda g: g.T),
        grad_modulation,
        grad_patch_table,
        grad_condition,
    ]
    square_big = jnp.sum(grad_modulation * grad_modulation)
    for g in totals.values():
        square_big = square_big + jnp.sum(g * g)
    square_small = jnp.sum(grad_patch_table * grad_patch_table) + jnp.sum(
        grad_condition * grad_condition
    )
    square_local = square_big + (wide_index == 0).astype(jnp.float32) * square_small
    scalars = jnp.stack([mse_local, nce_local, square_local])
    scalars = jnp.pad(scalars[None, :], ((0, 7), (0, 125)))
    (scalars_all,) = route.step(Exchange([scalars], [(ALL, "same")]))
    sums = jnp.sum(scalars_all[:, 0], 0)
    grad_norm = jnp.sqrt(sums[2])
    factor = clip_norm / jnp.maximum(grad_norm, clip_norm)
    fresh = [
        adam(params[i], grads[i], moments[i], seconds[i], averages[i], factor) for i in range(7)
    ]
    loss_parts = jnp.stack([sums[0] / count_all, sums[1] / images])
    return (loss_parts, grad_norm) + tuple(fresh[i][k] for k in range(4) for i in range(7))


def solution(mesh):
    wide, narrow = mesh.devices.shape
    planes = wide // 2
    across = max(n for n in range(1, math.isqrt(planes) + 1) if planes % n == 0)
    grid = Mesh(mesh.devices.reshape(across, planes // across, 2, narrow // 2, 2), ALL)
    image_specs = (
        P(WIDE, None, None),
        P(WIDE, None, None),
        P(WIDE, None),
        P(WIDE),
        P(WIDE),
        P(WIDE),
        P(WIDE, None),
    )
    table_specs = (
        P(None, WIDE, None, NARROW),
        P(None, NARROW, WIDE),
        P(None, WIDE, NARROW),
        P(None, NARROW, WIDE),
        P(None, WIDE, None, NARROW),
        P(None, NARROW),
        P(None, NARROW),
    )
    return jax.shard_map(
        shards,
        mesh=grid,
        in_specs=image_specs + table_specs * 4,
        out_specs=(P(), P()) + table_specs * 4,
        check_vma=False,
    )
```

```python
from functools import partial
import math

import jax
import jax.numpy as jnp
from jax import lax
from jax.experimental import pallas as pl
from jax.experimental.pallas import tpu as pltpu
from jax.sharding import Mesh
from jax.sharding import PartitionSpec as P

HEAD_DIM = 72
CLASSES = 1000
FREQ = 256
PATCH_IN = 16
STEP = 10

MESH = pl.DeviceIdType.MESH
PY, PX, CORE, ZH, ZL = "py", "px", "core", "zh", "zl"
WIDE = (PY, PX, CORE)
NARROW = (ZH, ZL)
ALL = WIDE + NARROW
EACH, SAME = range(2)
IN, OUT, EXPAND, CONTRACT = range(4)
TERM_SQUARE, TERM_HEAD, TERM_GATE, TERM_SHIFT, TERM_SCALE, TERM_MASK, TERM_PATCH = range(7)
ENTER, STRAIGHT, CROSS, RELAY, FAR, NEAR, PASS, LEAVE = range(8)

highest_float_accuracy = lax.Precision.HIGHEST
norm_eps = 1e-06
contrast_sharpness_divisor = 0.02
nce_weight = 0.5
learn_rate = 0.05
beta_first = 0.9
beta_second = 0.999
adam_eps = 1e-08
weight_decay = 0.05
clip_norm = 0.05
ema_decay = 0.9999


def layer_norm(values):
    center = values - jnp.mean(values, -1, keepdims=True)
    return center * lax.rsqrt(jnp.mean(center * center, -1, keepdims=True) + norm_eps)


def modulate(values, shift, scale):
    return layer_norm(values) * (1.0 + scale[None, :]) + shift[None, :]


def sinusoid(places, width):
    half = width // 2
    freqs = jnp.exp(-math.log(10000.0) * jnp.arange(half, dtype=jnp.float32) / half)
    angle = places.astype(jnp.float32)[:, None] * freqs[None, :]
    return jnp.concatenate([jnp.cos(angle), jnp.sin(angle)], -1)


def flat_place(axes):
    place = 0
    for axis in axes:
        place = place * lax.axis_size(axis) + lax.axis_index(axis)
    return place


def group_size(axes):
    size = 1
    for axis in axes:
        size = size * lax.axis_size(axis)
    return size


def device_at(axes, place):
    where = {}
    for axis in reversed(axes):
        where[axis] = lax.rem(place, lax.axis_size(axis))
        place = place // lax.axis_size(axis)
    return where


def turned(axis, offset):
    size = lax.axis_size(axis)
    return lax.rem(lax.axis_index(axis) + (offset % size), size)


def other(axis):
    return 1 - lax.axis_index(axis)


class Part:
    def __init__(self):
        self.arrays, self.in_spaces = [], []
        self.shapes, self.out_spaces = [], []
        self.aliases = {}
        self.scratch = []
        self.peers = []

    def take(self, array, space=pltpu.HBM):
        self.arrays.append(array)
        self.in_spaces.append(space)
        return len(self.arrays) - 1

    def give(self, shape, dtype=jnp.bfloat16, space=pltpu.HBM, source=None):
        held = pltpu.HBM if space == pltpu.HBM else jax.ShapeDtypeStruct
        self.shapes.append(held(shape, dtype))
        self.out_spaces.append(space)
        if source is not None:
            self.aliases[source] = len(self.shapes) - 1
        return len(self.shapes) - 1

    def greet(self, barrier):
        for peer in self.peers:
            pl.semaphore_signal(barrier, inc=1, device_id=peer(), device_id_type=MESH)
        return len(self.peers)

    def begin(self, ins, outs, scratch, halfway):
        pass

    def go(self, step, ins, outs, scratch):
        pass


class Exchange(Part):
    def __init__(self, arrays, specs):
        super().__init__()
        self.specs = specs
        for array, (axes, mode) in zip(arrays, specs):
            size = group_size(axes)
            piece = array.shape[1:] if mode == EACH else array.shape
            self.take(array, pltpu.VMEM)
            self.give((size,) + piece, array.dtype, pltpu.VMEM)
            self.scratch += [pltpu.SemaphoreType.DMA((size,)), pltpu.SemaphoreType.DMA((size,))]

    def greet(self, barrier):
        greeted = 0
        for axes, _ in self.specs:
            size, me = group_size(axes), flat_place(axes)
            greeted += size - 1

            def signal(offset, carry, axes=axes, size=size, me=me):
                target = lax.rem(me + offset, size)
                pl.semaphore_signal(
                    barrier, inc=1, device_id=device_at(axes, target), device_id_type=MESH
                )
                return carry

            lax.fori_loop(1, size, signal, 0)
        return greeted

    def begin(self, ins, outs, scratch, halfway):
        def copy_to(index, offset, arriving):
            axes, mode = self.specs[index]
            size, me = group_size(axes), flat_place(axes)
            target = lax.rem(me + offset, size)
            return pltpu.make_async_remote_copy(
                src_ref=ins[index].at[target] if mode == EACH else ins[index],
                dst_ref=outs[index].at[target if arriving else me],
                send_sem=scratch[2 * index].at[target],
                recv_sem=scratch[2 * index + 1].at[target if arriving else me],
                device_id=device_at(axes, target),
                device_id_type=MESH,
            )

        for index, (axes, mode) in enumerate(self.specs):

            def start(offset, carry, index=index):
                copy_to(index, offset, False).start()
                return carry

            lax.fori_loop(1, group_size(axes), start, 0)
        for index, (axes, mode) in enumerate(self.specs):
            me = flat_place(axes)
            outs[index][me] = ins[index][me] if mode == EACH else ins[index][...]
        for index, (axes, mode) in enumerate(self.specs):

            def end(offset, carry, index=index):
                copy_to(index, offset, True).wait_recv()
                copy_to(index, offset, False).wait_send()
                return carry

            lax.fori_loop(1, group_size(axes), end, 0)
        halfway()


class Norm(Exchange):
    def __init__(self, scalars, mets):
        super().__init__([scalars], [(ALL, SAME)])
        for met in mets:
            self.take(met, pltpu.VMEM)
        self.scratch.append(pltpu.VMEM(scalars.shape, jnp.float32))

    def begin(self, ins, outs, scratch, halfway):
        square = jnp.zeros((8, 128), jnp.float32)
        for met in ins[1:]:
            total = met[0].astype(jnp.float32) + met[1].astype(jnp.float32)
            columns = total.shape[1]
            squares = total * total
            if squares.shape[0] % 8:
                squares = jnp.pad(fold(squares), ((0, 7), (0, 0)))
            eights = jnp.sum(squares.reshape(-1, 8, columns), 0)
            for start in range(0, columns, 128):
                lanes = eights[:, start : start + 128]
                if lanes.shape[1] < 128:
                    lanes = jnp.pad(lanes, ((0, 0), (0, 128 - lanes.shape[1])))
                square = square + lanes
        lane = lax.broadcasted_iota(jnp.int32, (8, 128), 1)
        scratch[2][...] = ins[0][...] + jnp.where(lane == 2, jnp.sum(square), 0.0)
        super().begin([scratch[2]], outs, scratch[:2], halfway)


class RowPieces(Part):
    def __init__(self, pieces):
        super().__init__()
        self.each = pieces.shape[0]
        wides, narrows = group_size(WIDE), group_size(NARROW)
        self.take(pieces, pltpu.VMEM)
        self.give((wides,) + pieces.shape[1:], pieces.dtype, pltpu.VMEM)
        self.scratch = [
            pltpu.SemaphoreType.DMA((self.each * narrows,)),
            pltpu.SemaphoreType.DMA((wides,)),
        ]

    def sends(self):
        narrows, me = group_size(NARROW), flat_place(WIDE) * group_size(NARROW) + flat_place(NARROW)
        for j in range(self.each):
            for z in range(narrows):
                wide = flat_place(NARROW) * self.each + j
                to = {**device_at(WIDE, wide), **device_at(NARROW, jnp.int32(z))}
                yield j, z, to, wide * narrows + z != me

    def receives(self):
        narrows, me = group_size(NARROW), flat_place(WIDE) * group_size(NARROW) + flat_place(NARROW)
        z = flat_place(WIDE) // self.each
        for w in range(group_size(WIDE)):
            to = {**device_at(WIDE, jnp.int32(w)), **device_at(NARROW, z)}
            yield w, to, w * narrows + z != me

    def greet(self, barrier):
        for _, _, to, remote in self.sends():

            @pl.when(remote)
            def _(to=to):
                pl.semaphore_signal(barrier, inc=1, device_id=to, device_id_type=MESH)

        for _, to, remote in self.receives():

            @pl.when(remote)
            def _(to=to):
                pl.semaphore_signal(barrier, inc=1, device_id=to, device_id_type=MESH)

        counts = [r.astype(jnp.int32) for _, _, _, r in self.sends()]
        counts += [r.astype(jnp.int32) for _, _, r in self.receives()]
        return sum(counts)

    def begin(self, ins, outs, scratch, halfway):
        me = flat_place(WIDE)
        z = flat_place(WIDE) // self.each
        narrows = group_size(NARROW)

        def copy(j, slot, sem, to):
            return pltpu.make_async_remote_copy(
                src_ref=ins[0].at[j],
                dst_ref=outs[0].at[slot],
                send_sem=scratch[0].at[sem],
                recv_sem=scratch[1].at[slot],
                device_id=to,
                device_id_type=MESH,
            )

        for j, t, to, remote in self.sends():

            @pl.when(remote)
            def _(j=j, t=t, to=to):
                copy(j, me, j * narrows + t, to).start()

            @pl.when(jnp.logical_not(remote))
            def _(j=j):
                outs[0][me] = ins[0][j]

        for w, to, remote in self.receives():

            @pl.when(remote)
            def _(w=w, to=to):
                copy(0, w, 0, to).wait_recv()

        for j, t, to, remote in self.sends():

            @pl.when(remote)
            def _(j=j, t=t, to=to):
                copy(j, me, j * narrows + t, to).wait_send()

        halfway()


def chunk_of(length):
    return 64 if length % 64 == 0 else 32


def normal(values):
    center = values - jnp.mean(values, -1, keepdims=True)
    scale = lax.rsqrt(jnp.mean(center * center, -1, keepdims=True) + norm_eps)
    return center * scale, scale


def normal_back(grad, unit, scale):
    flat = jnp.mean(grad, -1, keepdims=True)
    tilt = jnp.mean(grad * unit, -1, keepdims=True)
    return scale * (grad - flat - unit * tilt)


def fold(values):
    return jnp.sum(values, 0, keepdims=True)


def full_dot(left, right):
    return jnp.dot(
        left, right, precision=highest_float_accuracy, preferred_element_type=jnp.float32
    )


SHIFT_A, SCALE_A, GATE_A, SHIFT_M, SCALE_M, GATE_M = range(6)


class Bridge(Part):
    whole = False
    sends_on = True

    def __init__(self, terms, more, width, length_in, length_out):
        super().__init__()
        self.length_in, self.length_out, self.width = length_in, length_out, width
        self.sums = terms is not None
        self.first = 0
        if self.sums:
            self.take(terms, pltpu.VMEM)
            self.first = 1
        for array in more:
            self.take(array, pltpu.VMEM)
        if self.sends_on:
            self.give((4, length_out, width), jnp.bfloat16, pltpu.VMEM)
        self.peers = [lambda: {CORE: other(CORE)}, lambda: {ZL: other(ZL)}]
        self.scratch = []
        if self.sums:
            self.scratch += [pltpu.VMEM((length_in, width), jnp.bfloat16)] * 4
            self.scratch += self.sems(length_in)
        if self.sends_on:
            self.scratch += self.sems(length_out)

    def result(self, shape, dtype=jnp.float32):
        self.give(shape, dtype, pltpu.VMEM)

    def sems(self, length):
        steps = length // chunk_of(length)
        return [pltpu.SemaphoreType.DMA((3, steps)), pltpu.SemaphoreType.DMA((3, steps))]

    def ranks(self):
        core, low = lax.axis_index(CORE), lax.axis_index(ZL)
        return core * 2 + low, (1 - core) * 2 + low, core * 2 + 1 - low, (1 - core) * 2 + 1 - low

    def copy(self, source, target, sems, kind, step):
        return pltpu.make_async_remote_copy(
            src_ref=source,
            dst_ref=target,
            send_sem=sems[0].at[kind, step],
            recv_sem=sems[1].at[kind, step],
            device_id={ZL: other(ZL)} if kind == 0 else {CORE: other(CORE)},
            device_id_type=MESH,
        )

    def rows(self, length):
        chunk = chunk_of(length)
        return [pl.ds(s * chunk, chunk) for s in range(length // chunk)]

    def begin(self, ins, outs, scratch, halfway):
        me, mate, away, away_mate = self.ranks()
        given = ins[self.first :]
        made = outs[1:] if self.sends_on else outs
        state = self.start(given, made)
        sends = []
        rows_in, rows_out = self.rows(self.length_in), self.rows(self.length_out)
        if self.sums:
            terms = ins[0]
            near, home, stage, far = scratch[:4]
            sems = scratch[4:6]
            to_near = [
                self.copy(terms.at[away_mate, r], near.at[r], sems, 1, s)
                for s, r in enumerate(rows_in)
            ]
            to_home = [
                self.copy(terms.at[mate, r], home.at[r], sems, 2, s) for s, r in enumerate(rows_in)
            ]
            to_far = [self.copy(stage.at[r], far.at[r], sems, 0, s) for s, r in enumerate(rows_in)]
            for each in to_near:
                each.start()
            for each in to_home:
                each.start()
            for s, r in enumerate(rows_in):
                to_near[s].wait_recv()
                both = terms[away, r].astype(jnp.float32) + near[r].astype(jnp.float32)
                stage[r] = both.astype(jnp.bfloat16)
                to_far[s].start()
            sends += to_near + to_home + to_far

            def total(s, r):
                to_home[s].wait_recv()
                own = terms[me, r].astype(jnp.float32) + home[r].astype(jnp.float32)
                to_far[s].wait_recv()
                return own + far[r].astype(jnp.float32)

        else:

            def total(s, r):
                return None

        if self.sends_on:
            every = outs[0]
            sems_out = scratch[-2:]

            def move(kind, here, there, s, r):
                return self.copy(every.at[here, r], every.at[there, r], sems_out, kind, s)

            def pass_on(s, r, fresh):
                every[me, r] = fresh
                for kind in (0, 1):
                    each = move(kind, me, me, s, r)
                    each.start()
                    sends.append(each)

        if self.whole:
            for s, r in enumerate(rows_in):
                self.collect(r, total(s, r), given, made, state)
            self.turn(given, made, state)
            for s, r in enumerate(rows_out):
                pass_on(s, r, self.work(r, None, given, made, state))
        else:
            for s, r in enumerate(rows_in):
                fresh = self.work(r, total(s, r), given, made, state)
                if self.sends_on:
                    pass_on(s, r, fresh)
        self.end(given, made, state)
        self.aside(given, made)
        if self.sums:
            halfway()
        if self.sends_on:
            for s, r in enumerate(rows_out):
                move(0, me, away, s, r).wait_recv()
                each = move(2, away, away, s, r)
                each.start()
                sends.append(each)
            for s, r in enumerate(rows_out):
                move(1, me, mate, s, r).wait_recv()
                move(2, away, away_mate, s, r).wait_recv()
        for each in sends:
            each.wait_send()
        if not self.sums:
            halfway()

    def start(self, given, made):
        return {}

    def add(self, state, name, value):
        state[name] = value if name not in state else state[name] + value

    def end(self, given, made, state):
        pass

    def aside(self, given, made):
        pass


def outer(left, right, result):
    step = 384 if left.shape[2] % 384 == 0 else 128

    def tile(i, carry):
        columns = pl.ds(pl.multiple_of(i * step, step), step)
        value = lax.dot_general(
            left[:, :, columns].reshape(-1, step),
            right[...].reshape(-1, right.shape[2]),
            (((0,), (0,)), ((), ())),
            preferred_element_type=jnp.float32,
        )
        result[columns] = value.astype(jnp.bfloat16)
        return carry

    lax.fori_loop(0, left.shape[2] // step, tile, 0)


class Enter(Bridge):
    def __init__(self, values, mod):
        length, width = values.shape
        super().__init__(None, [values, mod], width, length, length)

    def work(self, r, total, given, made, state):
        values, mod = given
        unit, _ = normal(values[r])
        return (unit * (1.0 + mod[SCALE_A : SCALE_A + 1]) + mod[SHIFT_A : SHIFT_A + 1]).astype(
            jnp.bfloat16
        )


class Middle(Bridge):
    def __init__(self, terms, values, mod):
        length, width = values.shape
        super().__init__(terms, [values, mod], width, length, length)
        self.result((length, width))
        self.result((length, width))

    def work(self, r, total, given, made, state):
        values, mod = given
        attn, middle = made
        attn[r] = total
        fresh = values[r] + mod[GATE_A : GATE_A + 1] * total
        middle[r] = fresh
        unit, _ = normal(fresh)
        return (unit * (1.0 + mod[SCALE_M : SCALE_M + 1]) + mod[SHIFT_M : SHIFT_M + 1]).astype(
            jnp.bfloat16
        )


class Decode(Bridge):
    whole = True

    def __init__(self, terms, middle, mod, mod_next, place, base):
        (length, width), (length_next, _) = middle.shape, base.shape
        super().__init__(terms, [middle, mod, mod_next, place, base], width, length, length_next)
        self.result((length, width))
        self.result((length, width))
        self.result((length_next, width))

    def collect(self, r, total, given, made, state):
        middle, mod = given[:2]
        branch, encoded = made[:2]
        branch[r] = total
        encoded[r] = middle[r] + mod[GATE_M : GATE_M + 1] * total

    def turn(self, given, made, state):
        place, base = given[3:]
        made[2][...] = full_dot(place[...], made[1][...]) + base[...]

    def work(self, r, total, given, made, state):
        mod = given[2]
        unit, _ = normal(made[2][r])
        return (unit * (1.0 + mod[SCALE_A : SCALE_A + 1]) + mod[SHIFT_A : SHIFT_A + 1]).astype(
            jnp.bfloat16
        )


class Turn(Bridge):
    def __init__(self, terms, middle, mod, head, noise, count_all):
        length, width = middle.shape
        super().__init__(terms, [middle, mod, head, noise], width, length, length)
        self.scale = 2.0 / count_all
        self.result((length, width))
        self.result((1, width))
        self.result(head.shape)
        self.result((1, 1))

    def work(self, r, total, given, made, state):
        middle, mod, head, noise = given
        gate = mod[GATE_M : GATE_M + 1]
        unit, scale = normal(middle[r] + gate * total)
        low = unit.astype(jnp.bfloat16)
        rows_by_rows = (((1,), (1,)), ((), ()))
        predict = lax.dot_general(low, head[...], rows_by_rows, preferred_element_type=jnp.float32)
        error = predict - noise[r]
        self.add(state, TERM_SQUARE, jnp.sum(error * error, keepdims=True))
        grad_predict = (error * self.scale).astype(jnp.bfloat16)
        columns_by_columns = (((0,), (0,)), ((), ()))
        self.add(
            state,
            TERM_HEAD,
            lax.dot_general(
                grad_predict, low, columns_by_columns, preferred_element_type=jnp.float32
            ),
        )
        grad_final = jnp.dot(grad_predict, head[...], preferred_element_type=jnp.float32)
        grad = normal_back(grad_final, unit, scale)
        made[0][r] = grad
        self.add(state, TERM_GATE, fold(grad * total))
        return (gate * grad).astype(jnp.bfloat16)

    def end(self, given, made, state):
        made[1][...] = state[TERM_GATE]
        made[2][...] = state[TERM_HEAD]
        made[3][...] = state[TERM_SQUARE]


class MiddleBack(Bridge):
    def __init__(self, terms, middle, attn, grad, mod):
        length, width = middle.shape
        super().__init__(terms, [middle, attn, grad, mod], width, length, length)
        self.result((length, width))
        self.result((3, width))

    def work(self, r, total, given, made, state):
        middle, attn, grad, mod = given
        unit, scale = normal(middle[r])
        self.add(state, TERM_SHIFT, fold(total))
        self.add(state, TERM_SCALE, fold(total * unit))
        back = normal_back(total * (1.0 + mod[SCALE_M : SCALE_M + 1]), unit, scale)
        fresh = grad[r] + back
        made[0][r] = fresh
        self.add(state, TERM_GATE, fold(fresh * attn[r]))
        return (mod[GATE_A : GATE_A + 1] * fresh).astype(jnp.bfloat16)

    def end(self, given, made, state):
        made[1][0:1] = state[TERM_SHIFT]
        made[1][1:2] = state[TERM_SCALE]
        made[1][2:3] = state[TERM_GATE]


class Encode(Bridge):
    whole = True

    def __init__(self, terms, values, grad, mod, open_place, select, pool, branch, mod_next, pairs):
        (length, width), (length_next, _) = values.shape, branch.shape
        super().__init__(
            terms,
            [values, grad, mod, open_place, select, pool, branch, mod_next, *pairs],
            width,
            length,
            length_next,
        )
        self.result((length_next, width))
        self.result((4, width))
        self.result((width, pairs[1].shape[2]), jnp.bfloat16)
        self.result((width, pairs[3].shape[2]), jnp.bfloat16)
        self.scratch = [pltpu.VMEM((length, width), jnp.float32)] + self.scratch

    def begin(self, ins, outs, scratch, halfway):
        self.held = scratch[0]
        super().begin(ins, outs, scratch[1:], halfway)

    def collect(self, r, total, given, made, state):
        values, grad, mod, open_place = given[:4]
        unit, scale = normal(values[r])
        self.add(state, TERM_SHIFT, fold(total))
        self.add(state, TERM_SCALE, fold(total * unit))
        back = normal_back(total * (1.0 + mod[SCALE_A : SCALE_A + 1]), unit, scale)
        fresh = grad[r] + back
        self.held[r] = fresh
        self.add(state, TERM_MASK, fold(open_place[r] * fresh))

    def turn(self, given, made, state):
        select, pool = given[4:6]
        made[0][...] = full_dot(select[...], self.held[...]) + pool[...]

    def work(self, r, total, given, made, state):
        branch, mod_next = given[6:8]
        fresh = made[0][r]
        self.add(state, TERM_GATE, fold(fresh * branch[r]))
        return (mod_next[GATE_M : GATE_M + 1] * fresh).astype(jnp.bfloat16)

    def end(self, given, made, state):
        made[1][0:1] = state[TERM_SHIFT]
        made[1][1:2] = state[TERM_SCALE]
        made[1][2:3] = state[TERM_GATE]
        made[1][3:4] = state[TERM_MASK]

    def aside(self, given, made):
        outer(given[8], given[9], made[2])
        outer(given[10], given[11], made[3])


class Leave(Bridge):
    sends_on = False

    def __init__(self, terms, values, grad, mod, kept, sums, pairs):
        length, width = values.shape
        super().__init__(terms, [values, grad, mod, kept, *sums, *pairs], width, length, length)
        narrows = group_size(NARROW)
        piece = jax.ShapeDtypeStruct((narrows, 48, width // narrows), jnp.float32)
        self.tell = Exchange([piece], [(NARROW, EACH)])
        self.result(piece.shape)
        self.result((width, pairs[1].shape[2]), jnp.bfloat16)
        self.result((width, pairs[3].shape[2]), jnp.bfloat16)
        self.scratch = (
            [pltpu.VMEM((48, width), jnp.float32), pltpu.VMEM(piece.shape, jnp.float32)]
            + self.tell.scratch
            + self.scratch
        )

    def greet(self, barrier):
        return super().greet(barrier) + self.tell.greet(barrier)

    def begin(self, ins, outs, scratch, halfway):
        self.table, self.piece = scratch[:2]
        self.tell_sems = scratch[2:4]
        super().begin(ins, outs, scratch[4:], halfway)

    def work(self, r, total, given, made, state):
        values, grad, mod, kept = given[:4]
        unit, scale = normal(values[r])
        self.add(state, TERM_SHIFT, fold(total))
        self.add(state, TERM_SCALE, fold(total * unit))
        back = normal_back(total * (1.0 + mod[SCALE_A : SCALE_A + 1]), unit, scale)
        columns_by_columns = (((0,), (0,)), ((), ()))
        self.add(
            state,
            TERM_PATCH,
            lax.dot_general(
                kept[r],
                grad[r] + back,
                columns_by_columns,
                precision=highest_float_accuracy,
                preferred_element_type=jnp.float32,
            ),
        )

    def end(self, given, made, state):
        sums_m0, sums_a1, sums_m1, gate_m1, head = given[4:9]
        table = self.table
        table[...] = jnp.zeros(table.shape, jnp.float32)
        table[0:1] = state[TERM_SHIFT]
        table[1:2] = state[TERM_SCALE]
        table[2:3] = sums_m0[2:3]
        table[3:5] = sums_m0[0:2]
        table[5:6] = sums_a1[2:3]
        table[6:8] = sums_a1[0:2]
        table[8:9] = sums_m1[2:3]
        table[9:11] = sums_m1[0:2]
        table[11:12] = gate_m1[...]
        table[12:28] = state[TERM_PATCH]
        table[28:44] = head[...]
        table[44:45] = sums_a1[3:4]
        local = self.piece.shape[2]
        for z in range(self.piece.shape[0]):
            self.piece[z] = table[:, z * local : (z + 1) * local]
        self.tell.begin([self.piece], made[:1], self.tell_sems, lambda: None)

    def aside(self, given, made):
        outer(given[9], given[10], made[1])
        outer(given[11], given[12], made[2])


class Errand(Part):
    def plan(self, ins, outs):
        raise NotImplementedError

    def local(self, ins, outs):
        return []

    def reserve(self, count, local=0):
        self.scratch = [pltpu.SemaphoreType.DMA((count,)), pltpu.SemaphoreType.DMA((count,))]
        if local:
            self.scratch.append(pltpu.SemaphoreType.DMA((local,)))

    def go(self, step, ins, outs, scratch):
        first = 0
        plans = self.plan(ins, outs)
        if step == 1 and len(plans) == 1:
            return
        for turn, moves in enumerate(plans):
            last = turn == len(plans) - 1
            if step == (2 if last else turn + 1):
                self.run(moves, first, scratch, True)
            if step == turn:
                self.run(moves, first, scratch, False)
            first += len(moves)
        if step != 1:
            for i, (source, target, when) in enumerate(self.local(ins, outs)):

                def act_local(i=i, source=source, target=target):
                    copy = pltpu.make_async_copy(source, target, scratch[2].at[i])
                    if step:
                        copy.wait()
                    else:
                        copy.start()

                pl.when(when)(act_local)

    def run(self, moves, first, scratch, ending):
        for i, (source, target, landing, device, when) in enumerate(moves):

            def remote(place, i=first + i, source=source, device=device):
                return pltpu.make_async_remote_copy(
                    src_ref=source,
                    dst_ref=place,
                    send_sem=scratch[0].at[i],
                    recv_sem=scratch[1].at[i],
                    device_id=device,
                    device_id_type=MESH,
                )

            def act(remote=remote, target=target, landing=landing):
                if ending:
                    remote(landing).wait_recv()
                    remote(target).wait_send()
                else:
                    remote(target).start()

            if when is None:
                act()
            else:
                pl.when(when)(act)


def plane_peers():
    peers = []
    for axis in (PY, PX):
        for offset in range(1, lax.axis_size(axis)):
            peers.append(lambda axis=axis, offset=offset: {axis: turned(axis, offset)})
    return peers


SWAP_PEERS = [
    lambda: {CORE: other(CORE)},
    lambda: {ZH: other(ZH)},
    lambda: {CORE: other(CORE), ZH: other(ZH)},
]


class SwapIn(Errand):
    def __init__(self, shard):
        super().__init__()
        self.take(shard)
        self.give((lax.axis_size(PY), lax.axis_size(PX), 2) + shard.shape)
        self.peers = SWAP_PEERS
        self.reserve(2, 1)

    def plan(self, ins, outs):
        core, half = lax.axis_index(CORE), lax.axis_index(ZH)
        home = outs[0].at[lax.axis_index(PY), lax.axis_index(PX)]
        crossed = jnp.where(core == 0, 1 - half, half)
        return [
            [
                (ins[0], home.at[core], home.at[1 - core], {CORE: 1 - core, ZH: crossed}, None),
                (ins[0], home.at[1], home.at[1], {ZH: 1 - half}, core == 1),
            ]
        ]

    def local(self, ins, outs):
        home = outs[0].at[lax.axis_index(PY), lax.axis_index(PX)]
        return [(ins[0], home.at[0], lax.axis_index(CORE) == 0)]


class Spread(Errand):
    def __init__(self, rows, stages):
        super().__init__()
        self.stages = stages
        self.give(rows.shape, rows.dtype, pltpu.HBM, self.take(rows))
        self.peers = plane_peers()
        ny, nx = rows.shape[:2]
        straight, relayed = nx + ny - 2, 2 * (nx - 1) * (ny - 1)
        self.reserve(sum(relayed if stage == RELAY else straight for stage in stages))

    def plan(self, ins, outs):
        rows = outs[0]
        ny, nx = rows.shape[:2]
        first, then = [], []
        own = {PY: lax.axis_index(PY), PX: lax.axis_index(PX)}
        sides = [(PX, nx), (PY, ny)]

        def along(moves, axis, offset, at, core):
            land = dict(at)
            land[axis] = turned(axis, -offset)
            here = rows.at[at[PY], at[PX], core]
            there = rows.at[land[PY], land[PX], core]
            moves.append((here, here, there, {axis: turned(axis, offset)}, None))

        for stage in self.stages:
            if stage == RELAY:
                for e in range(1, nx):
                    for offset in range(1, ny):
                        along(then, PY, offset, {**own, PX: turned(PX, e)}, 0)
                for e in range(1, ny):
                    for offset in range(1, nx):
                        along(then, PX, offset, {**own, PY: turned(PY, e)}, 1)
            else:
                for core, (axis, size) in enumerate(sides if stage == STRAIGHT else sides[::-1]):
                    for offset in range(1, size):
                        along(first, axis, offset, own, core)
        if STRAIGHT in self.stages:
            return [first, then] if then else [first]
        return [first + then]


class FoldFar(Errand):
    def __init__(self, grad):
        super().__init__()
        self.take(grad)
        ny, nx, _, rows, columns = grad.shape
        self.give((ny - 1, nx - 1, rows, columns))
        self.give((nx - 1, ny - 1, rows, columns))
        self.peers = plane_peers()
        self.reserve(2 * (nx - 1) * (ny - 1))

    def plan(self, ins, outs):
        grad = ins[0]
        ny, nx = grad.shape[:2]
        moves = []
        for e in range(1, nx):
            for d in range(1, ny):
                slot = outs[0].at[d - 1, e - 1]
                to = turned(PY, d)
                moves.append((grad.at[to, turned(PX, e), 0], slot, slot, {PY: to}, None))
        for e in range(1, ny):
            for d in range(1, nx):
                slot = outs[1].at[d - 1, e - 1]
                to = turned(PX, d)
                moves.append((grad.at[turned(PY, e), to, 1], slot, slot, {PX: to}, None))
        return [moves]


class FoldNear(Errand):
    def __init__(self, grad):
        super().__init__()
        self.take(grad)
        ny, nx, _, rows, columns = grad.shape
        self.give((ny - 1, rows, columns))
        self.give((nx - 1, rows, columns))
        self.peers = plane_peers()
        self.reserve(nx + ny - 2)

    def plan(self, ins, outs):
        grad = ins[0]
        ny, nx = grad.shape[:2]
        y, x = lax.axis_index(PY), lax.axis_index(PX)
        moves = []
        for d in range(1, ny):
            to, slot = turned(PY, d), outs[0].at[d - 1]
            moves.append((grad.at[to, x, 0], slot, slot, {PY: to}, None))
        for d in range(1, nx):
            to, slot = turned(PX, d), outs[1].at[d - 1]
            moves.append((grad.at[y, to, 1], slot, slot, {PX: to}, None))
        return [moves]


class FoldRelay(Errand):
    def __init__(self, sums):
        super().__init__()
        for each in sums:
            self.take(each)
            self.give(each.shape)
        self.peers = plane_peers()
        self.reserve(sums[0].shape[0] + sums[1].shape[0])

    def plan(self, ins, outs):
        moves = []
        for i, axis in enumerate((PX, PY)):
            for e in range(1, lax.axis_size(axis)):
                slot = outs[i].at[e - 1]
                moves.append((ins[i].at[e - 1], slot, slot, {axis: turned(axis, e)}, None))
        return [moves]


class SwapOut(Errand):
    def __init__(self, pair):
        super().__init__()
        self.take(pair)
        self.give(pair.shape)
        self.peers = SWAP_PEERS
        self.reserve(2, 1)

    def plan(self, ins, outs):
        core, half = lax.axis_index(CORE), lax.axis_index(ZH)
        crossed = jnp.where(core == 0, half, 1 - half)
        pair, met = ins[0], outs[0]
        return [
            [
                (pair.at[1 - core], met.at[0], met.at[0], {CORE: 1 - core, ZH: crossed}, None),
                (pair.at[1], met.at[1], met.at[1], {ZH: 1 - half}, core == 1),
            ]
        ]

    def local(self, ins, outs):
        return [(ins[0].at[0], outs[0].at[1], lax.axis_index(CORE) == 0)]


def take_counts(refs, sizes):
    taken, rest = [], list(refs)
    for size in sizes:
        taken.append(rest[:size])
        rest = rest[size:]
    return taken, rest


def kernel(parts, *refs):
    ins, refs = take_counts(refs, [len(part.arrays) for part in parts])
    outs, refs = take_counts(refs, [len(part.shapes) for part in parts])
    scratch, _ = take_counts(refs, [len(part.scratch) for part in parts])
    barrier = pltpu.get_barrier_semaphore()
    greeted = sum(part.greet(barrier) for part in parts)
    pl.semaphore_wait(barrier, greeted)

    def errands(step):
        for i in range(1, len(parts)):
            parts[i].go(step, ins[i], outs[i], scratch[i])

    errands(0)
    parts[0].begin(ins[0], outs[0], scratch[0], partial(errands, 1))
    errands(2)


def travel(collective_id, *parts):
    aliases, first_in, first_out = {}, 0, 0
    for part in parts:
        for source, result in part.aliases.items():
            aliases[first_in + source] = first_out + result
        first_in += len(part.arrays)
        first_out += len(part.shapes)
    results = pl.pallas_call(
        partial(kernel, parts),
        out_shape=[shape for part in parts for shape in part.shapes],
        in_specs=[pl.BlockSpec(memory_space=space) for part in parts for space in part.in_spaces],
        out_specs=[pl.BlockSpec(memory_space=space) for part in parts for space in part.out_spaces],
        scratch_shapes=[each for part in parts for each in part.scratch],
        input_output_aliases=aliases,
        compiler_params=pltpu.CompilerParams(
            collective_id=collective_id, has_side_effects=True, vmem_limit_bytes=24 * 2**20
        ),
        cost_estimate=pl.CostEstimate(flops=2 * 10**10, bytes_accessed=1024, transcendentals=0),
    )(*[array for part in parts for array in part.arrays])
    split, _ = take_counts(results, [len(part.shapes) for part in parts])
    return split


class Route:
    def __init__(self, shards, errands):
        self.shards = shards
        self.errands = iter(errands)
        self.rows, self.grads, self.got = {}, {}, {FAR: {}, NEAR: {}, PASS: {}, LEAVE: {}}
        self.count = 0

    def step(self, main):
        errands, parts = next(self.errands), [main]
        for name, what in errands:
            if what == (ENTER,):
                parts.append(SwapIn(self.shards[name]))
            elif what == (FAR,):
                parts.append(FoldFar(self.grads[name]))
            elif what == (NEAR,):
                parts.append(FoldNear(self.grads[name]))
            elif what == (PASS,):
                parts.append(FoldRelay(self.far_sums(name)))
            elif what == (LEAVE,):
                parts.append(SwapOut(self.pair(name)))
            else:
                parts.append(Spread(self.rows[name], what))
        results = travel(self.count, *parts)
        self.count += 1
        for (name, what), got in zip(errands, results[1:]):
            if what[0] in self.got:
                self.got[what[0]][name] = got
            else:
                self.rows[name] = got[0]
        return results[0]

    def weight(self, kind, block):
        rows = self.rows[kind, block]
        return rows.reshape(-1, rows.shape[-1])

    def give_grad(self, kind, block, grad):
        name = (kind, block)
        self.grads[name] = grad.astype(jnp.bfloat16).reshape(self.rows[name].shape)

    def own_rows(self, name, py, px, core):
        grad = self.grads[name]
        at = lax.dynamic_slice(grad, (py, px, core, 0, 0), (1, 1, 1) + grad.shape[3:])
        return at[0, 0, 0].astype(jnp.float32)

    def far_sums(self, name):
        y, x = lax.axis_index(PY), lax.axis_index(PX)
        along_y, along_x = self.got[FAR][name]
        first = [
            self.own_rows(name, y, turned(PX, e), 0)
            + jnp.sum(along_y[:, e - 1].astype(jnp.float32), 0)
            for e in range(1, lax.axis_size(PX))
        ]
        last = [
            self.own_rows(name, turned(PY, e), x, 1)
            + jnp.sum(along_x[:, e - 1].astype(jnp.float32), 0)
            for e in range(1, lax.axis_size(PY))
        ]
        return jnp.stack(first).astype(jnp.bfloat16), jnp.stack(last).astype(jnp.bfloat16)

    def pair(self, name):
        y, x = lax.axis_index(PY), lax.axis_index(PX)
        halves = []
        for core in range(2):
            near = jnp.sum(self.got[NEAR][name][core].astype(jnp.float32), 0)
            relayed = jnp.sum(self.got[PASS][name][core].astype(jnp.float32), 0)
            halves.append(self.own_rows(name, y, x, core) + near + relayed)
        return jnp.stack(halves).astype(jnp.bfloat16)

    def met(self, kind, block):
        return self.got[LEAVE][kind, block][0]


def scores_of(query, key, key_valid):
    scale = 1.0 / math.sqrt(HEAD_DIM)
    scores = jnp.einsum("bqhe,bkhe->bhqk", query, key, preferred_element_type=jnp.float32) * scale
    if key_valid is None:
        return scores
    return jnp.where(key_valid[:, None, None, :] > 0, scores, -1e30)


def attend_forward(query, key, value, key_valid):
    scores = scores_of(query, key, key_valid)
    peak = jnp.max(scores, -1, keepdims=True)
    expo = jnp.exp(scores - peak)
    total = jnp.sum(expo, -1, keepdims=True)
    probs = (expo / total).astype(jnp.bfloat16)
    context = jnp.einsum(
        "bhqk,bkhe->bqhe", probs, value, preferred_element_type=jnp.float32
    ).astype(jnp.bfloat16)
    return (context, peak + jnp.log(total))


def attend_backward(query, key, value, log_total, grad_context, key_valid):
    scale = 1.0 / math.sqrt(HEAD_DIM)
    probs = jnp.exp(scores_of(query, key, key_valid) - log_total)
    grad_value = jnp.einsum(
        "bhqk,bqhe->bkhe",
        probs.astype(jnp.bfloat16),
        grad_context,
        preferred_element_type=jnp.float32,
    ).astype(jnp.bfloat16)
    grad_probs = jnp.einsum(
        "bqhe,bkhe->bhqk", grad_context, value, preferred_element_type=jnp.float32
    )
    grad_scores = (probs * (grad_probs - jnp.sum(grad_probs * probs, -1, keepdims=True))).astype(
        jnp.bfloat16
    )
    grad_query = (
        jnp.einsum("bhqk,bkhe->bqhe", grad_scores, key, preferred_element_type=jnp.float32) * scale
    ).astype(jnp.bfloat16)
    grad_key = (
        jnp.einsum("bhqk,bqhe->bkhe", grad_scores, query, preferred_element_type=jnp.float32)
        * scale
    ).astype(jnp.bfloat16)
    return (grad_query, grad_key, grad_value)


def split_heads(triple):
    batch, length, three = triple.shape
    local = three // 3
    return [
        triple[:, :, i * local : (i + 1) * local].reshape(
            batch, length, local // HEAD_DIM, HEAD_DIM
        )
        for i in range(3)
    ]


def low_dot(spec, left, right):
    return jnp.einsum(spec, left, right, preferred_element_type=jnp.float32)


def attend(normed, key_valid, block, route):
    triple = low_dot("bld,dc->blc", normed, route.weight(IN, block)).astype(jnp.bfloat16)
    context, log_total = attend_forward(*split_heads(triple), key_valid)
    flat_context = context.reshape(triple.shape[0], triple.shape[1], triple.shape[2] // 3)
    terms = low_dot("ble,de->bld", flat_context, route.weight(OUT, block)).astype(jnp.bfloat16)
    return terms, (triple, flat_context, log_total)


def feed(normed, block, route):
    inner = low_dot("bld,df->blf", normed, route.weight(EXPAND, block))
    active = jax.nn.gelu(inner, approximate=True).astype(jnp.bfloat16)
    terms = low_dot("blf,df->bld", active, route.weight(CONTRACT, block)).astype(jnp.bfloat16)
    return terms, (inner, active)


def feed_back(grad_branch, normed, saved, block, route):
    inner, active = saved
    grad_active = low_dot("bld,df->blf", grad_branch, route.weight(CONTRACT, block))
    gelu_back = jax.vjp(partial(jax.nn.gelu, approximate=True), inner)[1]
    grad_inner = gelu_back(grad_active)[0].astype(jnp.bfloat16)
    terms = low_dot("blf,df->bld", grad_inner, route.weight(EXPAND, block)).astype(jnp.bfloat16)
    route.give_grad(CONTRACT, block, low_dot("bld,blf->df", grad_branch, active))
    route.give_grad(EXPAND, block, low_dot("bld,blf->df", normed, grad_inner))
    return terms


def attend_back(grad_attn, normed, saved, key_valid, block, route):
    triple, flat_context, log_total = saved
    grad_flat = low_dot("bld,de->ble", grad_attn, route.weight(OUT, block)).astype(jnp.bfloat16)
    query, key, value = split_heads(triple)
    grad_context = grad_flat.reshape(query.shape)
    grad_parts = attend_backward(query, key, value, log_total, grad_context, key_valid)
    grad_triple = jnp.concatenate([g.reshape(flat_context.shape) for g in grad_parts], 2)
    terms = low_dot("blc,dc->bld", grad_triple, route.weight(IN, block)).astype(jnp.bfloat16)
    return terms, (normed, grad_triple, grad_attn, flat_context)


def errands_in_turn():
    def attend(block, *what):
        return [((IN, block), what), ((OUT, block), what)]

    def expand(block, *what):
        return [((EXPAND, block), what)]

    def contract(block, *what):
        return [((CONTRACT, block), what)]

    def feed(block, *what):
        return expand(block, *what) + contract(block, *what)

    return [
        attend(0, ENTER),
        attend(0, STRAIGHT) + expand(0, ENTER),
        attend(0, CROSS, RELAY) + contract(0, ENTER),
        expand(0, STRAIGHT, CROSS, RELAY) + attend(1, ENTER),
        contract(0, STRAIGHT, CROSS, RELAY) + expand(1, ENTER),
        attend(1, STRAIGHT, CROSS, RELAY) + expand(1, STRAIGHT) + contract(1, ENTER),
        contract(1, STRAIGHT, CROSS, RELAY) + expand(1, CROSS, RELAY),
        [],
        feed(1, FAR) + feed(1, NEAR),
        feed(1, PASS),
        feed(0, FAR) + attend(1, FAR) + attend(1, NEAR) + expand(1, LEAVE),
        feed(0, NEAR) + feed(0, PASS) + attend(1, PASS) + contract(1, LEAVE),
        attend(0, FAR) + feed(0, LEAVE),
        attend(0, NEAR) + attend(0, PASS) + attend(1, LEAVE),
        attend(0, LEAVE),
        [],
    ]


def adam(weight, grad, moment, second, average, factor):
    grad = grad * factor
    moment = beta_first * moment + (1.0 - beta_first) * grad
    second = beta_second * second + (1.0 - beta_second) * grad * grad
    update = (
        moment
        / (1.0 - beta_first**STEP)
        / (jnp.sqrt(second / (1.0 - beta_second**STEP)) + adam_eps)
    )
    fresh = weight - learn_rate * (update + weight_decay * weight)
    average_decay = min(ema_decay, (1.0 + STEP) / (10.0 + STEP))
    average = average_decay * average + (1.0 - average_decay) * fresh
    return (fresh, moment, second, average)


def shards(
    patches,
    target_noise,
    kept_slots,
    kept_count,
    time_step,
    labels,
    teacher,
    *tables,
):
    params, moments, seconds, averages = tables[:7], tables[7:14], tables[14:21], tables[21:]
    attend_in, attend_out, expand, contract, modulation, patch_table, condition = params
    batch, length = (patches.shape[0], patches.shape[1])
    capacity = kept_slots.shape[1]
    rows, local = (attend_in.shape[1], attend_in.shape[3])
    wides, narrows = (group_size(WIDE), group_size(NARROW))
    wide_index, narrow_index = (flat_place(WIDE), flat_place(NARROW))
    images = batch * wides
    width = local * narrows
    assert batch == narrows

    shards_low = {}
    for i in range(2):
        shards_low[IN, i] = attend_in[i].reshape(rows, 3 * local).astype(jnp.bfloat16)
        shards_low[OUT, i] = attend_out[i].T.astype(jnp.bfloat16)
        shards_low[EXPAND, i] = expand[i].astype(jnp.bfloat16)
        shards_low[CONTRACT, i] = contract[i].T.astype(jnp.bfloat16)
    route = Route(shards_low, errands_in_turn())

    def own(array):
        return lax.dynamic_index_in_dim(array, narrow_index, 0, keepdims=False)

    condition_low = condition.astype(jnp.bfloat16)
    features = sinusoid(time_step, FREQ)
    onehot = (labels[:, None] == jnp.arange(CLASSES)[None, :]).astype(jnp.bfloat16)
    cond_part = jnp.dot(
        features, condition_low[:FREQ].astype(jnp.float32), precision=highest_float_accuracy
    ) + low_dot("bc,cd->bd", onehot, condition_low[FREQ:])
    pieces = jax.nn.silu(cond_part).reshape(batch, local // rows, rows)
    pieces = jnp.pad(jnp.transpose(pieces, (1, 0, 2)), ((0, 0), (0, 8 - batch), (0, 0)))
    (silu_wide,) = route.step(RowPieces(pieces))
    silu_rows = silu_wide[:, :batch].reshape(images, rows).astype(jnp.bfloat16)
    modulation_low = modulation.astype(jnp.bfloat16)
    mod_part = low_dot("ip,npkc->inkc", silu_rows, modulation_low)
    mod_part = mod_part.reshape(wides, batch, 12 * local)
    (mod_wide,) = route.step(Exchange([mod_part], [(WIDE, EACH)]))
    facts = jnp.stack([kept_count, time_step, labels], 1).astype(jnp.float32)
    facts = jnp.pad(facts, ((0, 4), (0, local - 3)))
    teacher_rows = teacher.reshape(batch * narrows, local)
    payload = jnp.concatenate([cond_part, facts[:batch], teacher_rows], 0)
    table_pad = jnp.pad(patch_table.astype(jnp.bfloat16), ((0, 15), (0, 0)))
    mod_near, everyone, tables_near = route.step(
        Exchange(
            [jnp.sum(mod_wide, 0).reshape(batch, 12, local), payload, table_pad],
            [(NARROW, EACH), (WIDE, SAME), (NARROW, SAME)],
        )
    )
    mods = jnp.transpose(mod_near, (1, 0, 2)).reshape(12, width)
    mod_enc, mod_dec = mods[:6], mods[6:]
    cond_cols = everyone[:, :batch].reshape(images, local)
    facts_all = everyone[:, batch : 2 * batch, :3]
    negatives = everyone[:, 2 * batch :].reshape(images, width)
    time_all = facts_all[:, :, 1].reshape(images).astype(jnp.int32)
    labels_all = facts_all[:, :, 2].reshape(images).astype(jnp.int32)
    patch_full = jnp.transpose(tables_near, (1, 0, 2)).reshape(48, width)

    count_own = own(kept_count).astype(jnp.float32)
    slot_valid = (jnp.arange(capacity) < own(kept_count)).astype(jnp.float32)[:, None]
    select = (own(kept_slots)[:, None] == jnp.arange(length)[None, :]).astype(
        jnp.float32
    ) * slot_valid
    open_place = 1.0 - jnp.sum(select, 0)[:, None]
    places = sinusoid(jnp.arange(length), width)
    group_counts = lax.dynamic_slice(
        facts_all[:, :, 0],
        (flat_place((PY, PX)) * 2, lax.axis_index(ZH) * 2),
        (2, 2),
    ).reshape(4)
    group_valid = (jnp.arange(capacity)[None, :] < group_counts[:, None]).astype(jnp.float32)
    kept_patches = low_dot("cl,lp->cp", select.astype(jnp.bfloat16), own(patches))
    embed = low_dot("cp,pd->cd", kept_patches.astype(jnp.bfloat16), patch_full[:PATCH_IN])
    embed = embed + jnp.dot(select, places, precision=highest_float_accuracy)
    mask_token = patch_full[2 * PATCH_IN : 2 * PATCH_IN + 1].astype(jnp.float32)
    base = open_place * mask_token + places
    head = patch_full[PATCH_IN : 2 * PATCH_IN]
    count_all = images * length * PATCH_IN

    (normed_a0,) = route.step(Enter(embed, mod_enc))
    terms, saved_a0 = attend(normed_a0, group_valid, 0, route)
    normed_m0, attn0, middle0 = route.step(Middle(terms, embed, mod_enc))
    terms, saved_m0 = feed(normed_m0, 0, route)
    normed_a1, branch0, encoded, decode_in = route.step(
        Decode(terms, middle0, mod_enc, mod_dec, select.T, base)
    )
    terms, saved_a1 = attend(normed_a1, None, 1, route)
    normed_m1, attn1, middle1 = route.step(Middle(terms, decode_in, mod_dec))
    terms, saved_m1 = feed(normed_m1, 1, route)
    grad_branch, grad_decoded, gate_m1, grad_head, square = route.step(
        Turn(terms, middle1, mod_dec, head, own(target_noise), count_all)
    )

    def pool_unit(values):
        pooled = jnp.sum(values * slot_valid, 0, keepdims=True) / count_own
        return pooled * lax.rsqrt(jnp.sum(pooled * pooled, -1, keepdims=True) + 1e-06)

    normalised_direction, pool_back = jax.vjp(pool_unit, encoded)
    frozen_target_direction = negatives * lax.rsqrt(
        jnp.sum(negatives * negatives, -1, keepdims=True) + 1e-06
    )
    cosine_match_scores = (
        jnp.sum(normalised_direction * frozen_target_direction, -1, keepdims=True)
        / contrast_sharpness_divisor
    )
    peak = jnp.max(cosine_match_scores)
    expo = jnp.exp(cosine_match_scores - peak)
    total = jnp.sum(expo)
    positive = ((wide_index * batch + narrow_index) == jnp.arange(images)).astype(jnp.float32)
    positive = positive[:, None]
    nce_local = peak + jnp.log(total) - jnp.sum(cosine_match_scores * positive)
    derivative_of_raw_scores = (expo / total - positive) * (nce_weight / images)
    unit_vector_gradient = (
        jnp.sum(derivative_of_raw_scores * frozen_target_direction, 0, keepdims=True)
        / contrast_sharpness_divisor
    )
    grad_pool = pool_back(unit_vector_gradient)[0]

    terms = feed_back(grad_branch, normed_m1, saved_m1, 1, route)
    grad_attn, grad_mid, sums_m1 = route.step(
        MiddleBack(terms, middle1, attn1, grad_decoded, mod_dec)
    )
    terms, pairs = attend_back(grad_attn, normed_a1, saved_a1, None, 1, route)
    back_to = (open_place, select, grad_pool, branch0, mod_enc)
    grad_branch, grad_encoded, sums_a1, grad_in, grad_out = route.step(
        Encode(terms, decode_in, grad_mid, mod_dec, *back_to, pairs)
    )
    route.give_grad(IN, 1, grad_in)
    route.give_grad(OUT, 1, grad_out)
    terms = feed_back(grad_branch, normed_m0, saved_m0, 0, route)
    grad_attn, grad_mid, sums_m0 = route.step(
        MiddleBack(terms, middle0, attn0, grad_encoded, mod_enc)
    )
    terms, pairs = attend_back(grad_attn, normed_a0, saved_a0, group_valid, 0, route)
    sums = (sums_m0, sums_a1, sums_m1, gate_m1, grad_head)
    rows_near, grad_in, grad_out = route.step(
        Leave(terms, embed, grad_mid, mod_enc, kept_patches, sums, pairs)
    )
    route.give_grad(IN, 0, grad_in)
    route.give_grad(OUT, 0, grad_out)

    mods_near = rows_near[:, :12].reshape(narrows, 12 * local)
    table_near = rows_near[:, 12:45]
    table_sum = jnp.pad(jnp.sum(table_near, 0), ((0, 15), (0, 0))).astype(jnp.bfloat16)
    mods_all, table_all = route.step(
        Exchange([mods_near, table_sum], [(WIDE, SAME), (WIDE, SAME)])
    )
    grad_patch_table = jnp.sum(table_all.astype(jnp.float32), 0)[:33]
    mods_all = mods_all.reshape(images, 2, 6, local)
    silu_broad = silu_rows.astype(jnp.float32)
    grad_modulation = jnp.einsum(
        "ip,inkc->npkc", silu_broad, mods_all, precision=highest_float_accuracy
    )
    grad_silu = jnp.einsum(
        "inkc,npkc->ip",
        mods_all,
        modulation_low.astype(jnp.float32),
        precision=highest_float_accuracy,
    )
    (silu_near,) = route.step(Exchange([grad_silu], [(NARROW, SAME)]))
    (silu_wide,) = route.step(Exchange([jnp.sum(silu_near, 0)], [(WIDE, SAME)]))
    grad_silu = jnp.transpose(silu_wide, (1, 0, 2)).reshape(images, width)
    grad_silu = lax.dynamic_slice_in_dim(grad_silu, narrow_index * local, local, 1)
    grad_cond = jax.vjp(jax.nn.silu, cond_cols)[1](grad_silu)[0]
    features_all = sinusoid(time_all, FREQ)
    onehot_all = (labels_all[:, None] == jnp.arange(CLASSES)[None, :]).astype(jnp.float32)
    grad_condition = jnp.dot(
        jnp.concatenate([features_all, onehot_all], 1).T, grad_cond, precision=highest_float_accuracy
    )


    def totals(kind, shape):
        both = [route.met(kind, i).astype(jnp.float32) for i in range(2)]
        return jnp.stack([shape(each[0] + each[1]) for each in both])

    def by_third(g):
        thirds = [g[:, i * local : (i + 1) * local] for i in range(3)]
        return jnp.transpose(jnp.stack(thirds), (1, 0, 2))

    grads = [
        totals(IN, by_third),
        totals(OUT, lambda g: g.T),
        totals(EXPAND, lambda g: g),
        totals(CONTRACT, lambda g: g.T),
        grad_modulation,
        grad_patch_table,
        grad_condition,
    ]
    square_small = jnp.sum(grad_patch_table * grad_patch_table) + jnp.sum(
        grad_condition * grad_condition
    )
    square_local = jnp.sum(grad_modulation * grad_modulation)
    square_local = square_local + (wide_index == 0).astype(jnp.float32) * square_small
    scalars = jnp.stack([square[0, 0], nce_local, square_local])
    scalars = jnp.pad(scalars[None, :], ((0, 7), (0, 125)))
    mets = [route.met(kind, i) for i in range(2) for kind in (IN, OUT, EXPAND, CONTRACT)]
    (scalars_all,) = route.step(Norm(scalars, mets))
    sums = jnp.sum(scalars_all[:, 0], 0)
    grad_norm = jnp.sqrt(sums[2])
    factor = clip_norm / jnp.maximum(grad_norm, clip_norm)
    fresh = [
        adam(params[i], grads[i], moments[i], seconds[i], averages[i], factor) for i in range(7)
    ]
    loss_parts = jnp.stack([sums[0] / count_all, sums[1] / images])
    return (loss_parts, grad_norm) + tuple(fresh[i][k] for k in range(4) for i in range(7))


def solution(mesh):
    wide, narrow = mesh.devices.shape
    planes = wide // 2
    across = max(n for n in range(1, math.isqrt(planes) + 1) if planes % n == 0)
    grid = Mesh(mesh.devices.reshape(across, planes // across, 2, narrow // 2, 2), ALL)
    image_specs = (
        P(WIDE, None, None),
        P(WIDE, None, None),
        P(WIDE, None),
        P(WIDE),
        P(WIDE),
        P(WIDE),
        P(WIDE, None),
    )
    table_specs = (
        P(None, WIDE, None, NARROW),
        P(None, NARROW, WIDE),
        P(None, WIDE, NARROW),
        P(None, NARROW, WIDE),
        P(None, WIDE, None, NARROW),
        P(None, NARROW),
        P(None, NARROW),
    )
    return jax.shard_map(
        shards,
        mesh=grid,
        in_specs=image_specs + table_specs * 4,
        out_specs=(P(), P()) + table_specs * 4,
        check_vma=False,
    )
```

```python
from functools import partial
import math

import jax
import jax.numpy as jnp
from jax import lax
from jax.experimental import pallas as pl
from jax.experimental.pallas import tpu as pltpu
from jax.sharding import Mesh
from jax.sharding import PartitionSpec as P

HEAD_DIM = 72
CLASSES = 1000
FREQ = 256
PATCH_IN = 16
STEP = 10

MESH = pl.DeviceIdType.MESH
PY, PX, CORE, ZH, ZL = "py", "px", "core", "zh", "zl"
WIDE = (PY, PX, CORE)
NARROW = (ZH, ZL)
ALL = WIDE + NARROW
EACH, SAME = range(2)
IN, OUT, EXPAND, CONTRACT = range(4)
TERM_SQUARE, TERM_HEAD, TERM_GATE, TERM_SHIFT, TERM_SCALE, TERM_MASK, TERM_PATCH = range(7)
ENTER, STRAIGHT, CROSS, RELAY, FAR, NEAR, PASS, LEAVE = range(8)

highest_float_accuracy = lax.Precision.HIGHEST
norm_eps = 1e-06
contrast_sharpness_divisor = 0.02
nce_weight = 0.5
learn_rate = 0.05
beta_first = 0.9
beta_second = 0.999
adam_eps = 1e-08
weight_decay = 0.05
clip_norm = 0.05
ema_decay = 0.9999


def layer_norm(values):
    center = values - jnp.mean(values, -1, keepdims=True)
    return center * lax.rsqrt(jnp.mean(center * center, -1, keepdims=True) + norm_eps)


def modulate(values, shift, scale):
    return layer_norm(values) * (1.0 + scale[None, :]) + shift[None, :]


def sinusoid(places, width):
    half = width // 2
    freqs = jnp.exp(-math.log(10000.0) * jnp.arange(half, dtype=jnp.float32) / half)
    angle = places.astype(jnp.float32)[:, None] * freqs[None, :]
    return jnp.concatenate([jnp.cos(angle), jnp.sin(angle)], -1)


def flat_place(axes):
    place = 0
    for axis in axes:
        place = place * lax.axis_size(axis) + lax.axis_index(axis)
    return place


def group_size(axes):
    size = 1
    for axis in axes:
        size = size * lax.axis_size(axis)
    return size


def device_at(axes, place):
    where = {}
    for axis in reversed(axes):
        where[axis] = lax.rem(place, lax.axis_size(axis))
        place = place // lax.axis_size(axis)
    return where


def turned(axis, offset):
    size = lax.axis_size(axis)
    return lax.rem(lax.axis_index(axis) + (offset % size), size)


def other(axis):
    return 1 - lax.axis_index(axis)


class Part:
    def __init__(self):
        self.arrays, self.in_spaces = [], []
        self.shapes, self.out_spaces = [], []
        self.aliases = {}
        self.scratch = []
        self.peers = []

    def take(self, array, space=pltpu.HBM):
        self.arrays.append(array)
        self.in_spaces.append(space)
        return len(self.arrays) - 1

    def give(self, shape, dtype=jnp.bfloat16, space=pltpu.HBM, source=None):
        held = pltpu.HBM if space == pltpu.HBM else jax.ShapeDtypeStruct
        self.shapes.append(held(shape, dtype))
        self.out_spaces.append(space)
        if source is not None:
            self.aliases[source] = len(self.shapes) - 1
        return len(self.shapes) - 1

    def greet(self, barrier):
        for peer in self.peers:
            pl.semaphore_signal(barrier, inc=1, device_id=peer(), device_id_type=MESH)
        return len(self.peers)

    def begin(self, ins, outs, scratch, halfway):
        pass

    def go(self, step, ins, outs, scratch):
        pass


class Exchange(Part):
    def __init__(self, arrays, specs):
        super().__init__()
        self.specs = specs
        for array, (axes, mode) in zip(arrays, specs):
            size = group_size(axes)
            piece = array.shape[1:] if mode == EACH else array.shape
            self.take(array, pltpu.VMEM)
            self.give((size,) + piece, array.dtype, pltpu.VMEM)
            self.scratch += [pltpu.SemaphoreType.DMA((size,)), pltpu.SemaphoreType.DMA((size,))]

    def greet(self, barrier):
        greeted = 0
        for axes, _ in self.specs:
            size, me = group_size(axes), flat_place(axes)
            greeted += size - 1

            def signal(offset, carry, axes=axes, size=size, me=me):
                target = lax.rem(me + offset, size)
                pl.semaphore_signal(
                    barrier, inc=1, device_id=device_at(axes, target), device_id_type=MESH
                )
                return carry

            lax.fori_loop(1, size, signal, 0)
        return greeted

    def begin(self, ins, outs, scratch, halfway):
        def copy_to(index, offset, arriving):
            axes, mode = self.specs[index]
            size, me = group_size(axes), flat_place(axes)
            target = lax.rem(me + offset, size)
            return pltpu.make_async_remote_copy(
                src_ref=ins[index].at[target] if mode == EACH else ins[index],
                dst_ref=outs[index].at[target if arriving else me],
                send_sem=scratch[2 * index].at[target],
                recv_sem=scratch[2 * index + 1].at[target if arriving else me],
                device_id=device_at(axes, target),
                device_id_type=MESH,
            )

        for index, (axes, mode) in enumerate(self.specs):

            def start(offset, carry, index=index):
                copy_to(index, offset, False).start()
                return carry

            lax.fori_loop(1, group_size(axes), start, 0)
        for index, (axes, mode) in enumerate(self.specs):
            me = flat_place(axes)
            outs[index][me] = ins[index][me] if mode == EACH else ins[index][...]
        for index, (axes, mode) in enumerate(self.specs):

            def end(offset, carry, index=index):
                copy_to(index, offset, True).wait_recv()
                copy_to(index, offset, False).wait_send()
                return carry

            lax.fori_loop(1, group_size(axes), end, 0)
        halfway()


class Norm(Exchange):
    def __init__(self, scalars, mets):
        super().__init__([scalars], [(ALL, SAME)])
        for met in mets:
            self.take(met, pltpu.VMEM)
        self.scratch.append(pltpu.VMEM(scalars.shape, jnp.float32))

    def begin(self, ins, outs, scratch, halfway):
        square = jnp.zeros((8, 128), jnp.float32)
        for met in ins[1:]:
            total = met[0].astype(jnp.float32) + met[1].astype(jnp.float32)
            columns = total.shape[1]
            squares = total * total
            if squares.shape[0] % 8:
                squares = jnp.pad(fold(squares), ((0, 7), (0, 0)))
            eights = jnp.sum(squares.reshape(-1, 8, columns), 0)
            for start in range(0, columns, 128):
                lanes = eights[:, start : start + 128]
                if lanes.shape[1] < 128:
                    lanes = jnp.pad(lanes, ((0, 0), (0, 128 - lanes.shape[1])))
                square = square + lanes
        lane = lax.broadcasted_iota(jnp.int32, (8, 128), 1)
        scratch[2][...] = ins[0][...] + jnp.where(lane == 2, jnp.sum(square), 0.0)
        super().begin([scratch[2]], outs, scratch[:2], halfway)


class RowPieces(Part):
    def __init__(self, pieces):
        super().__init__()
        self.each = pieces.shape[0]
        wides, narrows = group_size(WIDE), group_size(NARROW)
        self.take(pieces, pltpu.VMEM)
        self.give((wides,) + pieces.shape[1:], pieces.dtype, pltpu.VMEM)
        self.scratch = [
            pltpu.SemaphoreType.DMA((self.each * narrows,)),
            pltpu.SemaphoreType.DMA((wides,)),
        ]

    def sends(self):
        narrows, me = group_size(NARROW), flat_place(WIDE) * group_size(NARROW) + flat_place(NARROW)
        for j in range(self.each):
            for z in range(narrows):
                wide = flat_place(NARROW) * self.each + j
                to = {**device_at(WIDE, wide), **device_at(NARROW, jnp.int32(z))}
                yield j, z, to, wide * narrows + z != me

    def receives(self):
        narrows, me = group_size(NARROW), flat_place(WIDE) * group_size(NARROW) + flat_place(NARROW)
        z = flat_place(WIDE) // self.each
        for w in range(group_size(WIDE)):
            to = {**device_at(WIDE, jnp.int32(w)), **device_at(NARROW, z)}
            yield w, to, w * narrows + z != me

    def greet(self, barrier):
        for _, _, to, remote in self.sends():

            @pl.when(remote)
            def _(to=to):
                pl.semaphore_signal(barrier, inc=1, device_id=to, device_id_type=MESH)

        for _, to, remote in self.receives():

            @pl.when(remote)
            def _(to=to):
                pl.semaphore_signal(barrier, inc=1, device_id=to, device_id_type=MESH)

        counts = [r.astype(jnp.int32) for _, _, _, r in self.sends()]
        counts += [r.astype(jnp.int32) for _, _, r in self.receives()]
        return sum(counts)

    def begin(self, ins, outs, scratch, halfway):
        me = flat_place(WIDE)
        z = flat_place(WIDE) // self.each
        narrows = group_size(NARROW)

        def copy(j, slot, sem, to):
            return pltpu.make_async_remote_copy(
                src_ref=ins[0].at[j],
                dst_ref=outs[0].at[slot],
                send_sem=scratch[0].at[sem],
                recv_sem=scratch[1].at[slot],
                device_id=to,
                device_id_type=MESH,
            )

        for j, t, to, remote in self.sends():

            @pl.when(remote)
            def _(j=j, t=t, to=to):
                copy(j, me, j * narrows + t, to).start()

            @pl.when(jnp.logical_not(remote))
            def _(j=j):
                outs[0][me] = ins[0][j]

        for w, to, remote in self.receives():

            @pl.when(remote)
            def _(w=w, to=to):
                copy(0, w, 0, to).wait_recv()

        for j, t, to, remote in self.sends():

            @pl.when(remote)
            def _(j=j, t=t, to=to):
                copy(j, me, j * narrows + t, to).wait_send()

        halfway()


def chunk_of(length):
    return 64 if length % 64 == 0 else 32


def normal(values):
    center = values - jnp.mean(values, -1, keepdims=True)
    scale = lax.rsqrt(jnp.mean(center * center, -1, keepdims=True) + norm_eps)
    return center * scale, scale


def normal_back(grad, unit, scale):
    flat = jnp.mean(grad, -1, keepdims=True)
    tilt = jnp.mean(grad * unit, -1, keepdims=True)
    return scale * (grad - flat - unit * tilt)


def fold(values):
    return jnp.sum(values, 0, keepdims=True)


def full_dot(left, right):
    return jnp.dot(
        left, right, precision=highest_float_accuracy, preferred_element_type=jnp.float32
    )


SHIFT_A, SCALE_A, GATE_A, SHIFT_M, SCALE_M, GATE_M = range(6)


class Bridge(Part):
    whole = False
    sends_on = True

    def __init__(self, terms, more, width, length_in, length_out):
        super().__init__()
        self.length_in, self.length_out, self.width = length_in, length_out, width
        self.sums = terms is not None
        self.first = 0
        if self.sums:
            self.take(terms, pltpu.VMEM)
            self.first = 1
        self.fetched = []
        for array in more:
            large = array.size * array.dtype.itemsize >= 2**18
            if large:
                array = pltpu.with_memory_space_constraint(array, pltpu.HBM)
            self.fetched.append(large)
            self.take(array, pltpu.HBM if large else pltpu.VMEM)
        if self.sends_on:
            self.give((4, length_out, width), jnp.bfloat16, pltpu.VMEM)
        self.peers = [lambda: {CORE: other(CORE)}, lambda: {ZL: other(ZL)}]
        self.scratch = [
            pltpu.VMEM(array.shape, array.dtype)
            for array, large in zip(more, self.fetched)
            if large
        ]
        self.scratch.append(pltpu.SemaphoreType.DMA((len(more),)))
        if self.sums:
            self.scratch += [pltpu.VMEM((length_in, width), jnp.bfloat16)] * 4
            self.scratch += self.sems(length_in)
        if self.sends_on:
            self.scratch += self.sems(length_out)

    def result(self, shape, dtype=jnp.float32):
        self.give(shape, dtype, pltpu.VMEM)

    def sems(self, length):
        steps = length // chunk_of(length)
        return [pltpu.SemaphoreType.DMA((3, steps)), pltpu.SemaphoreType.DMA((3, steps))]

    def ranks(self):
        core, low = lax.axis_index(CORE), lax.axis_index(ZL)
        return core * 2 + low, (1 - core) * 2 + low, core * 2 + 1 - low, (1 - core) * 2 + 1 - low

    def copy(self, source, target, sems, kind, step):
        return pltpu.make_async_remote_copy(
            src_ref=source,
            dst_ref=target,
            send_sem=sems[0].at[kind, step],
            recv_sem=sems[1].at[kind, step],
            device_id={ZL: other(ZL)} if kind == 0 else {CORE: other(CORE)},
            device_id_type=MESH,
        )

    def rows(self, length):
        chunk = chunk_of(length)
        return [pl.ds(s * chunk, chunk) for s in range(length // chunk)]

    def begin(self, ins, outs, scratch, halfway):
        me, mate, away, away_mate = self.ranks()
        given = list(ins[self.first :])
        made = outs[1:] if self.sends_on else outs
        fetches = []
        held, scratch = scratch[: sum(self.fetched)], scratch[sum(self.fetched) :]
        for i, large in enumerate(self.fetched):
            if large:
                place = held[len(fetches)]
                fetches.append(pltpu.make_async_copy(given[i], place, scratch[0].at[i]))
                fetches[-1].start()
                given[i] = place
        scratch = scratch[1:]
        state = self.start(given, made)
        sends = []
        rows_in, rows_out = self.rows(self.length_in), self.rows(self.length_out)
        if self.sums:
            terms = ins[0]
            near, home, stage, far = scratch[:4]
            sems = scratch[4:6]
            to_near = [
                self.copy(terms.at[away_mate, r], near.at[r], sems, 1, s)
                for s, r in enumerate(rows_in)
            ]
            to_home = [
                self.copy(terms.at[mate, r], home.at[r], sems, 2, s) for s, r in enumerate(rows_in)
            ]
            to_far = [self.copy(stage.at[r], far.at[r], sems, 0, s) for s, r in enumerate(rows_in)]
            for each in to_near:
                each.start()
            for each in to_home:
                each.start()
            for s, r in enumerate(rows_in):
                to_near[s].wait_recv()
                both = terms[away, r].astype(jnp.float32) + near[r].astype(jnp.float32)
                stage[r] = both.astype(jnp.bfloat16)
                to_far[s].start()
            sends += to_near + to_home + to_far

            def total(s, r):
                to_home[s].wait_recv()
                own = terms[me, r].astype(jnp.float32) + home[r].astype(jnp.float32)
                to_far[s].wait_recv()
                return own + far[r].astype(jnp.float32)

        else:

            def total(s, r):
                return None

        if self.sends_on:
            every = outs[0]
            sems_out = scratch[-2:]

            def move(kind, here, there, s, r):
                return self.copy(every.at[here, r], every.at[there, r], sems_out, kind, s)

            def pass_on(s, r, fresh):
                every[me, r] = fresh
                for kind in (0, 1):
                    each = move(kind, me, me, s, r)
                    each.start()
                    sends.append(each)

        for each in fetches:
            each.wait()
        if self.whole:
            for s, r in enumerate(rows_in):
                self.collect(r, total(s, r), given, made, state)
            self.turn(given, made, state)
            for s, r in enumerate(rows_out):
                pass_on(s, r, self.work(r, None, given, made, state))
        else:
            for s, r in enumerate(rows_in):
                fresh = self.work(r, total(s, r), given, made, state)
                if self.sends_on:
                    pass_on(s, r, fresh)
        self.end(given, made, state)
        self.aside(given, made)
        if self.sums:
            halfway()
        if self.sends_on:
            for s, r in enumerate(rows_out):
                move(0, me, away, s, r).wait_recv()
                each = move(2, away, away, s, r)
                each.start()
                sends.append(each)
            for s, r in enumerate(rows_out):
                move(1, me, mate, s, r).wait_recv()
                move(2, away, away_mate, s, r).wait_recv()
        for each in sends:
            each.wait_send()
        if not self.sums:
            halfway()

    def start(self, given, made):
        return {}

    def add(self, state, name, value):
        state[name] = value if name not in state else state[name] + value

    def end(self, given, made, state):
        pass

    def aside(self, given, made):
        pass


def outer(left, right, result):
    step = 384 if left.shape[2] % 384 == 0 else 128

    def tile(i, carry):
        columns = pl.ds(pl.multiple_of(i * step, step), step)
        value = lax.dot_general(
            left[:, :, columns].reshape(-1, step),
            right[...].reshape(-1, right.shape[2]),
            (((0,), (0,)), ((), ())),
            preferred_element_type=jnp.float32,
        )
        result[columns] = value.astype(jnp.bfloat16)
        return carry

    lax.fori_loop(0, left.shape[2] // step, tile, 0)


class Enter(Bridge):
    def __init__(self, values, mod):
        length, width = values.shape
        super().__init__(None, [values, mod], width, length, length)

    def work(self, r, total, given, made, state):
        values, mod = given
        unit, _ = normal(values[r])
        return (unit * (1.0 + mod[SCALE_A : SCALE_A + 1]) + mod[SHIFT_A : SHIFT_A + 1]).astype(
            jnp.bfloat16
        )


class Middle(Bridge):
    def __init__(self, terms, values, mod):
        length, width = values.shape
        super().__init__(terms, [values, mod], width, length, length)
        self.result((length, width))
        self.result((length, width))

    def work(self, r, total, given, made, state):
        values, mod = given
        attn, middle = made
        attn[r] = total
        fresh = values[r] + mod[GATE_A : GATE_A + 1] * total
        middle[r] = fresh
        unit, _ = normal(fresh)
        return (unit * (1.0 + mod[SCALE_M : SCALE_M + 1]) + mod[SHIFT_M : SHIFT_M + 1]).astype(
            jnp.bfloat16
        )


class Decode(Bridge):
    whole = True

    def __init__(self, terms, middle, mod, mod_next, place, base, contrast):
        (length, width), (length_next, _) = middle.shape, base.shape
        more = [middle, mod, mod_next, place, base, *contrast]
        super().__init__(terms, more, width, length, length_next)
        self.result((length, width))
        self.result((length, width))
        self.result((length_next, width))
        self.result((1, width))
        self.result((1, 1))

    def collect(self, r, total, given, made, state):
        middle, mod = given[:2]
        branch, encoded = made[:2]
        branch[r] = total
        encoded[r] = middle[r] + mod[GATE_M : GATE_M + 1] * total

    def turn(self, given, made, state):
        place, base = given[3:5]
        made[2][...] = full_dot(place[...], made[1][...]) + base[...]

    def work(self, r, total, given, made, state):
        mod = given[2]
        unit, _ = normal(made[2][r])
        return (unit * (1.0 + mod[SCALE_A : SCALE_A + 1]) + mod[SHIFT_A : SHIFT_A + 1]).astype(
            jnp.bfloat16
        )


    def aside(self, given, made):
        valid, count, teachers, positive = given[5:]
        pooled = fold(made[1][...] * valid[...]) / count[...]
        scale = lax.rsqrt(jnp.sum(pooled * pooled, -1, keepdims=True) + 1e-06)
        others = teachers[...]
        others = others * lax.rsqrt(jnp.sum(others * others, -1, keepdims=True) + 1e-06)
        logits = jnp.sum(pooled * scale * others, -1, keepdims=True) / contrast_sharpness_divisor
        peak = jnp.max(logits, 0, keepdims=True)
        expo = jnp.exp(logits - peak)
        total = fold(expo)
        made[4][...] = peak + jnp.log(total) - fold(logits * positive[...])
        weight = (expo / total - positive[...]) * (nce_weight / others.shape[0])
        grad = fold(weight * others) / contrast_sharpness_divisor
        along = jnp.sum(pooled * grad, -1, keepdims=True)
        made[3][...] = scale * (grad - pooled * (scale * scale * along)) / count[...]


class Turn(Bridge):
    def __init__(self, terms, middle, mod, head, noise, count_all):
        length, width = middle.shape
        super().__init__(terms, [middle, mod, head, noise], width, length, length)
        self.scale = 2.0 / count_all
        self.result((length, width))
        self.result((1, width))
        self.result(head.shape)
        self.result((1, 1))

    def work(self, r, total, given, made, state):
        middle, mod, head, noise = given
        gate = mod[GATE_M : GATE_M + 1]
        unit, scale = normal(middle[r] + gate * total)
        low = unit.astype(jnp.bfloat16)
        rows_by_rows = (((1,), (1,)), ((), ()))
        predict = lax.dot_general(low, head[...], rows_by_rows, preferred_element_type=jnp.float32)
        error = predict - noise[r]
        self.add(state, TERM_SQUARE, jnp.sum(error * error, keepdims=True))
        grad_predict = (error * self.scale).astype(jnp.bfloat16)
        columns_by_columns = (((0,), (0,)), ((), ()))
        self.add(
            state,
            TERM_HEAD,
            lax.dot_general(
                grad_predict, low, columns_by_columns, preferred_element_type=jnp.float32
            ),
        )
        grad_final = jnp.dot(grad_predict, head[...], preferred_element_type=jnp.float32)
        grad = normal_back(grad_final, unit, scale)
        made[0][r] = grad
        self.add(state, TERM_GATE, fold(grad * total))
        return (gate * grad).astype(jnp.bfloat16)

    def end(self, given, made, state):
        made[1][...] = state[TERM_GATE]
        made[2][...] = state[TERM_HEAD]
        made[3][...] = state[TERM_SQUARE]


class MiddleBack(Bridge):
    def __init__(self, terms, middle, attn, grad, mod):
        length, width = middle.shape
        super().__init__(terms, [middle, attn, grad, mod], width, length, length)
        self.result((length, width))
        self.result((3, width))

    def work(self, r, total, given, made, state):
        middle, attn, grad, mod = given
        unit, scale = normal(middle[r])
        self.add(state, TERM_SHIFT, fold(total))
        self.add(state, TERM_SCALE, fold(total * unit))
        back = normal_back(total * (1.0 + mod[SCALE_M : SCALE_M + 1]), unit, scale)
        fresh = grad[r] + back
        made[0][r] = fresh
        self.add(state, TERM_GATE, fold(fresh * attn[r]))
        return (mod[GATE_A : GATE_A + 1] * fresh).astype(jnp.bfloat16)

    def end(self, given, made, state):
        made[1][0:1] = state[TERM_SHIFT]
        made[1][1:2] = state[TERM_SCALE]
        made[1][2:3] = state[TERM_GATE]


class Encode(Bridge):
    whole = True

    def __init__(self, terms, values, grad, mod, more, pairs):
        branch = more[4]
        (length, width), (length_next, _) = values.shape, branch.shape
        super().__init__(
            terms,
            [values, grad, mod, *more, *pairs],
            width,
            length,
            length_next,
        )
        self.result((length_next, width))
        self.result((4, width))
        self.result((width, pairs[1].shape[2]), jnp.bfloat16)
        self.result((width, pairs[3].shape[2]), jnp.bfloat16)
        self.scratch = [pltpu.VMEM((length, width), jnp.float32)] + self.scratch

    def begin(self, ins, outs, scratch, halfway):
        self.held = scratch[0]
        super().begin(ins, outs, scratch[1:], halfway)

    def collect(self, r, total, given, made, state):
        values, grad, mod, open_place = given[:4]
        unit, scale = normal(values[r])
        self.add(state, TERM_SHIFT, fold(total))
        self.add(state, TERM_SCALE, fold(total * unit))
        back = normal_back(total * (1.0 + mod[SCALE_A : SCALE_A + 1]), unit, scale)
        fresh = grad[r] + back
        self.held[r] = fresh
        self.add(state, TERM_MASK, fold(open_place[r] * fresh))

    def turn(self, given, made, state):
        select, (valid, pool) = given[4], given[5:7]
        made[0][...] = full_dot(select[...], self.held[...]) + valid[...] * pool[...]

    def work(self, r, total, given, made, state):
        branch, mod_next = given[7:9]
        fresh = made[0][r]
        self.add(state, TERM_GATE, fold(fresh * branch[r]))
        return (mod_next[GATE_M : GATE_M + 1] * fresh).astype(jnp.bfloat16)

    def end(self, given, made, state):
        made[1][0:1] = state[TERM_SHIFT]
        made[1][1:2] = state[TERM_SCALE]
        made[1][2:3] = state[TERM_GATE]
        made[1][3:4] = state[TERM_MASK]

    def aside(self, given, made):
        outer(given[9], given[10], made[2])
        outer(given[11], given[12], made[3])


class Leave(Bridge):
    sends_on = False

    def __init__(self, terms, values, grad, mod, kept, sums, pairs):
        length, width = values.shape
        super().__init__(terms, [values, grad, mod, kept, *sums, *pairs], width, length, length)
        narrows = group_size(NARROW)
        piece = jax.ShapeDtypeStruct((narrows, 48, width // narrows), jnp.float32)
        self.tell = Exchange([piece], [(NARROW, EACH)])
        self.result(piece.shape)
        self.result((width, pairs[1].shape[2]), jnp.bfloat16)
        self.result((width, pairs[3].shape[2]), jnp.bfloat16)
        self.scratch = (
            [pltpu.VMEM((48, width), jnp.float32), pltpu.VMEM(piece.shape, jnp.float32)]
            + self.tell.scratch
            + self.scratch
        )

    def greet(self, barrier):
        return super().greet(barrier) + self.tell.greet(barrier)

    def begin(self, ins, outs, scratch, halfway):
        self.table, self.piece = scratch[:2]
        self.tell_sems = scratch[2:4]
        super().begin(ins, outs, scratch[4:], halfway)

    def work(self, r, total, given, made, state):
        values, grad, mod, kept = given[:4]
        unit, scale = normal(values[r])
        self.add(state, TERM_SHIFT, fold(total))
        self.add(state, TERM_SCALE, fold(total * unit))
        back = normal_back(total * (1.0 + mod[SCALE_A : SCALE_A + 1]), unit, scale)
        columns_by_columns = (((0,), (0,)), ((), ()))
        self.add(
            state,
            TERM_PATCH,
            lax.dot_general(
                kept[r],
                grad[r] + back,
                columns_by_columns,
                precision=highest_float_accuracy,
                preferred_element_type=jnp.float32,
            ),
        )

    def end(self, given, made, state):
        sums_m0, sums_a1, sums_m1, gate_m1, head = given[4:9]
        table = self.table
        table[...] = jnp.zeros(table.shape, jnp.float32)
        table[0:1] = state[TERM_SHIFT]
        table[1:2] = state[TERM_SCALE]
        table[2:3] = sums_m0[2:3]
        table[3:5] = sums_m0[0:2]
        table[5:6] = sums_a1[2:3]
        table[6:8] = sums_a1[0:2]
        table[8:9] = sums_m1[2:3]
        table[9:11] = sums_m1[0:2]
        table[11:12] = gate_m1[...]
        table[12:28] = state[TERM_PATCH]
        table[28:44] = head[...]
        table[44:45] = sums_a1[3:4]
        local = self.piece.shape[2]
        for z in range(self.piece.shape[0]):
            self.piece[z] = table[:, z * local : (z + 1) * local]
        self.tell.begin([self.piece], made[:1], self.tell_sems, lambda: None)

    def aside(self, given, made):
        outer(given[9], given[10], made[1])
        outer(given[11], given[12], made[2])


class Errand(Part):
    def plan(self, ins, outs):
        raise NotImplementedError

    def local(self, ins, outs):
        return []

    def reserve(self, count, local=0):
        self.scratch = [pltpu.SemaphoreType.DMA((count,)), pltpu.SemaphoreType.DMA((count,))]
        if local:
            self.scratch.append(pltpu.SemaphoreType.DMA((local,)))

    def go(self, step, ins, outs, scratch):
        first = 0
        plans = self.plan(ins, outs)
        if step == 1 and len(plans) == 1:
            return
        for turn, moves in enumerate(plans):
            last = turn == len(plans) - 1
            if step == (2 if last else turn + 1):
                self.run(moves, first, scratch, True)
            if step == turn:
                self.run(moves, first, scratch, False)
            first += len(moves)
        if step != 1:
            for i, (source, target, when) in enumerate(self.local(ins, outs)):

                def act_local(i=i, source=source, target=target):
                    copy = pltpu.make_async_copy(source, target, scratch[2].at[i])
                    if step:
                        copy.wait()
                    else:
                        copy.start()

                pl.when(when)(act_local)

    def run(self, moves, first, scratch, ending):
        for i, (source, target, landing, device, when) in enumerate(moves):

            def remote(place, i=first + i, source=source, device=device):
                return pltpu.make_async_remote_copy(
                    src_ref=source,
                    dst_ref=place,
                    send_sem=scratch[0].at[i],
                    recv_sem=scratch[1].at[i],
                    device_id=device,
                    device_id_type=MESH,
                )

            def act(remote=remote, target=target, landing=landing):
                if ending:
                    remote(landing).wait_recv()
                    remote(target).wait_send()
                else:
                    remote(target).start()

            if when is None:
                act()
            else:
                pl.when(when)(act)


def plane_peers():
    peers = []
    for axis in (PY, PX):
        for offset in range(1, lax.axis_size(axis)):
            peers.append(lambda axis=axis, offset=offset: {axis: turned(axis, offset)})
    return peers


SWAP_PEERS = [
    lambda: {CORE: other(CORE)},
    lambda: {ZH: other(ZH)},
    lambda: {CORE: other(CORE), ZH: other(ZH)},
]


class SwapIn(Errand):
    def __init__(self, shard):
        super().__init__()
        self.take(shard)
        self.give((lax.axis_size(PY), lax.axis_size(PX), 2) + shard.shape)
        self.peers = SWAP_PEERS
        self.reserve(2, 1)

    def plan(self, ins, outs):
        core, half = lax.axis_index(CORE), lax.axis_index(ZH)
        home = outs[0].at[lax.axis_index(PY), lax.axis_index(PX)]
        crossed = jnp.where(core == 0, 1 - half, half)
        return [
            [
                (ins[0], home.at[core], home.at[1 - core], {CORE: 1 - core, ZH: crossed}, None),
                (ins[0], home.at[1], home.at[1], {ZH: 1 - half}, core == 1),
            ]
        ]

    def local(self, ins, outs):
        home = outs[0].at[lax.axis_index(PY), lax.axis_index(PX)]
        return [(ins[0], home.at[0], lax.axis_index(CORE) == 0)]


class Spread(Errand):
    def __init__(self, rows, stages):
        super().__init__()
        self.stages = stages
        self.give(rows.shape, rows.dtype, pltpu.HBM, self.take(rows))
        self.peers = plane_peers()
        ny, nx = rows.shape[:2]
        straight, relayed = nx + ny - 2, 2 * (nx - 1) * (ny - 1)
        self.reserve(sum(relayed if stage == RELAY else straight for stage in stages))

    def plan(self, ins, outs):
        rows = outs[0]
        ny, nx = rows.shape[:2]
        first, then = [], []
        own = {PY: lax.axis_index(PY), PX: lax.axis_index(PX)}
        sides = [(PX, nx), (PY, ny)]

        def along(moves, axis, offset, at, core):
            land = dict(at)
            land[axis] = turned(axis, -offset)
            here = rows.at[at[PY], at[PX], core]
            there = rows.at[land[PY], land[PX], core]
            moves.append((here, here, there, {axis: turned(axis, offset)}, None))

        for stage in self.stages:
            if stage == RELAY:
                for e in range(1, nx):
                    for offset in range(1, ny):
                        along(then, PY, offset, {**own, PX: turned(PX, e)}, 0)
                for e in range(1, ny):
                    for offset in range(1, nx):
                        along(then, PX, offset, {**own, PY: turned(PY, e)}, 1)
            else:
                for core, (axis, size) in enumerate(sides if stage == STRAIGHT else sides[::-1]):
                    for offset in range(1, size):
                        along(first, axis, offset, own, core)
        if STRAIGHT in self.stages:
            return [first, then] if then else [first]
        return [first + then]


class FoldFar(Errand):
    def __init__(self, grad):
        super().__init__()
        self.take(grad)
        ny, nx, _, rows, columns = grad.shape
        self.give((ny - 1, nx - 1, rows, columns))
        self.give((nx - 1, ny - 1, rows, columns))
        self.peers = plane_peers()
        self.reserve(2 * (nx - 1) * (ny - 1))

    def plan(self, ins, outs):
        grad = ins[0]
        ny, nx = grad.shape[:2]
        moves = []
        for e in range(1, nx):
            for d in range(1, ny):
                slot = outs[0].at[d - 1, e - 1]
                to = turned(PY, d)
                moves.append((grad.at[to, turned(PX, e), 0], slot, slot, {PY: to}, None))
        for e in range(1, ny):
            for d in range(1, nx):
                slot = outs[1].at[d - 1, e - 1]
                to = turned(PX, d)
                moves.append((grad.at[turned(PY, e), to, 1], slot, slot, {PX: to}, None))
        return [moves]


class FoldNear(Errand):
    def __init__(self, grad):
        super().__init__()
        self.take(grad)
        ny, nx, _, rows, columns = grad.shape
        self.give((ny - 1, rows, columns))
        self.give((nx - 1, rows, columns))
        self.peers = plane_peers()
        self.reserve(nx + ny - 2)

    def plan(self, ins, outs):
        grad = ins[0]
        ny, nx = grad.shape[:2]
        y, x = lax.axis_index(PY), lax.axis_index(PX)
        moves = []
        for d in range(1, ny):
            to, slot = turned(PY, d), outs[0].at[d - 1]
            moves.append((grad.at[to, x, 0], slot, slot, {PY: to}, None))
        for d in range(1, nx):
            to, slot = turned(PX, d), outs[1].at[d - 1]
            moves.append((grad.at[y, to, 1], slot, slot, {PX: to}, None))
        return [moves]


class FoldRelay(Errand):
    def __init__(self, sums):
        super().__init__()
        for each in sums:
            self.take(each)
            self.give(each.shape)
        self.peers = plane_peers()
        self.reserve(sums[0].shape[0] + sums[1].shape[0])

    def plan(self, ins, outs):
        moves = []
        for i, axis in enumerate((PX, PY)):
            for e in range(1, lax.axis_size(axis)):
                slot = outs[i].at[e - 1]
                moves.append((ins[i].at[e - 1], slot, slot, {axis: turned(axis, e)}, None))
        return [moves]


class SwapOut(Errand):
    def __init__(self, pair):
        super().__init__()
        self.take(pair)
        self.give(pair.shape)
        self.peers = SWAP_PEERS
        self.reserve(2, 1)

    def plan(self, ins, outs):
        core, half = lax.axis_index(CORE), lax.axis_index(ZH)
        crossed = jnp.where(core == 0, half, 1 - half)
        pair, met = ins[0], outs[0]
        return [
            [
                (pair.at[1 - core], met.at[0], met.at[0], {CORE: 1 - core, ZH: crossed}, None),
                (pair.at[1], met.at[1], met.at[1], {ZH: 1 - half}, core == 1),
            ]
        ]

    def local(self, ins, outs):
        return [(ins[0].at[0], outs[0].at[1], lax.axis_index(CORE) == 0)]


def take_counts(refs, sizes):
    taken, rest = [], list(refs)
    for size in sizes:
        taken.append(rest[:size])
        rest = rest[size:]
    return taken, rest


def kernel(parts, *refs):
    ins, refs = take_counts(refs, [len(part.arrays) for part in parts])
    outs, refs = take_counts(refs, [len(part.shapes) for part in parts])
    scratch, _ = take_counts(refs, [len(part.scratch) for part in parts])
    barrier = pltpu.get_barrier_semaphore()
    greeted = sum(part.greet(barrier) for part in parts)
    pl.semaphore_wait(barrier, greeted)

    def errands(step):
        for i in range(1, len(parts)):
            parts[i].go(step, ins[i], outs[i], scratch[i])

    errands(0)
    parts[0].begin(ins[0], outs[0], scratch[0], partial(errands, 1))
    errands(2)


def travel(collective_id, *parts):
    aliases, first_in, first_out = {}, 0, 0
    for part in parts:
        for source, result in part.aliases.items():
            aliases[first_in + source] = first_out + result
        first_in += len(part.arrays)
        first_out += len(part.shapes)
    results = pl.pallas_call(
        partial(kernel, parts),
        out_shape=[shape for part in parts for shape in part.shapes],
        in_specs=[pl.BlockSpec(memory_space=space) for part in parts for space in part.in_spaces],
        out_specs=[pl.BlockSpec(memory_space=space) for part in parts for space in part.out_spaces],
        scratch_shapes=[each for part in parts for each in part.scratch],
        input_output_aliases=aliases,
        compiler_params=pltpu.CompilerParams(
            collective_id=collective_id, has_side_effects=True, vmem_limit_bytes=24 * 2**20
        ),
        cost_estimate=pl.CostEstimate(flops=2 * 10**10, bytes_accessed=1024, transcendentals=0),
    )(*[array for part in parts for array in part.arrays])
    split, _ = take_counts(results, [len(part.shapes) for part in parts])
    return split


class Route:
    def __init__(self, shards, errands):
        self.shards = shards
        self.errands = iter(errands)
        self.rows, self.grads, self.got = {}, {}, {FAR: {}, NEAR: {}, PASS: {}, LEAVE: {}}
        self.count = 0

    def step(self, main):
        errands, parts = next(self.errands), [main]
        for name, what in errands:
            if what == (ENTER,):
                parts.append(SwapIn(self.shards[name]))
            elif what == (FAR,):
                parts.append(FoldFar(self.grads[name]))
            elif what == (NEAR,):
                parts.append(FoldNear(self.grads[name]))
            elif what == (PASS,):
                parts.append(FoldRelay(self.far_sums(name)))
            elif what == (LEAVE,):
                parts.append(SwapOut(self.pair(name)))
            else:
                parts.append(Spread(self.rows[name], what))
        results = travel(self.count, *parts)
        self.count += 1
        for (name, what), got in zip(errands, results[1:]):
            if what[0] in self.got:
                self.got[what[0]][name] = got
            else:
                self.rows[name] = got[0]
        return results[0]

    def weight(self, kind, block):
        rows = self.rows[kind, block]
        return rows.reshape(-1, rows.shape[-1])

    def give_grad(self, kind, block, grad):
        name = (kind, block)
        self.grads[name] = grad.astype(jnp.bfloat16).reshape(self.rows[name].shape)

    def own_rows(self, name, py, px, core):
        grad = self.grads[name]
        at = lax.dynamic_slice(grad, (py, px, core, 0, 0), (1, 1, 1) + grad.shape[3:])
        return at[0, 0, 0].astype(jnp.float32)

    def far_sums(self, name):
        y, x = lax.axis_index(PY), lax.axis_index(PX)
        along_y, along_x = self.got[FAR][name]
        first = [
            self.own_rows(name, y, turned(PX, e), 0)
            + jnp.sum(along_y[:, e - 1].astype(jnp.float32), 0)
            for e in range(1, lax.axis_size(PX))
        ]
        last = [
            self.own_rows(name, turned(PY, e), x, 1)
            + jnp.sum(along_x[:, e - 1].astype(jnp.float32), 0)
            for e in range(1, lax.axis_size(PY))
        ]
        return jnp.stack(first).astype(jnp.bfloat16), jnp.stack(last).astype(jnp.bfloat16)

    def pair(self, name):
        y, x = lax.axis_index(PY), lax.axis_index(PX)
        halves = []
        for core in range(2):
            near = jnp.sum(self.got[NEAR][name][core].astype(jnp.float32), 0)
            relayed = jnp.sum(self.got[PASS][name][core].astype(jnp.float32), 0)
            halves.append(self.own_rows(name, y, x, core) + near + relayed)
        return jnp.stack(halves).astype(jnp.bfloat16)

    def met(self, kind, block):
        return self.got[LEAVE][kind, block][0]


ROWS_BY_ROWS = (((1,), (1,)), ((), ()))
COLUMNS_BY_COLUMNS = (((0,), (0,)), ((), ()))


def head_of(array, which, head, local):
    first = which * local + head * HEAD_DIM
    return array[0, :, first : first + HEAD_DIM]


def soft(query, key, valid):
    scores = lax.dot_general(query, key, ROWS_BY_ROWS, preferred_element_type=jnp.float32)
    scores = jnp.where(valid > 0, scores * (1.0 / math.sqrt(HEAD_DIM)), -1e30)
    expo = jnp.exp(scores - jnp.max(scores, -1, keepdims=True))
    return expo / jnp.sum(expo, -1, keepdims=True)


def attend_kernel(normed, valid, weight_in, weight_out, triple, context, terms):
    local = context.shape[2]
    triple[0] = jnp.dot(normed[0], weight_in[...], preferred_element_type=jnp.float32).astype(
        jnp.bfloat16
    )
    parts = []
    for head in range(local // HEAD_DIM):
        query, key, value = [head_of(triple, which, head, local) for which in range(3)]
        probs = soft(query, key, valid[0]).astype(jnp.bfloat16)
        parts.append(jnp.dot(probs, value, preferred_element_type=jnp.float32))
    flat = jnp.concatenate(parts, 1).astype(jnp.bfloat16)
    context[0] = flat
    terms[0] = lax.dot_general(
        flat, weight_out[...], ROWS_BY_ROWS, preferred_element_type=jnp.float32
    ).astype(jnp.bfloat16)


def attend_back_kernel(
    triple, valid, grad_attn, weight_in, weight_out, grad_triple, terms, grad_context
):
    local = weight_out.shape[1]
    scale = 1.0 / math.sqrt(HEAD_DIM)
    grad_context[0] = jnp.dot(
        grad_attn[0], weight_out[...], preferred_element_type=jnp.float32
    ).astype(jnp.bfloat16)
    queries, keys, values = [], [], []
    for head in range(local // HEAD_DIM):
        query, key, value = [head_of(triple, which, head, local) for which in range(3)]
        grad = head_of(grad_context, 0, head, local)
        probs = soft(query, key, valid[0])
        values.append(
            lax.dot_general(
                probs.astype(jnp.bfloat16),
                grad,
                COLUMNS_BY_COLUMNS,
                preferred_element_type=jnp.float32,
            )
        )
        grad_probs = lax.dot_general(
            grad, value, ROWS_BY_ROWS, preferred_element_type=jnp.float32
        )
        tilt = jnp.sum(grad_probs * probs, -1, keepdims=True)
        grad_scores = (probs * (grad_probs - tilt)).astype(jnp.bfloat16)
        queries.append(jnp.dot(grad_scores, key, preferred_element_type=jnp.float32) * scale)
        keys.append(
            lax.dot_general(
                grad_scores, query, COLUMNS_BY_COLUMNS, preferred_element_type=jnp.float32
            )
            * scale
        )
    fresh = jnp.concatenate(queries + keys + values, 1).astype(jnp.bfloat16)
    grad_triple[0] = fresh
    terms[0] = lax.dot_general(
        fresh, weight_in[...], ROWS_BY_ROWS, preferred_element_type=jnp.float32
    ).astype(jnp.bfloat16)


def by_image(body, arrays, weights, columns, scratch=()):
    images, length = arrays[0].shape[:2]

    def block(array):
        return pl.BlockSpec((1,) + array.shape[1:], lambda i: (i, 0, 0))

    made = [jax.ShapeDtypeStruct((images, length, each), jnp.bfloat16) for each in columns]
    return pl.pallas_call(
        body,
        grid=(images,),
        out_shape=made,
        in_specs=[block(array) for array in arrays]
        + [pl.BlockSpec(weight.shape, lambda i: (0, 0)) for weight in weights],
        out_specs=[block(each) for each in made],
        scratch_shapes=[pltpu.VMEM((1, length, each), jnp.bfloat16) for each in scratch],
        compiler_params=pltpu.CompilerParams(vmem_limit_bytes=24 * 2**20),
        cost_estimate=pl.CostEstimate(flops=5 * 10**9, bytes_accessed=1024, transcendentals=0),
    )(*arrays, *weights)


def low_dot(spec, left, right):
    return jnp.einsum(spec, left, right, preferred_element_type=jnp.float32)


def attend(normed, key_valid, block, route):
    weights = [route.weight(IN, block), route.weight(OUT, block)]
    width, local = weights[1].shape
    triple, flat_context, terms = by_image(
        attend_kernel, [normed, key_valid], weights, (3 * local, local, width)
    )
    return terms, (triple, flat_context)


def feed(normed, block, route):
    inner = low_dot("bld,df->blf", normed, route.weight(EXPAND, block))
    active = jax.nn.gelu(inner, approximate=True).astype(jnp.bfloat16)
    terms = low_dot("blf,df->bld", active, route.weight(CONTRACT, block)).astype(jnp.bfloat16)
    return terms, (inner, active)


def feed_back(grad_branch, normed, saved, block, route):
    inner, active = saved
    grad_active = low_dot("bld,df->blf", grad_branch, route.weight(CONTRACT, block))
    gelu_back = jax.vjp(partial(jax.nn.gelu, approximate=True), inner)[1]
    grad_inner = gelu_back(grad_active)[0].astype(jnp.bfloat16)
    terms = low_dot("blf,df->bld", grad_inner, route.weight(EXPAND, block)).astype(jnp.bfloat16)
    route.give_grad(CONTRACT, block, low_dot("bld,blf->df", grad_branch, active))
    route.give_grad(EXPAND, block, low_dot("bld,blf->df", normed, grad_inner))
    return terms


def attend_back(grad_attn, normed, saved, key_valid, block, route):
    triple, flat_context = saved
    weights = [route.weight(IN, block), route.weight(OUT, block)]
    width, local = weights[1].shape
    grad_triple, terms = by_image(
        attend_back_kernel,
        [triple, key_valid, grad_attn],
        weights,
        (3 * local, width),
        (local,),
    )
    return terms, (normed, grad_triple, grad_attn, flat_context)


def errands_in_turn():
    def attend(block, *what):
        return [((IN, block), what), ((OUT, block), what)]

    def expand(block, *what):
        return [((EXPAND, block), what)]

    def contract(block, *what):
        return [((CONTRACT, block), what)]

    def feed(block, *what):
        return expand(block, *what) + contract(block, *what)

    return [
        attend(0, ENTER),
        attend(0, STRAIGHT) + expand(0, ENTER),
        attend(0, CROSS, RELAY) + contract(0, ENTER),
        expand(0, STRAIGHT, CROSS, RELAY) + attend(1, ENTER),
        contract(0, STRAIGHT, CROSS, RELAY) + expand(1, ENTER),
        attend(1, STRAIGHT, CROSS, RELAY) + expand(1, STRAIGHT) + contract(1, ENTER),
        contract(1, STRAIGHT, CROSS, RELAY) + expand(1, CROSS, RELAY),
        [],
        feed(1, FAR) + feed(1, NEAR),
        feed(1, PASS),
        feed(0, FAR) + attend(1, FAR) + attend(1, NEAR) + expand(1, LEAVE),
        contract(0, NEAR) + feed(0, PASS) + attend(1, PASS) + contract(1, LEAVE),
        attend(0, FAR) + expand(0, NEAR) + contract(0, LEAVE) + attend(1, LEAVE),
        attend(0, NEAR) + attend(0, PASS) + expand(0, LEAVE),
        attend(0, LEAVE),
        [],
    ]


def adam(weight, grad, moment, second, average, factor):
    grad = grad * factor
    moment = beta_first * moment + (1.0 - beta_first) * grad
    second = beta_second * second + (1.0 - beta_second) * grad * grad
    update = (
        moment
        / (1.0 - beta_first**STEP)
        / (jnp.sqrt(second / (1.0 - beta_second**STEP)) + adam_eps)
    )
    fresh = weight - learn_rate * (update + weight_decay * weight)
    average_decay = min(ema_decay, (1.0 + STEP) / (10.0 + STEP))
    average = average_decay * average + (1.0 - average_decay) * fresh
    return (fresh, moment, second, average)


def shards(
    patches,
    target_noise,
    kept_slots,
    kept_count,
    time_step,
    labels,
    teacher,
    *tables,
):
    params, moments, seconds, averages = tables[:7], tables[7:14], tables[14:21], tables[21:]
    attend_in, attend_out, expand, contract, modulation, patch_table, condition = params
    batch, length = (patches.shape[0], patches.shape[1])
    capacity = kept_slots.shape[1]
    rows, local = (attend_in.shape[1], attend_in.shape[3])
    wides, narrows = (group_size(WIDE), group_size(NARROW))
    wide_index, narrow_index = (flat_place(WIDE), flat_place(NARROW))
    images = batch * wides
    width = local * narrows
    assert batch == narrows

    shards_low = {}
    for i in range(2):
        shards_low[IN, i] = attend_in[i].reshape(rows, 3 * local).astype(jnp.bfloat16)
        shards_low[OUT, i] = attend_out[i].T.astype(jnp.bfloat16)
        shards_low[EXPAND, i] = expand[i].astype(jnp.bfloat16)
        shards_low[CONTRACT, i] = contract[i].T.astype(jnp.bfloat16)
    route = Route(shards_low, errands_in_turn())

    def own(array):
        return lax.dynamic_index_in_dim(array, narrow_index, 0, keepdims=False)

    condition_low = condition.astype(jnp.bfloat16)
    features = sinusoid(time_step, FREQ)
    onehot = (labels[:, None] == jnp.arange(CLASSES)[None, :]).astype(jnp.bfloat16)
    cond_part = jnp.dot(
        features, condition_low[:FREQ].astype(jnp.float32), precision=highest_float_accuracy
    ) + low_dot("bc,cd->bd", onehot, condition_low[FREQ:])
    pieces = jax.nn.silu(cond_part).reshape(batch, local // rows, rows)
    pieces = jnp.pad(jnp.transpose(pieces, (1, 0, 2)), ((0, 0), (0, 8 - batch), (0, 0)))
    (silu_wide,) = route.step(RowPieces(pieces))
    silu_rows = silu_wide[:, :batch].reshape(images, rows).astype(jnp.bfloat16)
    modulation_low = modulation.astype(jnp.bfloat16)
    mod_part = low_dot("ip,npkc->inkc", silu_rows, modulation_low)
    mod_part = mod_part.reshape(wides, batch, 12 * local)
    (mod_wide,) = route.step(Exchange([mod_part], [(WIDE, EACH)]))
    facts = jnp.stack([kept_count, time_step, labels], 1).astype(jnp.float32)
    facts = jnp.pad(facts, ((0, 4), (0, local - 3)))
    teacher_rows = teacher.reshape(batch * narrows, local)
    payload = jnp.concatenate([cond_part, facts[:batch], teacher_rows], 0)
    table_pad = jnp.pad(patch_table.astype(jnp.bfloat16), ((0, 15), (0, 0)))
    mod_near, everyone, tables_near = route.step(
        Exchange(
            [jnp.sum(mod_wide, 0).reshape(batch, 12, local), payload, table_pad],
            [(NARROW, EACH), (WIDE, SAME), (NARROW, SAME)],
        )
    )
    mods = jnp.transpose(mod_near, (1, 0, 2)).reshape(12, width)
    mod_enc, mod_dec = mods[:6], mods[6:]
    cond_cols = everyone[:, :batch].reshape(images, local)
    facts_all = everyone[:, batch : 2 * batch, :3]
    negatives = everyone[:, 2 * batch :].reshape(images, width)
    time_all = facts_all[:, :, 1].reshape(images).astype(jnp.int32)
    labels_all = facts_all[:, :, 2].reshape(images).astype(jnp.int32)
    patch_full = jnp.transpose(tables_near, (1, 0, 2)).reshape(48, width)

    count_own = own(kept_count).astype(jnp.float32)
    slot_valid = (jnp.arange(capacity) < own(kept_count)).astype(jnp.float32)[:, None]
    select = (own(kept_slots)[:, None] == jnp.arange(length)[None, :]).astype(
        jnp.float32
    ) * slot_valid
    open_place = 1.0 - jnp.sum(select, 0)[:, None]
    places = sinusoid(jnp.arange(length), width)
    group_counts = lax.dynamic_slice(
        facts_all[:, :, 0],
        (flat_place((PY, PX)) * 2, lax.axis_index(ZH) * 2),
        (2, 2),
    ).reshape(4)
    group_valid = (jnp.arange(capacity)[None, None, :] < group_counts[:, None, None]).astype(
        jnp.float32
    )
    all_valid = jnp.ones((4, 1, length), jnp.float32)
    kept_patches = low_dot("cl,lp->cp", select.astype(jnp.bfloat16), own(patches))
    embed = low_dot("cp,pd->cd", kept_patches.astype(jnp.bfloat16), patch_full[:PATCH_IN])
    embed = embed + jnp.dot(select, places, precision=highest_float_accuracy)
    mask_token = patch_full[2 * PATCH_IN : 2 * PATCH_IN + 1].astype(jnp.float32)
    base = open_place * mask_token + places
    head = patch_full[PATCH_IN : 2 * PATCH_IN]
    count_all = images * length * PATCH_IN

    (normed_a0,) = route.step(Enter(embed, mod_enc))
    terms, saved_a0 = attend(normed_a0, group_valid, 0, route)
    normed_m0, attn0, middle0 = route.step(Middle(terms, embed, mod_enc))
    terms, saved_m0 = feed(normed_m0, 0, route)
    positive = ((wide_index * batch + narrow_index) == jnp.arange(images)).astype(jnp.float32)
    contrast = (slot_valid, count_own.reshape(1, 1), negatives, positive[:, None])
    normed_a1, branch0, _, decode_in, grad_pool, nce = route.step(
        Decode(terms, middle0, mod_enc, mod_dec, select.T, base, contrast)
    )
    terms, saved_a1 = attend(normed_a1, all_valid, 1, route)
    normed_m1, attn1, middle1 = route.step(Middle(terms, decode_in, mod_dec))
    terms, saved_m1 = feed(normed_m1, 1, route)
    grad_branch, grad_decoded, gate_m1, grad_head, square = route.step(
        Turn(terms, middle1, mod_dec, head, own(target_noise), count_all)
    )

    terms = feed_back(grad_branch, normed_m1, saved_m1, 1, route)
    grad_attn, grad_mid, sums_m1 = route.step(
        MiddleBack(terms, middle1, attn1, grad_decoded, mod_dec)
    )
    terms, pairs = attend_back(grad_attn, normed_a1, saved_a1, all_valid, 1, route)
    back_to = (open_place, select, slot_valid, grad_pool, branch0, mod_enc)
    grad_branch, grad_encoded, sums_a1, grad_in, grad_out = route.step(
        Encode(terms, decode_in, grad_mid, mod_dec, back_to, pairs)
    )
    route.give_grad(IN, 1, grad_in)
    route.give_grad(OUT, 1, grad_out)
    terms = feed_back(grad_branch, normed_m0, saved_m0, 0, route)
    grad_attn, grad_mid, sums_m0 = route.step(
        MiddleBack(terms, middle0, attn0, grad_encoded, mod_enc)
    )
    terms, pairs = attend_back(grad_attn, normed_a0, saved_a0, group_valid, 0, route)
    sums = (sums_m0, sums_a1, sums_m1, gate_m1, grad_head)
    rows_near, grad_in, grad_out = route.step(
        Leave(terms, embed, grad_mid, mod_enc, kept_patches, sums, pairs)
    )
    route.give_grad(IN, 0, grad_in)
    route.give_grad(OUT, 0, grad_out)

    mods_near = rows_near[:, :12].reshape(narrows, 12 * local)
    table_near = rows_near[:, 12:45]
    table_sum = jnp.pad(jnp.sum(table_near, 0), ((0, 15), (0, 0))).astype(jnp.bfloat16)
    mods_all, table_all = route.step(
        Exchange([mods_near, table_sum], [(WIDE, SAME), (WIDE, SAME)])
    )
    grad_patch_table = jnp.sum(table_all.astype(jnp.float32), 0)[:33]
    mods_all = mods_all.reshape(images, 2, 6, local)
    silu_broad = silu_rows.astype(jnp.float32)
    grad_modulation = jnp.einsum(
        "ip,inkc->npkc", silu_broad, mods_all, precision=highest_float_accuracy
    )
    grad_silu = jnp.einsum(
        "inkc,npkc->ip",
        mods_all,
        modulation_low.astype(jnp.float32),
        precision=highest_float_accuracy,
    )
    (silu_near,) = route.step(Exchange([grad_silu], [(NARROW, SAME)]))
    (silu_wide,) = route.step(Exchange([jnp.sum(silu_near, 0)], [(WIDE, SAME)]))
    grad_silu = jnp.transpose(silu_wide, (1, 0, 2)).reshape(images, width)
    grad_silu = lax.dynamic_slice_in_dim(grad_silu, narrow_index * local, local, 1)
    grad_cond = jax.vjp(jax.nn.silu, cond_cols)[1](grad_silu)[0]
    features_all = sinusoid(time_all, FREQ)
    onehot_all = (labels_all[:, None] == jnp.arange(CLASSES)[None, :]).astype(jnp.float32)
    grad_condition = jnp.dot(
        jnp.concatenate([features_all, onehot_all], 1).T, grad_cond, precision=highest_float_accuracy
    )


    def totals(kind, shape):
        both = [route.met(kind, i).astype(jnp.float32) for i in range(2)]
        return jnp.stack([shape(each[0] + each[1]) for each in both])

    def by_third(g):
        thirds = [g[:, i * local : (i + 1) * local] for i in range(3)]
        return jnp.transpose(jnp.stack(thirds), (1, 0, 2))

    grads = [
        totals(IN, by_third),
        totals(OUT, lambda g: g.T),
        totals(EXPAND, lambda g: g),
        totals(CONTRACT, lambda g: g.T),
        grad_modulation,
        grad_patch_table,
        grad_condition,
    ]
    square_small = jnp.sum(grad_patch_table * grad_patch_table) + jnp.sum(
        grad_condition * grad_condition
    )
    square_local = jnp.sum(grad_modulation * grad_modulation)
    square_local = square_local + (wide_index == 0).astype(jnp.float32) * square_small
    scalars = jnp.stack([square[0, 0], nce[0, 0], square_local])
    scalars = jnp.pad(scalars[None, :], ((0, 7), (0, 125)))
    mets = [route.met(kind, i) for i in range(2) for kind in (IN, OUT, EXPAND, CONTRACT)]
    (scalars_all,) = route.step(Norm(scalars, mets))
    sums = jnp.sum(scalars_all[:, 0], 0)
    grad_norm = jnp.sqrt(sums[2])
    factor = clip_norm / jnp.maximum(grad_norm, clip_norm)
    fresh = [
        adam(params[i], grads[i], moments[i], seconds[i], averages[i], factor) for i in range(7)
    ]
    loss_parts = jnp.stack([sums[0] / count_all, sums[1] / images])
    return (loss_parts, grad_norm) + tuple(fresh[i][k] for k in range(4) for i in range(7))


def solution(mesh):
    wide, narrow = mesh.devices.shape
    planes = wide // 2
    across = max(n for n in range(1, math.isqrt(planes) + 1) if planes % n == 0)
    grid = Mesh(mesh.devices.reshape(across, planes // across, 2, narrow // 2, 2), ALL)
    image_specs = (
        P(WIDE, None, None),
        P(WIDE, None, None),
        P(WIDE, None),
        P(WIDE),
        P(WIDE),
        P(WIDE),
        P(WIDE, None),
    )
    table_specs = (
        P(None, WIDE, None, NARROW),
        P(None, NARROW, WIDE),
        P(None, WIDE, NARROW),
        P(None, NARROW, WIDE),
        P(None, WIDE, None, NARROW),
        P(None, NARROW),
        P(None, NARROW),
    )
    return jax.shard_map(
        shards,
        mesh=grid,
        in_specs=image_specs + table_specs * 4,
        out_specs=(P(), P()) + table_specs * 4,
        check_vma=False,
    )
```

```python
from functools import partial
import math

import jax
import jax.numpy as jnp
from jax import lax
from jax.experimental import pallas as pl
from jax.experimental.pallas import tpu as pltpu
from jax.sharding import Mesh
from jax.sharding import PartitionSpec as P

HEAD_DIM = 72
CLASSES = 1000
FREQ = 256
PATCH_IN = 16
STEP = 10

MESH = pl.DeviceIdType.MESH
PY, PX, CORE, ZH, ZL = "py", "px", "core", "zh", "zl"
WIDE = (PY, PX, CORE)
NARROW = (ZH, ZL)
ALL = WIDE + NARROW
EACH, SAME = range(2)
IN, OUT, EXPAND, CONTRACT = range(4)
TERM_SQUARE, TERM_HEAD, TERM_GATE, TERM_SHIFT, TERM_SCALE, TERM_MASK, TERM_PATCH = range(7)
ENTER, STRAIGHT, CROSS, RELAY, FAR, NEAR, PASS, LEAVE = range(8)

highest_float_accuracy = lax.Precision.HIGHEST
norm_eps = 1e-06
contrast_sharpness_divisor = 0.02
nce_weight = 0.5
learn_rate = 0.05
beta_first = 0.9
beta_second = 0.999
adam_eps = 1e-08
weight_decay = 0.05
clip_norm = 0.05
ema_decay = 0.9999


def layer_norm(values):
    center = values - jnp.mean(values, -1, keepdims=True)
    return center * lax.rsqrt(jnp.mean(center * center, -1, keepdims=True) + norm_eps)


def modulate(values, shift, scale):
    return layer_norm(values) * (1.0 + scale[None, :]) + shift[None, :]


def sinusoid(places, width):
    half = width // 2
    freqs = jnp.exp(-math.log(10000.0) * jnp.arange(half, dtype=jnp.float32) / half)
    angle = places.astype(jnp.float32)[:, None] * freqs[None, :]
    return jnp.concatenate([jnp.cos(angle), jnp.sin(angle)], -1)


def flat_place(axes):
    place = 0
    for axis in axes:
        place = place * lax.axis_size(axis) + lax.axis_index(axis)
    return place


def group_size(axes):
    size = 1
    for axis in axes:
        size = size * lax.axis_size(axis)
    return size


def device_at(axes, place):
    where = {}
    for axis in reversed(axes):
        where[axis] = lax.rem(place, lax.axis_size(axis))
        place = place // lax.axis_size(axis)
    return where


def turned(axis, offset):
    size = lax.axis_size(axis)
    return lax.rem(lax.axis_index(axis) + (offset % size), size)


def other(axis):
    return 1 - lax.axis_index(axis)


class Part:
    def __init__(self):
        self.arrays, self.in_spaces = [], []
        self.shapes, self.out_spaces = [], []
        self.aliases = {}
        self.scratch = []
        self.peers = []

    def take(self, array, space=pltpu.HBM):
        self.arrays.append(array)
        self.in_spaces.append(space)
        return len(self.arrays) - 1

    def give(self, shape, dtype=jnp.bfloat16, space=pltpu.HBM, source=None):
        held = pltpu.HBM if space == pltpu.HBM else jax.ShapeDtypeStruct
        self.shapes.append(held(shape, dtype))
        self.out_spaces.append(space)
        if source is not None:
            self.aliases[source] = len(self.shapes) - 1
        return len(self.shapes) - 1

    def greet(self, barrier):
        for peer in self.peers:
            pl.semaphore_signal(barrier, inc=1, device_id=peer(), device_id_type=MESH)
        return len(self.peers)

    def begin(self, ins, outs, scratch, halfway):
        pass

    def go(self, step, ins, outs, scratch):
        pass


class Exchange(Part):
    def __init__(self, arrays, specs):
        super().__init__()
        self.specs = specs
        for array, (axes, mode) in zip(arrays, specs):
            size = group_size(axes)
            piece = array.shape[1:] if mode == EACH else array.shape
            self.take(array, pltpu.VMEM)
            self.give((size,) + piece, array.dtype, pltpu.VMEM)
            self.scratch += [pltpu.SemaphoreType.DMA((size,)), pltpu.SemaphoreType.DMA((size,))]

    def greet(self, barrier):
        greeted = 0
        for axes, _ in self.specs:
            size, me = group_size(axes), flat_place(axes)
            greeted += size - 1

            def signal(offset, carry, axes=axes, size=size, me=me):
                target = lax.rem(me + offset, size)
                pl.semaphore_signal(
                    barrier, inc=1, device_id=device_at(axes, target), device_id_type=MESH
                )
                return carry

            lax.fori_loop(1, size, signal, 0)
        return greeted

    def begin(self, ins, outs, scratch, halfway):
        def copy_to(index, offset, arriving):
            axes, mode = self.specs[index]
            size, me = group_size(axes), flat_place(axes)
            target = lax.rem(me + offset, size)
            return pltpu.make_async_remote_copy(
                src_ref=ins[index].at[target] if mode == EACH else ins[index],
                dst_ref=outs[index].at[target if arriving else me],
                send_sem=scratch[2 * index].at[target],
                recv_sem=scratch[2 * index + 1].at[target if arriving else me],
                device_id=device_at(axes, target),
                device_id_type=MESH,
            )

        for index, (axes, mode) in enumerate(self.specs):

            def start(offset, carry, index=index):
                copy_to(index, offset, False).start()
                return carry

            lax.fori_loop(1, group_size(axes), start, 0)
        for index, (axes, mode) in enumerate(self.specs):
            me = flat_place(axes)
            outs[index][me] = ins[index][me] if mode == EACH else ins[index][...]
        for index, (axes, mode) in enumerate(self.specs):

            def end(offset, carry, index=index):
                copy_to(index, offset, True).wait_recv()
                copy_to(index, offset, False).wait_send()
                return carry

            lax.fori_loop(1, group_size(axes), end, 0)
        halfway()


class Norm(Exchange):
    def __init__(self, scalars, mets):
        super().__init__([scalars], [(ALL, SAME)])
        for met in mets:
            self.take(met, pltpu.VMEM)
        self.scratch.append(pltpu.VMEM(scalars.shape, jnp.float32))

    def begin(self, ins, outs, scratch, halfway):
        square = jnp.zeros((8, 128), jnp.float32)
        for met in ins[1:]:
            total = met[0].astype(jnp.float32) + met[1].astype(jnp.float32)
            columns = total.shape[1]
            squares = total * total
            if squares.shape[0] % 8:
                squares = jnp.pad(fold(squares), ((0, 7), (0, 0)))
            eights = jnp.sum(squares.reshape(-1, 8, columns), 0)
            for start in range(0, columns, 128):
                lanes = eights[:, start : start + 128]
                if lanes.shape[1] < 128:
                    lanes = jnp.pad(lanes, ((0, 0), (0, 128 - lanes.shape[1])))
                square = square + lanes
        lane = lax.broadcasted_iota(jnp.int32, (8, 128), 1)
        scratch[2][...] = ins[0][...] + jnp.where(lane == 2, jnp.sum(square), 0.0)
        super().begin([scratch[2]], outs, scratch[:2], halfway)


class RowPieces(Part):
    def __init__(self, pieces):
        super().__init__()
        self.each = pieces.shape[0]
        wides, narrows = group_size(WIDE), group_size(NARROW)
        self.take(pieces, pltpu.VMEM)
        self.give((wides,) + pieces.shape[1:], pieces.dtype, pltpu.VMEM)
        self.scratch = [
            pltpu.SemaphoreType.DMA((self.each * narrows,)),
            pltpu.SemaphoreType.DMA((wides,)),
        ]

    def sends(self):
        narrows, me = group_size(NARROW), flat_place(WIDE) * group_size(NARROW) + flat_place(NARROW)
        for j in range(self.each):
            for z in range(narrows):
                wide = flat_place(NARROW) * self.each + j
                to = {**device_at(WIDE, wide), **device_at(NARROW, jnp.int32(z))}
                yield j, z, to, wide * narrows + z != me

    def receives(self):
        narrows, me = group_size(NARROW), flat_place(WIDE) * group_size(NARROW) + flat_place(NARROW)
        z = flat_place(WIDE) // self.each
        for w in range(group_size(WIDE)):
            to = {**device_at(WIDE, jnp.int32(w)), **device_at(NARROW, z)}
            yield w, to, w * narrows + z != me

    def greet(self, barrier):
        for _, _, to, remote in self.sends():

            @pl.when(remote)
            def _(to=to):
                pl.semaphore_signal(barrier, inc=1, device_id=to, device_id_type=MESH)

        for _, to, remote in self.receives():

            @pl.when(remote)
            def _(to=to):
                pl.semaphore_signal(barrier, inc=1, device_id=to, device_id_type=MESH)

        counts = [r.astype(jnp.int32) for _, _, _, r in self.sends()]
        counts += [r.astype(jnp.int32) for _, _, r in self.receives()]
        return sum(counts)

    def begin(self, ins, outs, scratch, halfway):
        me = flat_place(WIDE)
        z = flat_place(WIDE) // self.each
        narrows = group_size(NARROW)

        def copy(j, slot, sem, to):
            return pltpu.make_async_remote_copy(
                src_ref=ins[0].at[j],
                dst_ref=outs[0].at[slot],
                send_sem=scratch[0].at[sem],
                recv_sem=scratch[1].at[slot],
                device_id=to,
                device_id_type=MESH,
            )

        for j, t, to, remote in self.sends():

            @pl.when(remote)
            def _(j=j, t=t, to=to):
                copy(j, me, j * narrows + t, to).start()

            @pl.when(jnp.logical_not(remote))
            def _(j=j):
                outs[0][me] = ins[0][j]

        for w, to, remote in self.receives():

            @pl.when(remote)
            def _(w=w, to=to):
                copy(0, w, 0, to).wait_recv()

        for j, t, to, remote in self.sends():

            @pl.when(remote)
            def _(j=j, t=t, to=to):
                copy(j, me, j * narrows + t, to).wait_send()

        halfway()


def chunk_of(length):
    return 64 if length % 64 == 0 else 32


def normal(values):
    center = values - jnp.mean(values, -1, keepdims=True)
    scale = lax.rsqrt(jnp.mean(center * center, -1, keepdims=True) + norm_eps)
    return center * scale, scale


def normal_back(grad, unit, scale):
    flat = jnp.mean(grad, -1, keepdims=True)
    tilt = jnp.mean(grad * unit, -1, keepdims=True)
    return scale * (grad - flat - unit * tilt)


def fold(values):
    return jnp.sum(values, 0, keepdims=True)


def full_dot(left, right):
    return jnp.dot(
        left, right, precision=highest_float_accuracy, preferred_element_type=jnp.float32
    )


SHIFT_A, SCALE_A, GATE_A, SHIFT_M, SCALE_M, GATE_M = range(6)


class Bridge(Part):
    whole = False
    sends_on = True

    def __init__(self, terms, more, width, length_in, length_out):
        super().__init__()
        self.length_in, self.length_out, self.width = length_in, length_out, width
        self.sums = terms is not None
        self.first = 0
        if self.sums:
            self.take(terms, pltpu.VMEM)
            self.first = 1
        self.fetched = []
        for array in more:
            large = array.size * array.dtype.itemsize >= 2**18
            if large:
                array = pltpu.with_memory_space_constraint(array, pltpu.HBM)
            self.fetched.append(large)
            self.take(array, pltpu.HBM if large else pltpu.VMEM)
        if self.sends_on:
            self.give((4, length_out, width), jnp.bfloat16, pltpu.VMEM)
        self.peers = [lambda: {CORE: other(CORE)}, lambda: {ZL: other(ZL)}]
        self.scratch = [
            pltpu.VMEM(array.shape, array.dtype)
            for array, large in zip(more, self.fetched)
            if large
        ]
        self.scratch.append(pltpu.SemaphoreType.DMA((len(more),)))
        if self.sums:
            self.scratch += [pltpu.VMEM((length_in, width), jnp.bfloat16)] * 4
            self.scratch += self.sems(length_in)
        if self.sends_on:
            self.scratch += self.sems(length_out)

    def result(self, shape, dtype=jnp.float32):
        self.give(shape, dtype, pltpu.VMEM)

    def sems(self, length):
        steps = length // chunk_of(length)
        return [pltpu.SemaphoreType.DMA((3, steps)), pltpu.SemaphoreType.DMA((3, steps))]

    def ranks(self):
        core, low = lax.axis_index(CORE), lax.axis_index(ZL)
        return core * 2 + low, (1 - core) * 2 + low, core * 2 + 1 - low, (1 - core) * 2 + 1 - low

    def copy(self, source, target, sems, kind, step):
        return pltpu.make_async_remote_copy(
            src_ref=source,
            dst_ref=target,
            send_sem=sems[0].at[kind, step],
            recv_sem=sems[1].at[kind, step],
            device_id={ZL: other(ZL)} if kind == 0 else {CORE: other(CORE)},
            device_id_type=MESH,
        )

    def rows(self, length):
        chunk = chunk_of(length)
        return [pl.ds(s * chunk, chunk) for s in range(length // chunk)]

    def begin(self, ins, outs, scratch, halfway):
        me, mate, away, away_mate = self.ranks()
        given = list(ins[self.first :])
        made = outs[1:] if self.sends_on else outs
        fetches = []
        held, scratch = scratch[: sum(self.fetched)], scratch[sum(self.fetched) :]
        for i, large in enumerate(self.fetched):
            if large:
                place = held[len(fetches)]
                fetches.append(pltpu.make_async_copy(given[i], place, scratch[0].at[i]))
                fetches[-1].start()
                given[i] = place
        scratch = scratch[1:]
        state = self.start(given, made)
        sends = []
        rows_in, rows_out = self.rows(self.length_in), self.rows(self.length_out)
        if self.sums:
            terms = ins[0]
            near, home, stage, far = scratch[:4]
            sems = scratch[4:6]
            to_near = [
                self.copy(terms.at[away_mate, r], near.at[r], sems, 1, s)
                for s, r in enumerate(rows_in)
            ]
            to_home = [
                self.copy(terms.at[mate, r], home.at[r], sems, 2, s) for s, r in enumerate(rows_in)
            ]
            to_far = [self.copy(stage.at[r], far.at[r], sems, 0, s) for s, r in enumerate(rows_in)]
            for each in to_near:
                each.start()
            for each in to_home:
                each.start()
            for s, r in enumerate(rows_in):
                to_near[s].wait_recv()
                both = terms[away, r].astype(jnp.float32) + near[r].astype(jnp.float32)
                stage[r] = both.astype(jnp.bfloat16)
                to_far[s].start()
            sends += to_near + to_home + to_far

            def total(s, r):
                to_home[s].wait_recv()
                own = terms[me, r].astype(jnp.float32) + home[r].astype(jnp.float32)
                to_far[s].wait_recv()
                return own + far[r].astype(jnp.float32)

        else:

            def total(s, r):
                return None

        if self.sends_on:
            every = outs[0]
            sems_out = scratch[-2:]

            def move(kind, here, there, s, r):
                return self.copy(every.at[here, r], every.at[there, r], sems_out, kind, s)

            def pass_on(s, r, fresh):
                every[me, r] = fresh
                for kind in (0, 1):
                    each = move(kind, me, me, s, r)
                    each.start()
                    sends.append(each)

        for each in fetches:
            each.wait()
        if self.whole:
            for s, r in enumerate(rows_in):
                self.collect(r, total(s, r), given, made, state)
            self.turn(given, made, state)
            for s, r in enumerate(rows_out):
                pass_on(s, r, self.work(r, None, given, made, state))
        else:
            for s, r in enumerate(rows_in):
                fresh = self.work(r, total(s, r), given, made, state)
                if self.sends_on:
                    pass_on(s, r, fresh)
        self.end(given, made, state)
        self.aside(given, made)
        if self.sums:
            halfway()
        if self.sends_on:
            for s, r in enumerate(rows_out):
                move(0, me, away, s, r).wait_recv()
                each = move(2, away, away, s, r)
                each.start()
                sends.append(each)
            for s, r in enumerate(rows_out):
                move(1, me, mate, s, r).wait_recv()
                move(2, away, away_mate, s, r).wait_recv()
        for each in sends:
            each.wait_send()
        if not self.sums:
            halfway()

    def start(self, given, made):
        return {}

    def add(self, state, name, value):
        state[name] = value if name not in state else state[name] + value

    def end(self, given, made, state):
        pass

    def aside(self, given, made):
        pass


def outer(left, right, result):
    step = 384 if left.shape[2] % 384 == 0 else 128

    def tile(i, carry):
        columns = pl.ds(pl.multiple_of(i * step, step), step)
        value = lax.dot_general(
            left[:, :, columns].reshape(-1, step),
            right[...].reshape(-1, right.shape[2]),
            (((0,), (0,)), ((), ())),
            preferred_element_type=jnp.float32,
        )
        result[columns] = value.astype(jnp.bfloat16)
        return carry

    lax.fori_loop(0, left.shape[2] // step, tile, 0)


class Enter(Bridge):
    def __init__(self, values, mod):
        length, width = values.shape
        super().__init__(None, [values, mod], width, length, length)

    def work(self, r, total, given, made, state):
        values, mod = given
        unit, _ = normal(values[r])
        return (unit * (1.0 + mod[SCALE_A : SCALE_A + 1]) + mod[SHIFT_A : SHIFT_A + 1]).astype(
            jnp.bfloat16
        )


class Middle(Bridge):
    def __init__(self, terms, values, mod):
        length, width = values.shape
        super().__init__(terms, [values, mod], width, length, length)
        self.result((length, width))
        self.result((length, width))

    def work(self, r, total, given, made, state):
        values, mod = given
        attn, middle = made
        attn[r] = total
        fresh = values[r] + mod[GATE_A : GATE_A + 1] * total
        middle[r] = fresh
        unit, _ = normal(fresh)
        return (unit * (1.0 + mod[SCALE_M : SCALE_M + 1]) + mod[SHIFT_M : SHIFT_M + 1]).astype(
            jnp.bfloat16
        )


class Decode(Bridge):
    whole = True

    def __init__(self, terms, middle, mod, mod_next, place, base, contrast):
        (length, width), (length_next, _) = middle.shape, base.shape
        more = [middle, mod, mod_next, place, base, *contrast]
        super().__init__(terms, more, width, length, length_next)
        self.result((length, width))
        self.result((length, width))
        self.result((length_next, width))
        self.result((1, width))
        self.result((1, 1))

    def collect(self, r, total, given, made, state):
        middle, mod = given[:2]
        branch, encoded = made[:2]
        branch[r] = total
        encoded[r] = middle[r] + mod[GATE_M : GATE_M + 1] * total

    def turn(self, given, made, state):
        place, base = given[3:5]
        made[2][...] = full_dot(place[...], made[1][...]) + base[...]

    def work(self, r, total, given, made, state):
        mod = given[2]
        unit, _ = normal(made[2][r])
        return (unit * (1.0 + mod[SCALE_A : SCALE_A + 1]) + mod[SHIFT_A : SHIFT_A + 1]).astype(
            jnp.bfloat16
        )


    def aside(self, given, made):
        valid, count, teachers, positive = given[5:]
        pooled = fold(made[1][...] * valid[...]) / count[...]
        scale = lax.rsqrt(jnp.sum(pooled * pooled, -1, keepdims=True) + 1e-06)
        others = teachers[...]
        others = others * lax.rsqrt(jnp.sum(others * others, -1, keepdims=True) + 1e-06)
        logits = jnp.sum(pooled * scale * others, -1, keepdims=True) / contrast_sharpness_divisor
        peak = jnp.max(logits, 0, keepdims=True)
        expo = jnp.exp(logits - peak)
        total = fold(expo)
        made[4][...] = peak + jnp.log(total) - fold(logits * positive[...])
        weight = (expo / total - positive[...]) * (nce_weight / others.shape[0])
        grad = fold(weight * others) / contrast_sharpness_divisor
        along = jnp.sum(pooled * grad, -1, keepdims=True)
        made[3][...] = scale * (grad - pooled * (scale * scale * along)) / count[...]


class Turn(Bridge):
    def __init__(self, terms, middle, mod, head, noise, count_all):
        length, width = middle.shape
        super().__init__(terms, [middle, mod, head, noise], width, length, length)
        self.scale = 2.0 / count_all
        self.result((length, width))
        self.result((1, width))
        self.result(head.shape)
        self.result((1, 1))

    def work(self, r, total, given, made, state):
        middle, mod, head, noise = given
        gate = mod[GATE_M : GATE_M + 1]
        unit, scale = normal(middle[r] + gate * total)
        low = unit.astype(jnp.bfloat16)
        rows_by_rows = (((1,), (1,)), ((), ()))
        predict = lax.dot_general(low, head[...], rows_by_rows, preferred_element_type=jnp.float32)
        error = predict - noise[r]
        self.add(state, TERM_SQUARE, jnp.sum(error * error, keepdims=True))
        grad_predict = (error * self.scale).astype(jnp.bfloat16)
        columns_by_columns = (((0,), (0,)), ((), ()))
        self.add(
            state,
            TERM_HEAD,
            lax.dot_general(
                grad_predict, low, columns_by_columns, preferred_element_type=jnp.float32
            ),
        )
        grad_final = jnp.dot(grad_predict, head[...], preferred_element_type=jnp.float32)
        grad = normal_back(grad_final, unit, scale)
        made[0][r] = grad
        self.add(state, TERM_GATE, fold(grad * total))
        return (gate * grad).astype(jnp.bfloat16)

    def end(self, given, made, state):
        made[1][...] = state[TERM_GATE]
        made[2][...] = state[TERM_HEAD]
        made[3][...] = state[TERM_SQUARE]


class MiddleBack(Bridge):
    def __init__(self, terms, middle, attn, grad, mod):
        length, width = middle.shape
        super().__init__(terms, [middle, attn, grad, mod], width, length, length)
        self.result((length, width))
        self.result((3, width))

    def work(self, r, total, given, made, state):
        middle, attn, grad, mod = given
        unit, scale = normal(middle[r])
        self.add(state, TERM_SHIFT, fold(total))
        self.add(state, TERM_SCALE, fold(total * unit))
        back = normal_back(total * (1.0 + mod[SCALE_M : SCALE_M + 1]), unit, scale)
        fresh = grad[r] + back
        made[0][r] = fresh
        self.add(state, TERM_GATE, fold(fresh * attn[r]))
        return (mod[GATE_A : GATE_A + 1] * fresh).astype(jnp.bfloat16)

    def end(self, given, made, state):
        made[1][0:1] = state[TERM_SHIFT]
        made[1][1:2] = state[TERM_SCALE]
        made[1][2:3] = state[TERM_GATE]


class Encode(Bridge):
    whole = True

    def __init__(self, terms, values, grad, mod, more, pairs):
        branch = more[4]
        (length, width), (length_next, _) = values.shape, branch.shape
        super().__init__(
            terms,
            [values, grad, mod, *more, *pairs],
            width,
            length,
            length_next,
        )
        self.result((length_next, width))
        self.result((4, width))
        self.result((width, pairs[1].shape[2]), jnp.bfloat16)
        self.result((width, pairs[3].shape[2]), jnp.bfloat16)
        self.scratch = [pltpu.VMEM((length, width), jnp.float32)] + self.scratch

    def begin(self, ins, outs, scratch, halfway):
        self.held = scratch[0]
        super().begin(ins, outs, scratch[1:], halfway)

    def collect(self, r, total, given, made, state):
        values, grad, mod, open_place = given[:4]
        unit, scale = normal(values[r])
        self.add(state, TERM_SHIFT, fold(total))
        self.add(state, TERM_SCALE, fold(total * unit))
        back = normal_back(total * (1.0 + mod[SCALE_A : SCALE_A + 1]), unit, scale)
        fresh = grad[r] + back
        self.held[r] = fresh
        self.add(state, TERM_MASK, fold(open_place[r] * fresh))

    def turn(self, given, made, state):
        select, (valid, pool) = given[4], given[5:7]
        made[0][...] = full_dot(select[...], self.held[...]) + valid[...] * pool[...]

    def work(self, r, total, given, made, state):
        branch, mod_next = given[7:9]
        fresh = made[0][r]
        self.add(state, TERM_GATE, fold(fresh * branch[r]))
        return (mod_next[GATE_M : GATE_M + 1] * fresh).astype(jnp.bfloat16)

    def end(self, given, made, state):
        made[1][0:1] = state[TERM_SHIFT]
        made[1][1:2] = state[TERM_SCALE]
        made[1][2:3] = state[TERM_GATE]
        made[1][3:4] = state[TERM_MASK]

    def aside(self, given, made):
        outer(given[9], given[10], made[2])
        outer(given[11], given[12], made[3])


class Leave(Bridge):
    sends_on = False

    def __init__(self, terms, values, grad, mod, kept, sums, pairs):
        length, width = values.shape
        super().__init__(terms, [values, grad, mod, kept, *sums, *pairs], width, length, length)
        narrows = group_size(NARROW)
        piece = jax.ShapeDtypeStruct((narrows, 48, width // narrows), jnp.float32)
        self.tell = Exchange([piece], [(NARROW, EACH)])
        self.result(piece.shape)
        self.result((width, pairs[1].shape[2]), jnp.bfloat16)
        self.result((width, pairs[3].shape[2]), jnp.bfloat16)
        self.scratch = (
            [pltpu.VMEM((48, width), jnp.float32), pltpu.VMEM(piece.shape, jnp.float32)]
            + self.tell.scratch
            + self.scratch
        )

    def greet(self, barrier):
        return super().greet(barrier) + self.tell.greet(barrier)

    def begin(self, ins, outs, scratch, halfway):
        self.table, self.piece = scratch[:2]
        self.tell_sems = scratch[2:4]
        super().begin(ins, outs, scratch[4:], halfway)

    def work(self, r, total, given, made, state):
        values, grad, mod, kept = given[:4]
        unit, scale = normal(values[r])
        self.add(state, TERM_SHIFT, fold(total))
        self.add(state, TERM_SCALE, fold(total * unit))
        back = normal_back(total * (1.0 + mod[SCALE_A : SCALE_A + 1]), unit, scale)
        columns_by_columns = (((0,), (0,)), ((), ()))
        self.add(
            state,
            TERM_PATCH,
            lax.dot_general(
                kept[r],
                grad[r] + back,
                columns_by_columns,
                precision=highest_float_accuracy,
                preferred_element_type=jnp.float32,
            ),
        )

    def end(self, given, made, state):
        sums_m0, sums_a1, sums_m1, gate_m1, head = given[4:9]
        table = self.table
        table[...] = jnp.zeros(table.shape, jnp.float32)
        table[0:1] = state[TERM_SHIFT]
        table[1:2] = state[TERM_SCALE]
        table[2:3] = sums_m0[2:3]
        table[3:5] = sums_m0[0:2]
        table[5:6] = sums_a1[2:3]
        table[6:8] = sums_a1[0:2]
        table[8:9] = sums_m1[2:3]
        table[9:11] = sums_m1[0:2]
        table[11:12] = gate_m1[...]
        table[12:28] = state[TERM_PATCH]
        table[28:44] = head[...]
        table[44:45] = sums_a1[3:4]
        local = self.piece.shape[2]
        for z in range(self.piece.shape[0]):
            self.piece[z] = table[:, z * local : (z + 1) * local]
        self.tell.begin([self.piece], made[:1], self.tell_sems, lambda: None)

    def aside(self, given, made):
        outer(given[9], given[10], made[1])
        outer(given[11], given[12], made[2])


class Errand(Part):
    def plan(self, ins, outs):
        raise NotImplementedError

    def local(self, ins, outs):
        return []

    def reserve(self, count, local=0):
        self.scratch = [pltpu.SemaphoreType.DMA((count,)), pltpu.SemaphoreType.DMA((count,))]
        if local:
            self.scratch.append(pltpu.SemaphoreType.DMA((local,)))

    def go(self, step, ins, outs, scratch):
        first = 0
        plans = self.plan(ins, outs)
        if step == 1 and len(plans) == 1:
            return
        for turn, moves in enumerate(plans):
            last = turn == len(plans) - 1
            if step == (2 if last else turn + 1):
                self.run(moves, first, scratch, True)
            if step == turn:
                self.run(moves, first, scratch, False)
            first += len(moves)
        if step != 1:
            for i, (source, target, when) in enumerate(self.local(ins, outs)):

                def act_local(i=i, source=source, target=target):
                    copy = pltpu.make_async_copy(source, target, scratch[2].at[i])
                    if step:
                        copy.wait()
                    else:
                        copy.start()

                pl.when(when)(act_local)

    def run(self, moves, first, scratch, ending):
        for i, (source, target, landing, device, when) in enumerate(moves):

            def remote(place, i=first + i, source=source, device=device):
                return pltpu.make_async_remote_copy(
                    src_ref=source,
                    dst_ref=place,
                    send_sem=scratch[0].at[i],
                    recv_sem=scratch[1].at[i],
                    device_id=device,
                    device_id_type=MESH,
                )

            def act(remote=remote, target=target, landing=landing):
                if ending:
                    remote(landing).wait_recv()
                    remote(target).wait_send()
                else:
                    remote(target).start()

            if when is None:
                act()
            else:
                pl.when(when)(act)


def plane_peers():
    peers = []
    for axis in (PY, PX):
        for offset in range(1, lax.axis_size(axis)):
            peers.append(lambda axis=axis, offset=offset: {axis: turned(axis, offset)})
    return peers


SWAP_PEERS = [
    lambda: {CORE: other(CORE)},
    lambda: {ZH: other(ZH)},
    lambda: {CORE: other(CORE), ZH: other(ZH)},
]


class SwapIn(Errand):
    def __init__(self, shard):
        super().__init__()
        self.take(shard)
        self.give((lax.axis_size(PY), lax.axis_size(PX), 2) + shard.shape)
        self.peers = SWAP_PEERS
        self.reserve(2, 1)

    def plan(self, ins, outs):
        core, half = lax.axis_index(CORE), lax.axis_index(ZH)
        home = outs[0].at[lax.axis_index(PY), lax.axis_index(PX)]
        crossed = jnp.where(core == 0, 1 - half, half)
        return [
            [
                (ins[0], home.at[core], home.at[1 - core], {CORE: 1 - core, ZH: crossed}, None),
                (ins[0], home.at[1], home.at[1], {ZH: 1 - half}, core == 1),
            ]
        ]

    def local(self, ins, outs):
        home = outs[0].at[lax.axis_index(PY), lax.axis_index(PX)]
        return [(ins[0], home.at[0], lax.axis_index(CORE) == 0)]


class Spread(Errand):
    def __init__(self, rows, stages):
        super().__init__()
        self.stages = stages
        self.give(rows.shape, rows.dtype, pltpu.HBM, self.take(rows))
        self.peers = plane_peers()
        ny, nx = rows.shape[:2]
        straight, relayed = nx + ny - 2, 2 * (nx - 1) * (ny - 1)
        self.reserve(sum(relayed if stage == RELAY else straight for stage in stages))

    def plan(self, ins, outs):
        rows = outs[0]
        ny, nx = rows.shape[:2]
        first, then = [], []
        own = {PY: lax.axis_index(PY), PX: lax.axis_index(PX)}
        sides = [(PX, nx), (PY, ny)]

        def along(moves, axis, offset, at, core):
            land = dict(at)
            land[axis] = turned(axis, -offset)
            here = rows.at[at[PY], at[PX], core]
            there = rows.at[land[PY], land[PX], core]
            moves.append((here, here, there, {axis: turned(axis, offset)}, None))

        for stage in self.stages:
            if stage == RELAY:
                for e in range(1, nx):
                    for offset in range(1, ny):
                        along(then, PY, offset, {**own, PX: turned(PX, e)}, 0)
                for e in range(1, ny):
                    for offset in range(1, nx):
                        along(then, PX, offset, {**own, PY: turned(PY, e)}, 1)
            else:
                for core, (axis, size) in enumerate(sides if stage == STRAIGHT else sides[::-1]):
                    for offset in range(1, size):
                        along(first, axis, offset, own, core)
        if STRAIGHT in self.stages:
            return [first, then] if then else [first]
        return [first + then]


class FoldFar(Errand):
    def __init__(self, grad):
        super().__init__()
        self.take(grad)
        ny, nx, _, rows, columns = grad.shape
        self.give((ny - 1, nx - 1, rows, columns))
        self.give((nx - 1, ny - 1, rows, columns))
        self.peers = plane_peers()
        self.reserve(2 * (nx - 1) * (ny - 1))

    def plan(self, ins, outs):
        grad = ins[0]
        ny, nx = grad.shape[:2]
        moves = []
        for e in range(1, nx):
            for d in range(1, ny):
                slot = outs[0].at[d - 1, e - 1]
                to = turned(PY, d)
                moves.append((grad.at[to, turned(PX, e), 0], slot, slot, {PY: to}, None))
        for e in range(1, ny):
            for d in range(1, nx):
                slot = outs[1].at[d - 1, e - 1]
                to = turned(PX, d)
                moves.append((grad.at[turned(PY, e), to, 1], slot, slot, {PX: to}, None))
        return [moves]


class FoldNear(Errand):
    def __init__(self, grad):
        super().__init__()
        self.take(grad)
        ny, nx, _, rows, columns = grad.shape
        self.give((ny - 1, rows, columns))
        self.give((nx - 1, rows, columns))
        self.peers = plane_peers()
        self.reserve(nx + ny - 2)

    def plan(self, ins, outs):
        grad = ins[0]
        ny, nx = grad.shape[:2]
        y, x = lax.axis_index(PY), lax.axis_index(PX)
        moves = []
        for d in range(1, ny):
            to, slot = turned(PY, d), outs[0].at[d - 1]
            moves.append((grad.at[to, x, 0], slot, slot, {PY: to}, None))
        for d in range(1, nx):
            to, slot = turned(PX, d), outs[1].at[d - 1]
            moves.append((grad.at[y, to, 1], slot, slot, {PX: to}, None))
        return [moves]


class FoldRelay(Errand):
    def __init__(self, sums):
        super().__init__()
        for each in sums:
            self.take(each)
            self.give(each.shape)
        self.peers = plane_peers()
        self.reserve(sums[0].shape[0] + sums[1].shape[0])

    def plan(self, ins, outs):
        moves = []
        for i, axis in enumerate((PX, PY)):
            for e in range(1, lax.axis_size(axis)):
                slot = outs[i].at[e - 1]
                moves.append((ins[i].at[e - 1], slot, slot, {axis: turned(axis, e)}, None))
        return [moves]


class SwapOut(Errand):
    def __init__(self, pair):
        super().__init__()
        self.take(pair)
        self.give(pair.shape)
        self.peers = SWAP_PEERS
        self.reserve(2, 1)

    def plan(self, ins, outs):
        core, half = lax.axis_index(CORE), lax.axis_index(ZH)
        crossed = jnp.where(core == 0, half, 1 - half)
        pair, met = ins[0], outs[0]
        return [
            [
                (pair.at[1 - core], met.at[0], met.at[0], {CORE: 1 - core, ZH: crossed}, None),
                (pair.at[1], met.at[1], met.at[1], {ZH: 1 - half}, core == 1),
            ]
        ]

    def local(self, ins, outs):
        return [(ins[0].at[0], outs[0].at[1], lax.axis_index(CORE) == 0)]


def take_counts(refs, sizes):
    taken, rest = [], list(refs)
    for size in sizes:
        taken.append(rest[:size])
        rest = rest[size:]
    return taken, rest


def kernel(parts, *refs):
    ins, refs = take_counts(refs, [len(part.arrays) for part in parts])
    outs, refs = take_counts(refs, [len(part.shapes) for part in parts])
    scratch, _ = take_counts(refs, [len(part.scratch) for part in parts])
    barrier = pltpu.get_barrier_semaphore()
    greeted = sum(part.greet(barrier) for part in parts)
    pl.semaphore_wait(barrier, greeted)

    def errands(step):
        for i in range(1, len(parts)):
            parts[i].go(step, ins[i], outs[i], scratch[i])

    errands(0)
    parts[0].begin(ins[0], outs[0], scratch[0], partial(errands, 1))
    errands(2)


def travel(collective_id, *parts):
    aliases, first_in, first_out = {}, 0, 0
    for part in parts:
        for source, result in part.aliases.items():
            aliases[first_in + source] = first_out + result
        first_in += len(part.arrays)
        first_out += len(part.shapes)
    results = pl.pallas_call(
        partial(kernel, parts),
        out_shape=[shape for part in parts for shape in part.shapes],
        in_specs=[pl.BlockSpec(memory_space=space) for part in parts for space in part.in_spaces],
        out_specs=[pl.BlockSpec(memory_space=space) for part in parts for space in part.out_spaces],
        scratch_shapes=[each for part in parts for each in part.scratch],
        input_output_aliases=aliases,
        compiler_params=pltpu.CompilerParams(
            collective_id=collective_id, has_side_effects=True, vmem_limit_bytes=24 * 2**20
        ),
        cost_estimate=pl.CostEstimate(flops=2 * 10**10, bytes_accessed=1024, transcendentals=0),
    )(*[array for part in parts for array in part.arrays])
    split, _ = take_counts(results, [len(part.shapes) for part in parts])
    return split


class Route:
    def __init__(self, shards, errands):
        self.shards = shards
        self.errands = iter(errands)
        self.rows, self.grads, self.got = {}, {}, {FAR: {}, NEAR: {}, PASS: {}, LEAVE: {}}
        self.count = 0

    def step(self, main):
        errands, parts = next(self.errands), [main]
        for name, what in errands:
            if what == (ENTER,):
                parts.append(SwapIn(self.shards[name]))
            elif what == (FAR,):
                parts.append(FoldFar(self.grads[name]))
            elif what == (NEAR,):
                parts.append(FoldNear(self.grads[name]))
            elif what == (PASS,):
                parts.append(FoldRelay(self.far_sums(name)))
            elif what == (LEAVE,):
                parts.append(SwapOut(self.pair(name)))
            else:
                parts.append(Spread(self.rows[name], what))
        results = travel(self.count, *parts)
        self.count += 1
        for (name, what), got in zip(errands, results[1:]):
            if what[0] in self.got:
                self.got[what[0]][name] = got
            else:
                self.rows[name] = got[0]
        return results[0]

    def weight(self, kind, block):
        rows = self.rows[kind, block]
        return rows.reshape(-1, rows.shape[-1])

    def give_grad(self, kind, block, grad):
        name = (kind, block)
        self.grads[name] = grad.astype(jnp.bfloat16).reshape(self.rows[name].shape)

    def own_rows(self, name, py, px, core):
        grad = self.grads[name]
        at = lax.dynamic_slice(grad, (py, px, core, 0, 0), (1, 1, 1) + grad.shape[3:])
        return at[0, 0, 0].astype(jnp.float32)

    def far_sums(self, name):
        y, x = lax.axis_index(PY), lax.axis_index(PX)
        along_y, along_x = self.got[FAR][name]
        first = [
            self.own_rows(name, y, turned(PX, e), 0)
            + jnp.sum(along_y[:, e - 1].astype(jnp.float32), 0)
            for e in range(1, lax.axis_size(PX))
        ]
        last = [
            self.own_rows(name, turned(PY, e), x, 1)
            + jnp.sum(along_x[:, e - 1].astype(jnp.float32), 0)
            for e in range(1, lax.axis_size(PY))
        ]
        return jnp.stack(first).astype(jnp.bfloat16), jnp.stack(last).astype(jnp.bfloat16)

    def pair(self, name):
        y, x = lax.axis_index(PY), lax.axis_index(PX)
        halves = []
        for core in range(2):
            near = jnp.sum(self.got[NEAR][name][core].astype(jnp.float32), 0)
            relayed = jnp.sum(self.got[PASS][name][core].astype(jnp.float32), 0)
            halves.append(self.own_rows(name, y, x, core) + near + relayed)
        return jnp.stack(halves).astype(jnp.bfloat16)

    def met(self, kind, block):
        return self.got[LEAVE][kind, block][0]


ROWS_BY_ROWS = (((1,), (1,)), ((), ()))
COLUMNS_BY_COLUMNS = (((0,), (0,)), ((), ()))


def head_of(array, which, head, local):
    first = which * local + head * HEAD_DIM
    return array[0, :, first : first + HEAD_DIM]


def soft(query, key, valid):
    scores = lax.dot_general(query, key, ROWS_BY_ROWS, preferred_element_type=jnp.float32)
    scores = jnp.where(valid > 0, scores * (1.0 / math.sqrt(HEAD_DIM)), -1e30)
    expo = jnp.exp(scores - jnp.max(scores, -1, keepdims=True))
    return expo / jnp.sum(expo, -1, keepdims=True)


def attend_kernel(normed, valid, weight_in, weight_out, triple, context, terms):
    local = context.shape[2]
    triple[0] = jnp.dot(normed[0], weight_in[...], preferred_element_type=jnp.float32).astype(
        jnp.bfloat16
    )
    parts = []
    for head in range(local // HEAD_DIM):
        query, key, value = [head_of(triple, which, head, local) for which in range(3)]
        probs = soft(query, key, valid[0]).astype(jnp.bfloat16)
        parts.append(jnp.dot(probs, value, preferred_element_type=jnp.float32))
    flat = jnp.concatenate(parts, 1).astype(jnp.bfloat16)
    context[0] = flat
    terms[0] = lax.dot_general(
        flat, weight_out[...], ROWS_BY_ROWS, preferred_element_type=jnp.float32
    ).astype(jnp.bfloat16)


def attend_back_kernel(
    triple, valid, grad_attn, weight_in, weight_out, grad_triple, terms, grad_context
):
    local = weight_out.shape[1]
    scale = 1.0 / math.sqrt(HEAD_DIM)
    grad_context[0] = jnp.dot(
        grad_attn[0], weight_out[...], preferred_element_type=jnp.float32
    ).astype(jnp.bfloat16)
    queries, keys, values = [], [], []
    for head in range(local // HEAD_DIM):
        query, key, value = [head_of(triple, which, head, local) for which in range(3)]
        grad = head_of(grad_context, 0, head, local)
        probs = soft(query, key, valid[0])
        values.append(
            lax.dot_general(
                probs.astype(jnp.bfloat16),
                grad,
                COLUMNS_BY_COLUMNS,
                preferred_element_type=jnp.float32,
            )
        )
        grad_probs = lax.dot_general(
            grad, value, ROWS_BY_ROWS, preferred_element_type=jnp.float32
        )
        tilt = jnp.sum(grad_probs * probs, -1, keepdims=True)
        grad_scores = (probs * (grad_probs - tilt)).astype(jnp.bfloat16)
        queries.append(jnp.dot(grad_scores, key, preferred_element_type=jnp.float32) * scale)
        keys.append(
            lax.dot_general(
                grad_scores, query, COLUMNS_BY_COLUMNS, preferred_element_type=jnp.float32
            )
            * scale
        )
    fresh = jnp.concatenate(queries + keys + values, 1).astype(jnp.bfloat16)
    grad_triple[0] = fresh
    terms[0] = lax.dot_general(
        fresh, weight_in[...], ROWS_BY_ROWS, preferred_element_type=jnp.float32
    ).astype(jnp.bfloat16)


def by_image(body, arrays, weights, columns, scratch=()):
    images, length = arrays[0].shape[:2]

    def block(array):
        return pl.BlockSpec((1,) + array.shape[1:], lambda i: (i, 0, 0))

    made = [jax.ShapeDtypeStruct((images, length, each), jnp.bfloat16) for each in columns]
    return pl.pallas_call(
        body,
        grid=(images,),
        out_shape=made,
        in_specs=[block(array) for array in arrays]
        + [pl.BlockSpec(weight.shape, lambda i: (0, 0)) for weight in weights],
        out_specs=[block(each) for each in made],
        scratch_shapes=[pltpu.VMEM((1, length, each), jnp.bfloat16) for each in scratch],
        compiler_params=pltpu.CompilerParams(vmem_limit_bytes=24 * 2**20),
        cost_estimate=pl.CostEstimate(flops=5 * 10**9, bytes_accessed=1024, transcendentals=0),
    )(*arrays, *weights)


def low_dot(spec, left, right):
    return jnp.einsum(spec, left, right, preferred_element_type=jnp.float32)


def attend(normed, key_valid, block, route):
    weights = [route.weight(IN, block), route.weight(OUT, block)]
    width, local = weights[1].shape
    triple, flat_context, terms = by_image(
        attend_kernel, [normed, key_valid], weights, (3 * local, local, width)
    )
    return terms, (triple, flat_context)


def feed(normed, block, route):
    inner = low_dot("bld,df->blf", normed, route.weight(EXPAND, block))
    active = jax.nn.gelu(inner, approximate=True).astype(jnp.bfloat16)
    terms = low_dot("blf,df->bld", active, route.weight(CONTRACT, block)).astype(jnp.bfloat16)
    return terms, (inner, active)


def feed_back(grad_branch, normed, saved, block, route):
    inner, active = saved
    grad_active = low_dot("bld,df->blf", grad_branch, route.weight(CONTRACT, block))
    gelu_back = jax.vjp(partial(jax.nn.gelu, approximate=True), inner)[1]
    grad_inner = gelu_back(grad_active)[0].astype(jnp.bfloat16)
    terms = low_dot("blf,df->bld", grad_inner, route.weight(EXPAND, block)).astype(jnp.bfloat16)
    route.give_grad(CONTRACT, block, low_dot("bld,blf->df", grad_branch, active))
    route.give_grad(EXPAND, block, low_dot("bld,blf->df", normed, grad_inner))
    return terms


def attend_back(grad_attn, normed, saved, key_valid, block, route):
    triple, flat_context = saved
    weights = [route.weight(IN, block), route.weight(OUT, block)]
    width, local = weights[1].shape
    grad_triple, terms = by_image(
        attend_back_kernel,
        [triple, key_valid, grad_attn],
        weights,
        (3 * local, width),
        (local,),
    )
    return terms, (normed, grad_triple, grad_attn, flat_context)


def errands_in_turn():
    def attend(block, *what):
        return [((IN, block), what), ((OUT, block), what)]

    def expand(block, *what):
        return [((EXPAND, block), what)]

    def contract(block, *what):
        return [((CONTRACT, block), what)]

    def feed(block, *what):
        return expand(block, *what) + contract(block, *what)

    return [
        attend(0, ENTER),
        attend(0, STRAIGHT) + expand(0, ENTER),
        attend(0, CROSS, RELAY) + contract(0, ENTER) + expand(0, STRAIGHT),
        expand(0, CROSS, RELAY) + contract(0, STRAIGHT) + attend(1, ENTER),
        contract(0, CROSS, RELAY) + attend(1, STRAIGHT) + expand(1, ENTER),
        attend(1, CROSS, RELAY) + expand(1, STRAIGHT, CROSS) + contract(1, ENTER),
        contract(1, STRAIGHT, CROSS, RELAY) + expand(1, RELAY),
        [],
        feed(1, FAR) + feed(1, NEAR),
        feed(1, PASS),
        feed(0, FAR) + attend(1, FAR) + attend(1, NEAR) + expand(1, LEAVE),
        contract(0, NEAR) + feed(0, PASS) + attend(1, PASS) + contract(1, LEAVE),
        attend(0, FAR) + expand(0, NEAR) + contract(0, LEAVE) + attend(1, LEAVE),
        attend(0, NEAR) + attend(0, PASS) + expand(0, LEAVE),
        attend(0, LEAVE),
        [],
    ]


def adam(weight, grad, moment, second, average, factor):
    grad = grad * factor
    moment = beta_first * moment + (1.0 - beta_first) * grad
    second = beta_second * second + (1.0 - beta_second) * grad * grad
    update = (
        moment
        / (1.0 - beta_first**STEP)
        / (jnp.sqrt(second / (1.0 - beta_second**STEP)) + adam_eps)
    )
    fresh = weight - learn_rate * (update + weight_decay * weight)
    average_decay = min(ema_decay, (1.0 + STEP) / (10.0 + STEP))
    average = average_decay * average + (1.0 - average_decay) * fresh
    return (fresh, moment, second, average)


def shards(
    patches,
    target_noise,
    kept_slots,
    kept_count,
    time_step,
    labels,
    teacher,
    *tables,
):
    params, moments, seconds, averages = tables[:7], tables[7:14], tables[14:21], tables[21:]
    attend_in, attend_out, expand, contract, modulation, patch_table, condition = params
    batch, length = (patches.shape[0], patches.shape[1])
    capacity = kept_slots.shape[1]
    rows, local = (attend_in.shape[1], attend_in.shape[3])
    wides, narrows = (group_size(WIDE), group_size(NARROW))
    wide_index, narrow_index = (flat_place(WIDE), flat_place(NARROW))
    images = batch * wides
    width = local * narrows
    assert batch == narrows

    shards_low = {}
    for i in range(2):
        shards_low[IN, i] = attend_in[i].reshape(rows, 3 * local).astype(jnp.bfloat16)
        shards_low[OUT, i] = attend_out[i].T.astype(jnp.bfloat16)
        shards_low[EXPAND, i] = expand[i].astype(jnp.bfloat16)
        shards_low[CONTRACT, i] = contract[i].T.astype(jnp.bfloat16)
    route = Route(shards_low, errands_in_turn())

    def own(array):
        return lax.dynamic_index_in_dim(array, narrow_index, 0, keepdims=False)

    condition_low = condition.astype(jnp.bfloat16)
    features = sinusoid(time_step, FREQ)
    onehot = (labels[:, None] == jnp.arange(CLASSES)[None, :]).astype(jnp.bfloat16)
    cond_part = jnp.dot(
        features, condition_low[:FREQ].astype(jnp.float32), precision=highest_float_accuracy
    ) + low_dot("bc,cd->bd", onehot, condition_low[FREQ:])
    pieces = jax.nn.silu(cond_part).reshape(batch, local // rows, rows)
    pieces = jnp.pad(jnp.transpose(pieces, (1, 0, 2)), ((0, 0), (0, 8 - batch), (0, 0)))
    (silu_wide,) = route.step(RowPieces(pieces))
    silu_rows = silu_wide[:, :batch].reshape(images, rows).astype(jnp.bfloat16)
    modulation_low = modulation.astype(jnp.bfloat16)
    mod_part = low_dot("ip,npkc->inkc", silu_rows, modulation_low)
    mod_part = mod_part.reshape(wides, batch, 12 * local)
    (mod_wide,) = route.step(Exchange([mod_part], [(WIDE, EACH)]))
    facts = jnp.stack([kept_count, time_step, labels], 1).astype(jnp.float32)
    facts = jnp.pad(facts, ((0, 4), (0, local - 3)))
    teacher_rows = teacher.reshape(batch * narrows, local)
    payload = jnp.concatenate([cond_part, facts[:batch], teacher_rows], 0)
    table_pad = jnp.pad(patch_table.astype(jnp.bfloat16), ((0, 15), (0, 0)))
    mod_near, everyone, tables_near = route.step(
        Exchange(
            [jnp.sum(mod_wide, 0).reshape(batch, 12, local), payload, table_pad],
            [(NARROW, EACH), (WIDE, SAME), (NARROW, SAME)],
        )
    )
    mods = jnp.transpose(mod_near, (1, 0, 2)).reshape(12, width)
    mod_enc, mod_dec = mods[:6], mods[6:]
    cond_cols = everyone[:, :batch].reshape(images, local)
    facts_all = everyone[:, batch : 2 * batch, :3]
    negatives = everyone[:, 2 * batch :].reshape(images, width)
    time_all = facts_all[:, :, 1].reshape(images).astype(jnp.int32)
    labels_all = facts_all[:, :, 2].reshape(images).astype(jnp.int32)
    patch_full = jnp.transpose(tables_near, (1, 0, 2)).reshape(48, width)

    count_own = own(kept_count).astype(jnp.float32)
    slot_valid = (jnp.arange(capacity) < own(kept_count)).astype(jnp.float32)[:, None]
    select = (own(kept_slots)[:, None] == jnp.arange(length)[None, :]).astype(
        jnp.float32
    ) * slot_valid
    open_place = 1.0 - jnp.sum(select, 0)[:, None]
    places = sinusoid(jnp.arange(length), width)
    group_counts = lax.dynamic_slice(
        facts_all[:, :, 0],
        (flat_place((PY, PX)) * 2, lax.axis_index(ZH) * 2),
        (2, 2),
    ).reshape(4)
    group_valid = (jnp.arange(capacity)[None, None, :] < group_counts[:, None, None]).astype(
        jnp.float32
    )
    all_valid = jnp.ones((4, 1, length), jnp.float32)
    kept_patches = low_dot("cl,lp->cp", select.astype(jnp.bfloat16), own(patches))
    embed = low_dot("cp,pd->cd", kept_patches.astype(jnp.bfloat16), patch_full[:PATCH_IN])
    embed = embed + jnp.dot(select, places, precision=highest_float_accuracy)
    mask_token = patch_full[2 * PATCH_IN : 2 * PATCH_IN + 1].astype(jnp.float32)
    base = open_place * mask_token + places
    head = patch_full[PATCH_IN : 2 * PATCH_IN]
    count_all = images * length * PATCH_IN

    (normed_a0,) = route.step(Enter(embed, mod_enc))
    terms, saved_a0 = attend(normed_a0, group_valid, 0, route)
    normed_m0, attn0, middle0 = route.step(Middle(terms, embed, mod_enc))
    terms, saved_m0 = feed(normed_m0, 0, route)
    positive = ((wide_index * batch + narrow_index) == jnp.arange(images)).astype(jnp.float32)
    contrast = (slot_valid, count_own.reshape(1, 1), negatives, positive[:, None])
    normed_a1, branch0, _, decode_in, grad_pool, nce = route.step(
        Decode(terms, middle0, mod_enc, mod_dec, select.T, base, contrast)
    )
    terms, saved_a1 = attend(normed_a1, all_valid, 1, route)
    normed_m1, attn1, middle1 = route.step(Middle(terms, decode_in, mod_dec))
    terms, saved_m1 = feed(normed_m1, 1, route)
    grad_branch, grad_decoded, gate_m1, grad_head, square = route.step(
        Turn(terms, middle1, mod_dec, head, own(target_noise), count_all)
    )

    terms = feed_back(grad_branch, normed_m1, saved_m1, 1, route)
    grad_attn, grad_mid, sums_m1 = route.step(
        MiddleBack(terms, middle1, attn1, grad_decoded, mod_dec)
    )
    terms, pairs = attend_back(grad_attn, normed_a1, saved_a1, all_valid, 1, route)
    back_to = (open_place, select, slot_valid, grad_pool, branch0, mod_enc)
    grad_branch, grad_encoded, sums_a1, grad_in, grad_out = route.step(
        Encode(terms, decode_in, grad_mid, mod_dec, back_to, pairs)
    )
    route.give_grad(IN, 1, grad_in)
    route.give_grad(OUT, 1, grad_out)
    terms = feed_back(grad_branch, normed_m0, saved_m0, 0, route)
    grad_attn, grad_mid, sums_m0 = route.step(
        MiddleBack(terms, middle0, attn0, grad_encoded, mod_enc)
    )
    terms, pairs = attend_back(grad_attn, normed_a0, saved_a0, group_valid, 0, route)
    sums = (sums_m0, sums_a1, sums_m1, gate_m1, grad_head)
    rows_near, grad_in, grad_out = route.step(
        Leave(terms, embed, grad_mid, mod_enc, kept_patches, sums, pairs)
    )
    route.give_grad(IN, 0, grad_in)
    route.give_grad(OUT, 0, grad_out)

    mods_near = rows_near[:, :12].reshape(narrows, 12 * local)
    table_near = rows_near[:, 12:45]
    table_sum = jnp.pad(jnp.sum(table_near, 0), ((0, 15), (0, 0))).astype(jnp.bfloat16)
    mods_all, table_all = route.step(
        Exchange([mods_near, table_sum], [(WIDE, SAME), (WIDE, SAME)])
    )
    grad_patch_table = jnp.sum(table_all.astype(jnp.float32), 0)[:33]
    mods_all = mods_all.reshape(images, 2, 6, local)
    silu_broad = silu_rows.astype(jnp.float32)
    grad_modulation = jnp.einsum(
        "ip,inkc->npkc", silu_broad, mods_all, precision=highest_float_accuracy
    )
    grad_silu = jnp.einsum(
        "inkc,npkc->ip",
        mods_all,
        modulation_low.astype(jnp.float32),
        precision=highest_float_accuracy,
    )
    (silu_near,) = route.step(Exchange([grad_silu], [(NARROW, SAME)]))
    (silu_wide,) = route.step(Exchange([jnp.sum(silu_near, 0)], [(WIDE, SAME)]))
    grad_silu = jnp.transpose(silu_wide, (1, 0, 2)).reshape(images, width)
    grad_silu = lax.dynamic_slice_in_dim(grad_silu, narrow_index * local, local, 1)
    grad_cond = jax.vjp(jax.nn.silu, cond_cols)[1](grad_silu)[0]
    features_all = sinusoid(time_all, FREQ)
    onehot_all = (labels_all[:, None] == jnp.arange(CLASSES)[None, :]).astype(jnp.float32)
    grad_condition = jnp.dot(
        jnp.concatenate([features_all, onehot_all], 1).T, grad_cond, precision=highest_float_accuracy
    )


    def totals(kind, shape):
        both = [route.met(kind, i).astype(jnp.float32) for i in range(2)]
        return jnp.stack([shape(each[0] + each[1]) for each in both])

    def by_third(g):
        thirds = [g[:, i * local : (i + 1) * local] for i in range(3)]
        return jnp.transpose(jnp.stack(thirds), (1, 0, 2))

    grads = [
        totals(IN, by_third),
        totals(OUT, lambda g: g.T),
        totals(EXPAND, lambda g: g),
        totals(CONTRACT, lambda g: g.T),
        grad_modulation,
        grad_patch_table,
        grad_condition,
    ]
    square_small = jnp.sum(grad_patch_table * grad_patch_table) + jnp.sum(
        grad_condition * grad_condition
    )
    square_local = jnp.sum(grad_modulation * grad_modulation)
    square_local = square_local + (wide_index == 0).astype(jnp.float32) * square_small
    scalars = jnp.stack([square[0, 0], nce[0, 0], square_local])
    scalars = jnp.pad(scalars[None, :], ((0, 7), (0, 125)))
    mets = [route.met(kind, i) for i in range(2) for kind in (IN, OUT, EXPAND, CONTRACT)]
    (scalars_all,) = route.step(Norm(scalars, mets))
    sums = jnp.sum(scalars_all[:, 0], 0)
    grad_norm = jnp.sqrt(sums[2])
    factor = clip_norm / jnp.maximum(grad_norm, clip_norm)
    fresh = [
        adam(params[i], grads[i], moments[i], seconds[i], averages[i], factor) for i in range(7)
    ]
    loss_parts = jnp.stack([sums[0] / count_all, sums[1] / images])
    return (loss_parts, grad_norm) + tuple(fresh[i][k] for k in range(4) for i in range(7))


def solution(mesh):
    wide, narrow = mesh.devices.shape
    planes = wide // 2
    across = max(n for n in range(1, math.isqrt(planes) + 1) if planes % n == 0)
    grid = Mesh(mesh.devices.reshape(across, planes // across, 2, narrow // 2, 2), ALL)
    image_specs = (
        P(WIDE, None, None),
        P(WIDE, None, None),
        P(WIDE, None),
        P(WIDE),
        P(WIDE),
        P(WIDE),
        P(WIDE, None),
    )
    table_specs = (
        P(None, WIDE, None, NARROW),
        P(None, NARROW, WIDE),
        P(None, WIDE, NARROW),
        P(None, NARROW, WIDE),
        P(None, WIDE, None, NARROW),
        P(None, NARROW),
        P(None, NARROW),
    )
    return jax.shard_map(
        shards,
        mesh=grid,
        in_specs=image_specs + table_specs * 4,
        out_specs=(P(), P()) + table_specs * 4,
        check_vma=False,
    )
```

```python
from functools import partial
import math

import jax
import jax.numpy as jnp
from jax import lax
from jax.experimental import pallas as pl
from jax.experimental.pallas import tpu as pltpu
from jax.sharding import Mesh
from jax.sharding import PartitionSpec as P

HEAD_DIM = 72
CLASSES = 1000
FREQ = 256
PATCH_IN = 16
STEP = 10

MESH = pl.DeviceIdType.MESH
PY, PX, CORE, ZH, ZL = "py", "px", "core", "zh", "zl"
WIDE = (PY, PX, CORE)
NARROW = (ZH, ZL)
ALL = WIDE + NARROW
EACH, SAME = range(2)
IN, OUT, EXPAND, CONTRACT = range(4)
TERM_SQUARE, TERM_HEAD, TERM_GATE, TERM_SHIFT, TERM_SCALE, TERM_MASK, TERM_PATCH = range(7)
ENTER, STRAIGHT, CROSS, RELAY, FAR, NEAR, PASS, LEAVE = range(8)

highest_float_accuracy = lax.Precision.HIGHEST
norm_eps = 1e-06
contrast_sharpness_divisor = 0.02
nce_weight = 0.5
learn_rate = 0.05
beta_first = 0.9
beta_second = 0.999
adam_eps = 1e-08
weight_decay = 0.05
clip_norm = 0.05
ema_decay = 0.9999


def layer_norm(values):
    center = values - jnp.mean(values, -1, keepdims=True)
    return center * lax.rsqrt(jnp.mean(center * center, -1, keepdims=True) + norm_eps)


def modulate(values, shift, scale):
    return layer_norm(values) * (1.0 + scale[None, :]) + shift[None, :]


def sinusoid(places, width):
    half = width // 2
    freqs = jnp.exp(-math.log(10000.0) * jnp.arange(half, dtype=jnp.float32) / half)
    angle = places.astype(jnp.float32)[:, None] * freqs[None, :]
    return jnp.concatenate([jnp.cos(angle), jnp.sin(angle)], -1)


def flat_place(axes):
    place = 0
    for axis in axes:
        place = place * lax.axis_size(axis) + lax.axis_index(axis)
    return place


def group_size(axes):
    size = 1
    for axis in axes:
        size = size * lax.axis_size(axis)
    return size


def device_at(axes, place):
    where = {}
    for axis in reversed(axes):
        where[axis] = lax.rem(place, lax.axis_size(axis))
        place = place // lax.axis_size(axis)
    return where


def turned(axis, offset):
    size = lax.axis_size(axis)
    return lax.rem(lax.axis_index(axis) + (offset % size), size)


def other(axis):
    return 1 - lax.axis_index(axis)


class Part:
    def __init__(self):
        self.arrays, self.in_spaces = [], []
        self.shapes, self.out_spaces = [], []
        self.aliases = {}
        self.scratch = []
        self.peers = []

    def take(self, array, space=pltpu.HBM):
        self.arrays.append(array)
        self.in_spaces.append(space)
        return len(self.arrays) - 1

    def give(self, shape, dtype=jnp.bfloat16, space=pltpu.HBM, source=None):
        held = pltpu.HBM if space == pltpu.HBM else jax.ShapeDtypeStruct
        self.shapes.append(held(shape, dtype))
        self.out_spaces.append(space)
        if source is not None:
            self.aliases[source] = len(self.shapes) - 1
        return len(self.shapes) - 1

    def greet(self, barrier):
        for peer in self.peers:
            pl.semaphore_signal(barrier, inc=1, device_id=peer(), device_id_type=MESH)
        return len(self.peers)

    def begin(self, ins, outs, scratch, halfway):
        pass

    def go(self, step, ins, outs, scratch):
        pass


class Exchange(Part):
    def __init__(self, arrays, specs):
        super().__init__()
        self.specs = specs
        for array, (axes, mode) in zip(arrays, specs):
            size = group_size(axes)
            piece = array.shape[1:] if mode == EACH else array.shape
            self.take(array, pltpu.VMEM)
            self.give((size,) + piece, array.dtype, pltpu.VMEM)
            self.scratch += [pltpu.SemaphoreType.DMA((size,)), pltpu.SemaphoreType.DMA((size,))]

    def greet(self, barrier):
        greeted = 0
        for axes, _ in self.specs:
            size, me = group_size(axes), flat_place(axes)
            greeted += size - 1

            def signal(offset, carry, axes=axes, size=size, me=me):
                target = lax.rem(me + offset, size)
                pl.semaphore_signal(
                    barrier, inc=1, device_id=device_at(axes, target), device_id_type=MESH
                )
                return carry

            lax.fori_loop(1, size, signal, 0)
        return greeted

    def begin(self, ins, outs, scratch, halfway):
        def copy_to(index, offset, arriving):
            axes, mode = self.specs[index]
            size, me = group_size(axes), flat_place(axes)
            target = lax.rem(me + offset, size)
            return pltpu.make_async_remote_copy(
                src_ref=ins[index].at[target] if mode == EACH else ins[index],
                dst_ref=outs[index].at[target if arriving else me],
                send_sem=scratch[2 * index].at[target],
                recv_sem=scratch[2 * index + 1].at[target if arriving else me],
                device_id=device_at(axes, target),
                device_id_type=MESH,
            )

        for index, (axes, mode) in enumerate(self.specs):

            def start(offset, carry, index=index):
                copy_to(index, offset, False).start()
                return carry

            lax.fori_loop(1, group_size(axes), start, 0)
        for index, (axes, mode) in enumerate(self.specs):
            me = flat_place(axes)
            outs[index][me] = ins[index][me] if mode == EACH else ins[index][...]
        for index, (axes, mode) in enumerate(self.specs):

            def end(offset, carry, index=index):
                copy_to(index, offset, True).wait_recv()
                copy_to(index, offset, False).wait_send()
                return carry

            lax.fori_loop(1, group_size(axes), end, 0)
        halfway()


class Norm(Exchange):
    def __init__(self, scalars, mets):
        super().__init__([scalars], [(ALL, SAME)])
        for met in mets:
            self.take(met, pltpu.VMEM)
        self.scratch.append(pltpu.VMEM(scalars.shape, jnp.float32))

    def begin(self, ins, outs, scratch, halfway):
        square = jnp.zeros((8, 128), jnp.float32)
        for met in ins[1:]:
            total = met[0].astype(jnp.float32) + met[1].astype(jnp.float32)
            columns = total.shape[1]
            squares = total * total
            if squares.shape[0] % 8:
                squares = jnp.pad(fold(squares), ((0, 7), (0, 0)))
            eights = jnp.sum(squares.reshape(-1, 8, columns), 0)
            for start in range(0, columns, 128):
                lanes = eights[:, start : start + 128]
                if lanes.shape[1] < 128:
                    lanes = jnp.pad(lanes, ((0, 0), (0, 128 - lanes.shape[1])))
                square = square + lanes
        lane = lax.broadcasted_iota(jnp.int32, (8, 128), 1)
        scratch[2][...] = ins[0][...] + jnp.where(lane == 2, jnp.sum(square), 0.0)
        super().begin([scratch[2]], outs, scratch[:2], halfway)


class RowPieces(Part):
    def __init__(self, pieces):
        super().__init__()
        self.each = pieces.shape[0]
        wides, narrows = group_size(WIDE), group_size(NARROW)
        self.take(pieces, pltpu.VMEM)
        self.give((wides,) + pieces.shape[1:], pieces.dtype, pltpu.VMEM)
        self.scratch = [
            pltpu.SemaphoreType.DMA((self.each * narrows,)),
            pltpu.SemaphoreType.DMA((wides,)),
        ]

    def sends(self):
        narrows, me = group_size(NARROW), flat_place(WIDE) * group_size(NARROW) + flat_place(NARROW)
        for j in range(self.each):
            for z in range(narrows):
                wide = flat_place(NARROW) * self.each + j
                to = {**device_at(WIDE, wide), **device_at(NARROW, jnp.int32(z))}
                yield j, z, to, wide * narrows + z != me

    def receives(self):
        narrows, me = group_size(NARROW), flat_place(WIDE) * group_size(NARROW) + flat_place(NARROW)
        z = flat_place(WIDE) // self.each
        for w in range(group_size(WIDE)):
            to = {**device_at(WIDE, jnp.int32(w)), **device_at(NARROW, z)}
            yield w, to, w * narrows + z != me

    def greet(self, barrier):
        for _, _, to, remote in self.sends():

            @pl.when(remote)
            def _(to=to):
                pl.semaphore_signal(barrier, inc=1, device_id=to, device_id_type=MESH)

        for _, to, remote in self.receives():

            @pl.when(remote)
            def _(to=to):
                pl.semaphore_signal(barrier, inc=1, device_id=to, device_id_type=MESH)

        counts = [r.astype(jnp.int32) for _, _, _, r in self.sends()]
        counts += [r.astype(jnp.int32) for _, _, r in self.receives()]
        return sum(counts)

    def begin(self, ins, outs, scratch, halfway):
        me = flat_place(WIDE)
        z = flat_place(WIDE) // self.each
        narrows = group_size(NARROW)

        def copy(j, slot, sem, to):
            return pltpu.make_async_remote_copy(
                src_ref=ins[0].at[j],
                dst_ref=outs[0].at[slot],
                send_sem=scratch[0].at[sem],
                recv_sem=scratch[1].at[slot],
                device_id=to,
                device_id_type=MESH,
            )

        for j, t, to, remote in self.sends():

            @pl.when(remote)
            def _(j=j, t=t, to=to):
                copy(j, me, j * narrows + t, to).start()

            @pl.when(jnp.logical_not(remote))
            def _(j=j):
                outs[0][me] = ins[0][j]

        for w, to, remote in self.receives():

            @pl.when(remote)
            def _(w=w, to=to):
                copy(0, w, 0, to).wait_recv()

        for j, t, to, remote in self.sends():

            @pl.when(remote)
            def _(j=j, t=t, to=to):
                copy(j, me, j * narrows + t, to).wait_send()

        halfway()


def chunk_of(length):
    return 32 if length % 32 == 0 else 16


def normal(values):
    center = values - jnp.mean(values, -1, keepdims=True)
    scale = lax.rsqrt(jnp.mean(center * center, -1, keepdims=True) + norm_eps)
    return center * scale, scale


def normal_back(grad, unit, scale):
    flat = jnp.mean(grad, -1, keepdims=True)
    tilt = jnp.mean(grad * unit, -1, keepdims=True)
    return scale * (grad - flat - unit * tilt)


def fold(values):
    return jnp.sum(values, 0, keepdims=True)


def full_dot(left, right):
    return jnp.dot(
        left, right, precision=highest_float_accuracy, preferred_element_type=jnp.float32
    )


SHIFT_A, SCALE_A, GATE_A, SHIFT_M, SCALE_M, GATE_M = range(6)


class Bridge(Part):
    whole = False
    sends_on = True

    def __init__(self, terms, more, width, length_in, length_out):
        super().__init__()
        self.length_in, self.length_out, self.width = length_in, length_out, width
        self.sums = terms is not None
        self.first = 0
        if self.sums:
            self.take(terms, pltpu.VMEM)
            self.first = 1
        self.fetched = []
        for array in more:
            large = array.size * array.dtype.itemsize >= 2**18
            if large:
                array = pltpu.with_memory_space_constraint(array, pltpu.HBM)
            self.fetched.append(large)
            self.take(array, pltpu.HBM if large else pltpu.VMEM)
        if self.sends_on:
            self.give((4, length_out, width), jnp.bfloat16, pltpu.VMEM)
        self.peers = [lambda: {CORE: other(CORE)}, lambda: {ZL: other(ZL)}]
        self.scratch = [
            pltpu.VMEM(array.shape, array.dtype)
            for array, large in zip(more, self.fetched)
            if large
        ]
        self.scratch.append(pltpu.SemaphoreType.DMA((len(more),)))
        if self.sums:
            self.scratch += [pltpu.VMEM((length_in, width), jnp.bfloat16)] * 4
            self.scratch += self.sems(length_in)
        if self.sends_on:
            self.scratch += self.sems(length_out)

    def result(self, shape, dtype=jnp.float32):
        self.give(shape, dtype, pltpu.VMEM)

    def sems(self, length):
        steps = length // chunk_of(length)
        return [pltpu.SemaphoreType.DMA((3, steps)), pltpu.SemaphoreType.DMA((3, steps))]

    def ranks(self):
        core, low = lax.axis_index(CORE), lax.axis_index(ZL)
        return core * 2 + low, (1 - core) * 2 + low, core * 2 + 1 - low, (1 - core) * 2 + 1 - low

    def copy(self, source, target, sems, kind, step):
        return pltpu.make_async_remote_copy(
            src_ref=source,
            dst_ref=target,
            send_sem=sems[0].at[kind, step],
            recv_sem=sems[1].at[kind, step],
            device_id={ZL: other(ZL)} if kind == 0 else {CORE: other(CORE)},
            device_id_type=MESH,
        )

    def rows(self, length):
        chunk = chunk_of(length)
        return [pl.ds(s * chunk, chunk) for s in range(length // chunk)]

    def begin(self, ins, outs, scratch, halfway):
        me, mate, away, away_mate = self.ranks()
        given = list(ins[self.first :])
        made = outs[1:] if self.sends_on else outs
        fetches = []
        held, scratch = scratch[: sum(self.fetched)], scratch[sum(self.fetched) :]
        for i, large in enumerate(self.fetched):
            if large:
                place = held[len(fetches)]
                fetches.append(pltpu.make_async_copy(given[i], place, scratch[0].at[i]))
                fetches[-1].start()
                given[i] = place
        scratch = scratch[1:]
        state = self.start(given, made)
        sends = []
        rows_in, rows_out = self.rows(self.length_in), self.rows(self.length_out)
        if self.sums:
            terms = ins[0]
            near, home, stage, far = scratch[:4]
            sems = scratch[4:6]
            to_near = [
                self.copy(terms.at[away_mate, r], near.at[r], sems, 1, s)
                for s, r in enumerate(rows_in)
            ]
            to_home = [
                self.copy(terms.at[mate, r], home.at[r], sems, 2, s) for s, r in enumerate(rows_in)
            ]
            to_far = [self.copy(stage.at[r], far.at[r], sems, 0, s) for s, r in enumerate(rows_in)]
            for each in to_near:
                each.start()
            for each in to_home:
                each.start()
            for s, r in enumerate(rows_in):
                to_near[s].wait_recv()
                both = terms[away, r].astype(jnp.float32) + near[r].astype(jnp.float32)
                stage[r] = both.astype(jnp.bfloat16)
                to_far[s].start()
            sends += to_near + to_home + to_far

            def total(s, r):
                to_home[s].wait_recv()
                own = terms[me, r].astype(jnp.float32) + home[r].astype(jnp.float32)
                to_far[s].wait_recv()
                return own + far[r].astype(jnp.float32)

        else:

            def total(s, r):
                return None

        if self.sends_on:
            every = outs[0]
            sems_out = scratch[-2:]

            def move(kind, here, there, s, r):
                return self.copy(every.at[here, r], every.at[there, r], sems_out, kind, s)

            def pass_on(s, r, fresh):
                every[me, r] = fresh
                for kind in (0, 1):
                    each = move(kind, me, me, s, r)
                    each.start()
                    sends.append(each)

        for each in fetches:
            each.wait()
        if self.whole:
            for s, r in enumerate(rows_in):
                self.collect(r, total(s, r), given, made, state)
            self.turn(given, made, state)
            for s, r in enumerate(rows_out):
                pass_on(s, r, self.work(r, None, given, made, state))
        else:
            for s, r in enumerate(rows_in):
                fresh = self.work(r, total(s, r), given, made, state)
                if self.sends_on:
                    pass_on(s, r, fresh)
        self.end(given, made, state)
        self.aside(given, made)
        if self.sums:
            halfway()
        if self.sends_on:
            for s, r in enumerate(rows_out):
                move(0, me, away, s, r).wait_recv()
                each = move(2, away, away, s, r)
                each.start()
                sends.append(each)
            for s, r in enumerate(rows_out):
                move(1, me, mate, s, r).wait_recv()
                move(2, away, away_mate, s, r).wait_recv()
        for each in sends:
            each.wait_send()
        if not self.sums:
            halfway()

    def start(self, given, made):
        return {}

    def add(self, state, name, value):
        state[name] = value if name not in state else state[name] + value

    def end(self, given, made, state):
        pass

    def aside(self, given, made):
        pass


def outer(left, right, result):
    step = 384 if left.shape[2] % 384 == 0 else 128

    def tile(i, carry):
        columns = pl.ds(pl.multiple_of(i * step, step), step)
        value = lax.dot_general(
            left[:, :, columns].reshape(-1, step),
            right[...].reshape(-1, right.shape[2]),
            (((0,), (0,)), ((), ())),
            preferred_element_type=jnp.float32,
        )
        result[columns] = value.astype(jnp.bfloat16)
        return carry

    lax.fori_loop(0, left.shape[2] // step, tile, 0)


class Enter(Bridge):
    def __init__(self, values, mod):
        length, width = values.shape
        super().__init__(None, [values, mod], width, length, length)

    def work(self, r, total, given, made, state):
        values, mod = given
        unit, _ = normal(values[r])
        return (unit * (1.0 + mod[SCALE_A : SCALE_A + 1]) + mod[SHIFT_A : SHIFT_A + 1]).astype(
            jnp.bfloat16
        )


class Middle(Bridge):
    def __init__(self, terms, values, mod):
        length, width = values.shape
        super().__init__(terms, [values, mod], width, length, length)
        self.result((length, width))
        self.result((length, width))

    def work(self, r, total, given, made, state):
        values, mod = given
        attn, middle = made
        attn[r] = total
        fresh = values[r] + mod[GATE_A : GATE_A + 1] * total
        middle[r] = fresh
        unit, _ = normal(fresh)
        return (unit * (1.0 + mod[SCALE_M : SCALE_M + 1]) + mod[SHIFT_M : SHIFT_M + 1]).astype(
            jnp.bfloat16
        )


class Decode(Bridge):
    whole = True

    def __init__(self, terms, middle, mod, mod_next, place, base, contrast):
        (length, width), (length_next, _) = middle.shape, base.shape
        more = [middle, mod, mod_next, place, base, *contrast]
        super().__init__(terms, more, width, length, length_next)
        self.result((length, width))
        self.result((length, width))
        self.result((length_next, width))
        self.result((1, width))
        self.result((1, 1))

    def collect(self, r, total, given, made, state):
        middle, mod = given[:2]
        branch, encoded = made[:2]
        branch[r] = total
        encoded[r] = middle[r] + mod[GATE_M : GATE_M + 1] * total

    def turn(self, given, made, state):
        place, base = given[3:5]
        made[2][...] = full_dot(place[...], made[1][...]) + base[...]

    def work(self, r, total, given, made, state):
        mod = given[2]
        unit, _ = normal(made[2][r])
        return (unit * (1.0 + mod[SCALE_A : SCALE_A + 1]) + mod[SHIFT_A : SHIFT_A + 1]).astype(
            jnp.bfloat16
        )


    def aside(self, given, made):
        valid, count, teachers, positive = given[5:]
        pooled = fold(made[1][...] * valid[...]) / count[...]
        scale = lax.rsqrt(jnp.sum(pooled * pooled, -1, keepdims=True) + 1e-06)
        others = teachers[...]
        others = others * lax.rsqrt(jnp.sum(others * others, -1, keepdims=True) + 1e-06)
        logits = jnp.sum(pooled * scale * others, -1, keepdims=True) / contrast_sharpness_divisor
        peak = jnp.max(logits, 0, keepdims=True)
        expo = jnp.exp(logits - peak)
        total = fold(expo)
        made[4][...] = peak + jnp.log(total) - fold(logits * positive[...])
        weight = (expo / total - positive[...]) * (nce_weight / others.shape[0])
        grad = fold(weight * others) / contrast_sharpness_divisor
        along = jnp.sum(pooled * grad, -1, keepdims=True)
        made[3][...] = scale * (grad - pooled * (scale * scale * along)) / count[...]


class Turn(Bridge):
    def __init__(self, terms, middle, mod, head, noise, count_all):
        length, width = middle.shape
        super().__init__(terms, [middle, mod, head, noise], width, length, length)
        self.scale = 2.0 / count_all
        self.result((length, width))
        self.result((1, width))
        self.result(head.shape)
        self.result((1, 1))

    def work(self, r, total, given, made, state):
        middle, mod, head, noise = given
        gate = mod[GATE_M : GATE_M + 1]
        unit, scale = normal(middle[r] + gate * total)
        low = unit.astype(jnp.bfloat16)
        rows_by_rows = (((1,), (1,)), ((), ()))
        predict = lax.dot_general(low, head[...], rows_by_rows, preferred_element_type=jnp.float32)
        error = predict - noise[r]
        self.add(state, TERM_SQUARE, jnp.sum(error * error, keepdims=True))
        grad_predict = (error * self.scale).astype(jnp.bfloat16)
        columns_by_columns = (((0,), (0,)), ((), ()))
        self.add(
            state,
            TERM_HEAD,
            lax.dot_general(
                grad_predict, low, columns_by_columns, preferred_element_type=jnp.float32
            ),
        )
        grad_final = jnp.dot(grad_predict, head[...], preferred_element_type=jnp.float32)
        grad = normal_back(grad_final, unit, scale)
        made[0][r] = grad
        self.add(state, TERM_GATE, fold(grad * total))
        return (gate * grad).astype(jnp.bfloat16)

    def end(self, given, made, state):
        made[1][...] = state[TERM_GATE]
        made[2][...] = state[TERM_HEAD]
        made[3][...] = state[TERM_SQUARE]


class MiddleBack(Bridge):
    def __init__(self, terms, middle, attn, grad, mod):
        length, width = middle.shape
        super().__init__(terms, [middle, attn, grad, mod], width, length, length)
        self.result((length, width))
        self.result((3, width))

    def work(self, r, total, given, made, state):
        middle, attn, grad, mod = given
        unit, scale = normal(middle[r])
        self.add(state, TERM_SHIFT, fold(total))
        self.add(state, TERM_SCALE, fold(total * unit))
        back = normal_back(total * (1.0 + mod[SCALE_M : SCALE_M + 1]), unit, scale)
        fresh = grad[r] + back
        made[0][r] = fresh
        self.add(state, TERM_GATE, fold(fresh * attn[r]))
        return (mod[GATE_A : GATE_A + 1] * fresh).astype(jnp.bfloat16)

    def end(self, given, made, state):
        made[1][0:1] = state[TERM_SHIFT]
        made[1][1:2] = state[TERM_SCALE]
        made[1][2:3] = state[TERM_GATE]


class Encode(Bridge):
    whole = True

    def __init__(self, terms, values, grad, mod, more, pairs):
        branch = more[4]
        (length, width), (length_next, _) = values.shape, branch.shape
        super().__init__(
            terms,
            [values, grad, mod, *more, *pairs],
            width,
            length,
            length_next,
        )
        self.result((length_next, width))
        self.result((4, width))
        self.result((width, pairs[1].shape[2]), jnp.bfloat16)
        self.result((width, pairs[3].shape[2]), jnp.bfloat16)
        self.scratch = [pltpu.VMEM((length, width), jnp.float32)] + self.scratch

    def begin(self, ins, outs, scratch, halfway):
        self.held = scratch[0]
        super().begin(ins, outs, scratch[1:], halfway)

    def collect(self, r, total, given, made, state):
        values, grad, mod, open_place = given[:4]
        unit, scale = normal(values[r])
        self.add(state, TERM_SHIFT, fold(total))
        self.add(state, TERM_SCALE, fold(total * unit))
        back = normal_back(total * (1.0 + mod[SCALE_A : SCALE_A + 1]), unit, scale)
        fresh = grad[r] + back
        self.held[r] = fresh
        self.add(state, TERM_MASK, fold(open_place[r] * fresh))

    def turn(self, given, made, state):
        select, (valid, pool) = given[4], given[5:7]
        made[0][...] = full_dot(select[...], self.held[...]) + valid[...] * pool[...]

    def work(self, r, total, given, made, state):
        branch, mod_next = given[7:9]
        fresh = made[0][r]
        self.add(state, TERM_GATE, fold(fresh * branch[r]))
        return (mod_next[GATE_M : GATE_M + 1] * fresh).astype(jnp.bfloat16)

    def end(self, given, made, state):
        made[1][0:1] = state[TERM_SHIFT]
        made[1][1:2] = state[TERM_SCALE]
        made[1][2:3] = state[TERM_GATE]
        made[1][3:4] = state[TERM_MASK]

    def aside(self, given, made):
        outer(given[9], given[10], made[2])
        outer(given[11], given[12], made[3])


class Leave(Bridge):
    sends_on = False

    def __init__(self, terms, values, grad, mod, kept, sums, pairs):
        length, width = values.shape
        super().__init__(terms, [values, grad, mod, kept, *sums, *pairs], width, length, length)
        narrows = group_size(NARROW)
        piece = jax.ShapeDtypeStruct((narrows, 48, width // narrows), jnp.float32)
        self.tell = Exchange([piece], [(NARROW, EACH)])
        self.result(piece.shape)
        self.result((width, pairs[1].shape[2]), jnp.bfloat16)
        self.result((width, pairs[3].shape[2]), jnp.bfloat16)
        self.scratch = (
            [pltpu.VMEM((48, width), jnp.float32), pltpu.VMEM(piece.shape, jnp.float32)]
            + self.tell.scratch
            + self.scratch
        )

    def greet(self, barrier):
        return super().greet(barrier) + self.tell.greet(barrier)

    def begin(self, ins, outs, scratch, halfway):
        self.table, self.piece = scratch[:2]
        self.tell_sems = scratch[2:4]
        super().begin(ins, outs, scratch[4:], halfway)

    def work(self, r, total, given, made, state):
        values, grad, mod, kept = given[:4]
        unit, scale = normal(values[r])
        self.add(state, TERM_SHIFT, fold(total))
        self.add(state, TERM_SCALE, fold(total * unit))
        back = normal_back(total * (1.0 + mod[SCALE_A : SCALE_A + 1]), unit, scale)
        columns_by_columns = (((0,), (0,)), ((), ()))
        self.add(
            state,
            TERM_PATCH,
            lax.dot_general(
                kept[r],
                grad[r] + back,
                columns_by_columns,
                precision=highest_float_accuracy,
                preferred_element_type=jnp.float32,
            ),
        )

    def end(self, given, made, state):
        sums_m0, sums_a1, sums_m1, gate_m1, head = given[4:9]
        table = self.table
        table[...] = jnp.zeros(table.shape, jnp.float32)
        table[0:1] = state[TERM_SHIFT]
        table[1:2] = state[TERM_SCALE]
        table[2:3] = sums_m0[2:3]
        table[3:5] = sums_m0[0:2]
        table[5:6] = sums_a1[2:3]
        table[6:8] = sums_a1[0:2]
        table[8:9] = sums_m1[2:3]
        table[9:11] = sums_m1[0:2]
        table[11:12] = gate_m1[...]
        table[12:28] = state[TERM_PATCH]
        table[28:44] = head[...]
        table[44:45] = sums_a1[3:4]
        local = self.piece.shape[2]
        for z in range(self.piece.shape[0]):
            self.piece[z] = table[:, z * local : (z + 1) * local]
        self.tell.begin([self.piece], made[:1], self.tell_sems, lambda: None)

    def aside(self, given, made):
        outer(given[9], given[10], made[1])
        outer(given[11], given[12], made[2])


class Errand(Part):
    def plan(self, ins, outs):
        raise NotImplementedError

    def local(self, ins, outs):
        return []

    def reserve(self, count, local=0):
        self.scratch = [pltpu.SemaphoreType.DMA((count,)), pltpu.SemaphoreType.DMA((count,))]
        if local:
            self.scratch.append(pltpu.SemaphoreType.DMA((local,)))

    def go(self, step, ins, outs, scratch):
        first = 0
        plans = self.plan(ins, outs)
        if step == 1 and len(plans) == 1:
            return
        for turn, moves in enumerate(plans):
            last = turn == len(plans) - 1
            if step == (2 if last else turn + 1):
                self.run(moves, first, scratch, True)
            if step == turn:
                self.run(moves, first, scratch, False)
            first += len(moves)
        if step != 1:
            for i, (source, target, when) in enumerate(self.local(ins, outs)):

                def act_local(i=i, source=source, target=target):
                    copy = pltpu.make_async_copy(source, target, scratch[2].at[i])
                    if step:
                        copy.wait()
                    else:
                        copy.start()

                pl.when(when)(act_local)

    def run(self, moves, first, scratch, ending):
        for i, (source, target, landing, device, when) in enumerate(moves):

            def remote(place, i=first + i, source=source, device=device):
                return pltpu.make_async_remote_copy(
                    src_ref=source,
                    dst_ref=place,
                    send_sem=scratch[0].at[i],
                    recv_sem=scratch[1].at[i],
                    device_id=device,
                    device_id_type=MESH,
                )

            def act(remote=remote, target=target, landing=landing):
                if ending:
                    remote(landing).wait_recv()
                    remote(target).wait_send()
                else:
                    remote(target).start()

            if when is None:
                act()
            else:
                pl.when(when)(act)


def plane_peers():
    peers = []
    for axis in (PY, PX):
        for offset in range(1, lax.axis_size(axis)):
            peers.append(lambda axis=axis, offset=offset: {axis: turned(axis, offset)})
    return peers


SWAP_PEERS = [
    lambda: {CORE: other(CORE)},
    lambda: {ZH: other(ZH)},
    lambda: {CORE: other(CORE), ZH: other(ZH)},
]


class SwapIn(Errand):
    def __init__(self, shard):
        super().__init__()
        self.take(shard)
        self.give((lax.axis_size(PY), lax.axis_size(PX), 2) + shard.shape)
        self.peers = SWAP_PEERS
        self.reserve(2, 1)

    def plan(self, ins, outs):
        core, half = lax.axis_index(CORE), lax.axis_index(ZH)
        home = outs[0].at[lax.axis_index(PY), lax.axis_index(PX)]
        crossed = jnp.where(core == 0, 1 - half, half)
        return [
            [
                (ins[0], home.at[core], home.at[1 - core], {CORE: 1 - core, ZH: crossed}, None),
                (ins[0], home.at[1], home.at[1], {ZH: 1 - half}, core == 1),
            ]
        ]

    def local(self, ins, outs):
        home = outs[0].at[lax.axis_index(PY), lax.axis_index(PX)]
        return [(ins[0], home.at[0], lax.axis_index(CORE) == 0)]


class Spread(Errand):
    def __init__(self, rows, stages):
        super().__init__()
        self.stages = stages
        self.give(rows.shape, rows.dtype, pltpu.HBM, self.take(rows))
        self.peers = plane_peers()
        ny, nx = rows.shape[:2]
        straight, relayed = nx + ny - 2, 2 * (nx - 1) * (ny - 1)
        self.reserve(sum(relayed if stage == RELAY else straight for stage in stages))

    def plan(self, ins, outs):
        rows = outs[0]
        ny, nx = rows.shape[:2]
        first, then = [], []
        own = {PY: lax.axis_index(PY), PX: lax.axis_index(PX)}
        sides = [(PX, nx), (PY, ny)]

        def along(moves, axis, offset, at, core):
            land = dict(at)
            land[axis] = turned(axis, -offset)
            here = rows.at[at[PY], at[PX], core]
            there = rows.at[land[PY], land[PX], core]
            moves.append((here, here, there, {axis: turned(axis, offset)}, None))

        for stage in self.stages:
            if stage == RELAY:
                for e in range(1, nx):
                    for offset in range(1, ny):
                        along(then, PY, offset, {**own, PX: turned(PX, e)}, 0)
                for e in range(1, ny):
                    for offset in range(1, nx):
                        along(then, PX, offset, {**own, PY: turned(PY, e)}, 1)
            else:
                for core, (axis, size) in enumerate(sides if stage == STRAIGHT else sides[::-1]):
                    for offset in range(1, size):
                        along(first, axis, offset, own, core)
        if STRAIGHT in self.stages:
            return [first, then] if then else [first]
        return [first + then]


class FoldFar(Errand):
    def __init__(self, grad):
        super().__init__()
        self.take(grad)
        ny, nx, _, rows, columns = grad.shape
        self.give((ny - 1, nx - 1, rows, columns))
        self.give((nx - 1, ny - 1, rows, columns))
        self.peers = plane_peers()
        self.reserve(2 * (nx - 1) * (ny - 1))

    def plan(self, ins, outs):
        grad = ins[0]
        ny, nx = grad.shape[:2]
        moves = []
        for e in range(1, nx):
            for d in range(1, ny):
                slot = outs[0].at[d - 1, e - 1]
                to = turned(PY, d)
                moves.append((grad.at[to, turned(PX, e), 0], slot, slot, {PY: to}, None))
        for e in range(1, ny):
            for d in range(1, nx):
                slot = outs[1].at[d - 1, e - 1]
                to = turned(PX, d)
                moves.append((grad.at[turned(PY, e), to, 1], slot, slot, {PX: to}, None))
        return [moves]


class FoldNear(Errand):
    def __init__(self, grad):
        super().__init__()
        self.take(grad)
        ny, nx, _, rows, columns = grad.shape
        self.give((ny - 1, rows, columns))
        self.give((nx - 1, rows, columns))
        self.peers = plane_peers()
        self.reserve(nx + ny - 2)

    def plan(self, ins, outs):
        grad = ins[0]
        ny, nx = grad.shape[:2]
        y, x = lax.axis_index(PY), lax.axis_index(PX)
        moves = []
        for d in range(1, ny):
            to, slot = turned(PY, d), outs[0].at[d - 1]
            moves.append((grad.at[to, x, 0], slot, slot, {PY: to}, None))
        for d in range(1, nx):
            to, slot = turned(PX, d), outs[1].at[d - 1]
            moves.append((grad.at[y, to, 1], slot, slot, {PX: to}, None))
        return [moves]


class FoldRelay(Errand):
    def __init__(self, sums):
        super().__init__()
        for each in sums:
            self.take(each)
            self.give(each.shape)
        self.peers = plane_peers()
        self.reserve(sums[0].shape[0] + sums[1].shape[0])

    def plan(self, ins, outs):
        moves = []
        for i, axis in enumerate((PX, PY)):
            for e in range(1, lax.axis_size(axis)):
                slot = outs[i].at[e - 1]
                moves.append((ins[i].at[e - 1], slot, slot, {axis: turned(axis, e)}, None))
        return [moves]


class SwapOut(Errand):
    def __init__(self, pair):
        super().__init__()
        self.take(pair)
        self.give(pair.shape)
        self.peers = SWAP_PEERS
        self.reserve(2, 1)

    def plan(self, ins, outs):
        core, half = lax.axis_index(CORE), lax.axis_index(ZH)
        crossed = jnp.where(core == 0, half, 1 - half)
        pair, met = ins[0], outs[0]
        return [
            [
                (pair.at[1 - core], met.at[0], met.at[0], {CORE: 1 - core, ZH: crossed}, None),
                (pair.at[1], met.at[1], met.at[1], {ZH: 1 - half}, core == 1),
            ]
        ]

    def local(self, ins, outs):
        return [(ins[0].at[0], outs[0].at[1], lax.axis_index(CORE) == 0)]


def take_counts(refs, sizes):
    taken, rest = [], list(refs)
    for size in sizes:
        taken.append(rest[:size])
        rest = rest[size:]
    return taken, rest


def kernel(parts, *refs):
    ins, refs = take_counts(refs, [len(part.arrays) for part in parts])
    outs, refs = take_counts(refs, [len(part.shapes) for part in parts])
    scratch, _ = take_counts(refs, [len(part.scratch) for part in parts])
    barrier = pltpu.get_barrier_semaphore()
    greeted = sum(part.greet(barrier) for part in parts)
    pl.semaphore_wait(barrier, greeted)

    def errands(step):
        for i in range(1, len(parts)):
            parts[i].go(step, ins[i], outs[i], scratch[i])

    errands(0)
    parts[0].begin(ins[0], outs[0], scratch[0], partial(errands, 1))
    errands(2)


def travel(collective_id, *parts):
    aliases, first_in, first_out = {}, 0, 0
    for part in parts:
        for source, result in part.aliases.items():
            aliases[first_in + source] = first_out + result
        first_in += len(part.arrays)
        first_out += len(part.shapes)
    results = pl.pallas_call(
        partial(kernel, parts),
        out_shape=[shape for part in parts for shape in part.shapes],
        in_specs=[pl.BlockSpec(memory_space=space) for part in parts for space in part.in_spaces],
        out_specs=[pl.BlockSpec(memory_space=space) for part in parts for space in part.out_spaces],
        scratch_shapes=[each for part in parts for each in part.scratch],
        input_output_aliases=aliases,
        compiler_params=pltpu.CompilerParams(
            collective_id=collective_id, has_side_effects=True, vmem_limit_bytes=24 * 2**20
        ),
        cost_estimate=pl.CostEstimate(flops=2 * 10**10, bytes_accessed=1024, transcendentals=0),
    )(*[array for part in parts for array in part.arrays])
    split, _ = take_counts(results, [len(part.shapes) for part in parts])
    return split


class Route:
    def __init__(self, shards, errands):
        self.shards = shards
        self.errands = iter(errands)
        self.rows, self.grads, self.got = {}, {}, {FAR: {}, NEAR: {}, PASS: {}, LEAVE: {}}
        self.count = 0

    def step(self, main):
        errands, parts = next(self.errands), [main]
        for name, what in errands:
            if what == (ENTER,):
                parts.append(SwapIn(self.shards[name]))
            elif what == (FAR,):
                parts.append(FoldFar(self.grads[name]))
            elif what == (NEAR,):
                parts.append(FoldNear(self.grads[name]))
            elif what == (PASS,):
                parts.append(FoldRelay(self.far_sums(name)))
            elif what == (LEAVE,):
                parts.append(SwapOut(self.pair(name)))
            else:
                parts.append(Spread(self.rows[name], what))
        results = travel(self.count, *parts)
        self.count += 1
        for (name, what), got in zip(errands, results[1:]):
            if what[0] in self.got:
                self.got[what[0]][name] = got
            else:
                self.rows[name] = got[0]
        return results[0]

    def weight(self, kind, block):
        rows = self.rows[kind, block]
        return rows.reshape(-1, rows.shape[-1])

    def give_grad(self, kind, block, grad):
        name = (kind, block)
        self.grads[name] = grad.astype(jnp.bfloat16).reshape(self.rows[name].shape)

    def own_rows(self, name, py, px, core):
        grad = self.grads[name]
        at = lax.dynamic_slice(grad, (py, px, core, 0, 0), (1, 1, 1) + grad.shape[3:])
        return at[0, 0, 0].astype(jnp.float32)

    def far_sums(self, name):
        y, x = lax.axis_index(PY), lax.axis_index(PX)
        along_y, along_x = self.got[FAR][name]
        first = [
            self.own_rows(name, y, turned(PX, e), 0)
            + jnp.sum(along_y[:, e - 1].astype(jnp.float32), 0)
            for e in range(1, lax.axis_size(PX))
        ]
        last = [
            self.own_rows(name, turned(PY, e), x, 1)
            + jnp.sum(along_x[:, e - 1].astype(jnp.float32), 0)
            for e in range(1, lax.axis_size(PY))
        ]
        return jnp.stack(first).astype(jnp.bfloat16), jnp.stack(last).astype(jnp.bfloat16)

    def pair(self, name):
        y, x = lax.axis_index(PY), lax.axis_index(PX)
        halves = []
        for core in range(2):
            near = jnp.sum(self.got[NEAR][name][core].astype(jnp.float32), 0)
            relayed = jnp.sum(self.got[PASS][name][core].astype(jnp.float32), 0)
            halves.append(self.own_rows(name, y, x, core) + near + relayed)
        return jnp.stack(halves).astype(jnp.bfloat16)

    def met(self, kind, block):
        return self.got[LEAVE][kind, block][0]


ROWS_BY_ROWS = (((1,), (1,)), ((), ()))
COLUMNS_BY_COLUMNS = (((0,), (0,)), ((), ()))


def head_of(array, which, head, local):
    first = which * local + head * HEAD_DIM
    return array[0, :, first : first + HEAD_DIM]


def soft(query, key, valid):
    scores = lax.dot_general(query, key, ROWS_BY_ROWS, preferred_element_type=jnp.float32)
    scores = jnp.where(valid > 0, scores * (1.0 / math.sqrt(HEAD_DIM)), -1e30)
    expo = jnp.exp(scores - jnp.max(scores, -1, keepdims=True))
    return expo / jnp.sum(expo, -1, keepdims=True)


def attend_kernel(normed, valid, weight_in, weight_out, triple, context, terms):
    local = context.shape[2]
    triple[0] = jnp.dot(normed[0], weight_in[...], preferred_element_type=jnp.float32).astype(
        jnp.bfloat16
    )
    parts = []
    for head in range(local // HEAD_DIM):
        query, key, value = [head_of(triple, which, head, local) for which in range(3)]
        probs = soft(query, key, valid[0]).astype(jnp.bfloat16)
        parts.append(jnp.dot(probs, value, preferred_element_type=jnp.float32))
    flat = jnp.concatenate(parts, 1).astype(jnp.bfloat16)
    context[0] = flat
    terms[0] = lax.dot_general(
        flat, weight_out[...], ROWS_BY_ROWS, preferred_element_type=jnp.float32
    ).astype(jnp.bfloat16)


def attend_back_kernel(
    triple, valid, grad_attn, weight_in, weight_out, grad_triple, terms, grad_context
):
    local = weight_out.shape[1]
    scale = 1.0 / math.sqrt(HEAD_DIM)
    grad_context[0] = jnp.dot(
        grad_attn[0], weight_out[...], preferred_element_type=jnp.float32
    ).astype(jnp.bfloat16)
    queries, keys, values = [], [], []
    for head in range(local // HEAD_DIM):
        query, key, value = [head_of(triple, which, head, local) for which in range(3)]
        grad = head_of(grad_context, 0, head, local)
        probs = soft(query, key, valid[0])
        values.append(
            lax.dot_general(
                probs.astype(jnp.bfloat16),
                grad,
                COLUMNS_BY_COLUMNS,
                preferred_element_type=jnp.float32,
            )
        )
        grad_probs = lax.dot_general(
            grad, value, ROWS_BY_ROWS, preferred_element_type=jnp.float32
        )
        tilt = jnp.sum(grad_probs * probs, -1, keepdims=True)
        grad_scores = (probs * (grad_probs - tilt)).astype(jnp.bfloat16)
        queries.append(jnp.dot(grad_scores, key, preferred_element_type=jnp.float32) * scale)
        keys.append(
            lax.dot_general(
                grad_scores, query, COLUMNS_BY_COLUMNS, preferred_element_type=jnp.float32
            )
            * scale
        )
    fresh = jnp.concatenate(queries + keys + values, 1).astype(jnp.bfloat16)
    grad_triple[0] = fresh
    terms[0] = lax.dot_general(
        fresh, weight_in[...], ROWS_BY_ROWS, preferred_element_type=jnp.float32
    ).astype(jnp.bfloat16)


def by_image(body, arrays, weights, columns, scratch=()):
    images, length = arrays[0].shape[:2]

    def block(array):
        return pl.BlockSpec((1,) + array.shape[1:], lambda i: (i, 0, 0))

    made = [jax.ShapeDtypeStruct((images, length, each), jnp.bfloat16) for each in columns]
    return pl.pallas_call(
        body,
        grid=(images,),
        out_shape=made,
        in_specs=[block(array) for array in arrays]
        + [pl.BlockSpec(weight.shape, lambda i: (0, 0)) for weight in weights],
        out_specs=[block(each) for each in made],
        scratch_shapes=[pltpu.VMEM((1, length, each), jnp.bfloat16) for each in scratch],
        compiler_params=pltpu.CompilerParams(vmem_limit_bytes=24 * 2**20),
        cost_estimate=pl.CostEstimate(flops=5 * 10**9, bytes_accessed=1024, transcendentals=0),
    )(*arrays, *weights)


def low_dot(spec, left, right):
    return jnp.einsum(spec, left, right, preferred_element_type=jnp.float32)


def attend(normed, key_valid, block, route):
    weights = [route.weight(IN, block), route.weight(OUT, block)]
    width, local = weights[1].shape
    triple, flat_context, terms = by_image(
        attend_kernel, [normed, key_valid], weights, (3 * local, local, width)
    )
    return terms, (triple, flat_context)


def feed(normed, block, route):
    inner = low_dot("bld,df->blf", normed, route.weight(EXPAND, block))
    active = jax.nn.gelu(inner, approximate=True).astype(jnp.bfloat16)
    terms = low_dot("blf,df->bld", active, route.weight(CONTRACT, block)).astype(jnp.bfloat16)
    return terms, (inner, active)


def feed_back(grad_branch, normed, saved, block, route):
    inner, active = saved
    grad_active = low_dot("bld,df->blf", grad_branch, route.weight(CONTRACT, block))
    gelu_back = jax.vjp(partial(jax.nn.gelu, approximate=True), inner)[1]
    grad_inner = gelu_back(grad_active)[0].astype(jnp.bfloat16)
    terms = low_dot("blf,df->bld", grad_inner, route.weight(EXPAND, block)).astype(jnp.bfloat16)
    route.give_grad(CONTRACT, block, low_dot("bld,blf->df", grad_branch, active))
    route.give_grad(EXPAND, block, low_dot("bld,blf->df", normed, grad_inner))
    return terms


def attend_back(grad_attn, normed, saved, key_valid, block, route):
    triple, flat_context = saved
    weights = [route.weight(IN, block), route.weight(OUT, block)]
    width, local = weights[1].shape
    grad_triple, terms = by_image(
        attend_back_kernel,
        [triple, key_valid, grad_attn],
        weights,
        (3 * local, width),
        (local,),
    )
    return terms, (normed, grad_triple, grad_attn, flat_context)


def errands_in_turn():
    def attend(block, *what):
        return [((IN, block), what), ((OUT, block), what)]

    def expand(block, *what):
        return [((EXPAND, block), what)]

    def contract(block, *what):
        return [((CONTRACT, block), what)]

    def feed(block, *what):
        return expand(block, *what) + contract(block, *what)

    return [
        attend(0, ENTER),
        attend(0, STRAIGHT) + expand(0, ENTER),
        attend(0, CROSS, RELAY) + contract(0, ENTER) + expand(0, STRAIGHT),
        expand(0, CROSS, RELAY) + contract(0, STRAIGHT) + attend(1, ENTER),
        contract(0, CROSS, RELAY) + attend(1, STRAIGHT) + expand(1, ENTER),
        attend(1, CROSS, RELAY) + expand(1, STRAIGHT, CROSS) + contract(1, ENTER),
        contract(1, STRAIGHT, CROSS, RELAY) + expand(1, RELAY),
        [],
        feed(1, FAR) + feed(1, NEAR),
        feed(1, PASS),
        feed(0, FAR) + attend(1, FAR) + attend(1, NEAR) + expand(1, LEAVE),
        contract(0, NEAR) + feed(0, PASS) + attend(1, PASS) + contract(1, LEAVE),
        attend(0, FAR) + expand(0, NEAR) + contract(0, LEAVE) + attend(1, LEAVE),
        attend(0, NEAR) + attend(0, PASS) + expand(0, LEAVE),
        attend(0, LEAVE),
        [],
    ]


def adam(weight, grad, moment, second, average, factor):
    grad = grad * factor
    moment = beta_first * moment + (1.0 - beta_first) * grad
    second = beta_second * second + (1.0 - beta_second) * grad * grad
    update = (
        moment
        / (1.0 - beta_first**STEP)
        / (jnp.sqrt(second / (1.0 - beta_second**STEP)) + adam_eps)
    )
    fresh = weight - learn_rate * (update + weight_decay * weight)
    average_decay = min(ema_decay, (1.0 + STEP) / (10.0 + STEP))
    average = average_decay * average + (1.0 - average_decay) * fresh
    return (fresh, moment, second, average)


def shards(
    patches,
    target_noise,
    kept_slots,
    kept_count,
    time_step,
    labels,
    teacher,
    *tables,
):
    params, moments, seconds, averages = tables[:7], tables[7:14], tables[14:21], tables[21:]
    attend_in, attend_out, expand, contract, modulation, patch_table, condition = params
    batch, length = (patches.shape[0], patches.shape[1])
    capacity = kept_slots.shape[1]
    rows, local = (attend_in.shape[1], attend_in.shape[3])
    wides, narrows = (group_size(WIDE), group_size(NARROW))
    wide_index, narrow_index = (flat_place(WIDE), flat_place(NARROW))
    images = batch * wides
    width = local * narrows
    assert batch == narrows

    shards_low = {}
    for i in range(2):
        shards_low[IN, i] = attend_in[i].reshape(rows, 3 * local).astype(jnp.bfloat16)
        shards_low[OUT, i] = attend_out[i].T.astype(jnp.bfloat16)
        shards_low[EXPAND, i] = expand[i].astype(jnp.bfloat16)
        shards_low[CONTRACT, i] = contract[i].T.astype(jnp.bfloat16)
    route = Route(shards_low, errands_in_turn())

    def own(array):
        return lax.dynamic_index_in_dim(array, narrow_index, 0, keepdims=False)

    condition_low = condition.astype(jnp.bfloat16)
    features = sinusoid(time_step, FREQ)
    onehot = (labels[:, None] == jnp.arange(CLASSES)[None, :]).astype(jnp.bfloat16)
    cond_part = jnp.dot(
        features, condition_low[:FREQ].astype(jnp.float32), precision=highest_float_accuracy
    ) + low_dot("bc,cd->bd", onehot, condition_low[FREQ:])
    pieces = jax.nn.silu(cond_part).reshape(batch, local // rows, rows)
    pieces = jnp.pad(jnp.transpose(pieces, (1, 0, 2)), ((0, 0), (0, 8 - batch), (0, 0)))
    (silu_wide,) = route.step(RowPieces(pieces))
    silu_rows = silu_wide[:, :batch].reshape(images, rows).astype(jnp.bfloat16)
    modulation_low = modulation.astype(jnp.bfloat16)
    mod_part = low_dot("ip,npkc->inkc", silu_rows, modulation_low)
    mod_part = mod_part.reshape(wides, batch, 12 * local)
    (mod_wide,) = route.step(Exchange([mod_part], [(WIDE, EACH)]))
    facts = jnp.stack([kept_count, time_step, labels], 1).astype(jnp.float32)
    facts = jnp.pad(facts, ((0, 4), (0, local - 3)))
    teacher_rows = teacher.reshape(batch * narrows, local)
    payload = jnp.concatenate([cond_part, facts[:batch], teacher_rows], 0)
    table_pad = jnp.pad(patch_table.astype(jnp.bfloat16), ((0, 15), (0, 0)))
    mod_near, everyone, tables_near = route.step(
        Exchange(
            [jnp.sum(mod_wide, 0).reshape(batch, 12, local), payload, table_pad],
            [(NARROW, EACH), (WIDE, SAME), (NARROW, SAME)],
        )
    )
    mods = jnp.transpose(mod_near, (1, 0, 2)).reshape(12, width)
    mod_enc, mod_dec = mods[:6], mods[6:]
    cond_cols = everyone[:, :batch].reshape(images, local)
    facts_all = everyone[:, batch : 2 * batch, :3]
    negatives = everyone[:, 2 * batch :].reshape(images, width)
    time_all = facts_all[:, :, 1].reshape(images).astype(jnp.int32)
    labels_all = facts_all[:, :, 2].reshape(images).astype(jnp.int32)
    patch_full = jnp.transpose(tables_near, (1, 0, 2)).reshape(48, width)

    count_own = own(kept_count).astype(jnp.float32)
    slot_valid = (jnp.arange(capacity) < own(kept_count)).astype(jnp.float32)[:, None]
    select = (own(kept_slots)[:, None] == jnp.arange(length)[None, :]).astype(
        jnp.float32
    ) * slot_valid
    open_place = 1.0 - jnp.sum(select, 0)[:, None]
    places = sinusoid(jnp.arange(length), width)
    group_counts = lax.dynamic_slice(
        facts_all[:, :, 0],
        (flat_place((PY, PX)) * 2, lax.axis_index(ZH) * 2),
        (2, 2),
    ).reshape(4)
    group_valid = (jnp.arange(capacity)[None, None, :] < group_counts[:, None, None]).astype(
        jnp.float32
    )
    all_valid = jnp.ones((4, 1, length), jnp.float32)
    kept_patches = low_dot("cl,lp->cp", select.astype(jnp.bfloat16), own(patches))
    embed = low_dot("cp,pd->cd", kept_patches.astype(jnp.bfloat16), patch_full[:PATCH_IN])
    embed = embed + jnp.dot(select, places, precision=highest_float_accuracy)
    mask_token = patch_full[2 * PATCH_IN : 2 * PATCH_IN + 1].astype(jnp.float32)
    base = open_place * mask_token + places
    head = patch_full[PATCH_IN : 2 * PATCH_IN]
    count_all = images * length * PATCH_IN

    (normed_a0,) = route.step(Enter(embed, mod_enc))
    terms, saved_a0 = attend(normed_a0, group_valid, 0, route)
    normed_m0, attn0, middle0 = route.step(Middle(terms, embed, mod_enc))
    terms, saved_m0 = feed(normed_m0, 0, route)
    positive = ((wide_index * batch + narrow_index) == jnp.arange(images)).astype(jnp.float32)
    contrast = (slot_valid, count_own.reshape(1, 1), negatives, positive[:, None])
    normed_a1, branch0, _, decode_in, grad_pool, nce = route.step(
        Decode(terms, middle0, mod_enc, mod_dec, select.T, base, contrast)
    )
    terms, saved_a1 = attend(normed_a1, all_valid, 1, route)
    normed_m1, attn1, middle1 = route.step(Middle(terms, decode_in, mod_dec))
    terms, saved_m1 = feed(normed_m1, 1, route)
    grad_branch, grad_decoded, gate_m1, grad_head, square = route.step(
        Turn(terms, middle1, mod_dec, head, own(target_noise), count_all)
    )

    terms = feed_back(grad_branch, normed_m1, saved_m1, 1, route)
    grad_attn, grad_mid, sums_m1 = route.step(
        MiddleBack(terms, middle1, attn1, grad_decoded, mod_dec)
    )
    terms, pairs = attend_back(grad_attn, normed_a1, saved_a1, all_valid, 1, route)
    back_to = (open_place, select, slot_valid, grad_pool, branch0, mod_enc)
    grad_branch, grad_encoded, sums_a1, grad_in, grad_out = route.step(
        Encode(terms, decode_in, grad_mid, mod_dec, back_to, pairs)
    )
    route.give_grad(IN, 1, grad_in)
    route.give_grad(OUT, 1, grad_out)
    terms = feed_back(grad_branch, normed_m0, saved_m0, 0, route)
    grad_attn, grad_mid, sums_m0 = route.step(
        MiddleBack(terms, middle0, attn0, grad_encoded, mod_enc)
    )
    terms, pairs = attend_back(grad_attn, normed_a0, saved_a0, group_valid, 0, route)
    sums = (sums_m0, sums_a1, sums_m1, gate_m1, grad_head)
    rows_near, grad_in, grad_out = route.step(
        Leave(terms, embed, grad_mid, mod_enc, kept_patches, sums, pairs)
    )
    route.give_grad(IN, 0, grad_in)
    route.give_grad(OUT, 0, grad_out)

    mods_near = rows_near[:, :12].reshape(narrows, 12 * local)
    table_near = rows_near[:, 12:45]
    table_sum = jnp.pad(jnp.sum(table_near, 0), ((0, 15), (0, 0))).astype(jnp.bfloat16)
    mods_all, table_all = route.step(
        Exchange([mods_near, table_sum], [(WIDE, SAME), (WIDE, SAME)])
    )
    grad_patch_table = jnp.sum(table_all.astype(jnp.float32), 0)[:33]
    mods_all = mods_all.reshape(images, 2, 6, local)
    silu_broad = silu_rows.astype(jnp.float32)
    grad_modulation = jnp.einsum(
        "ip,inkc->npkc", silu_broad, mods_all, precision=highest_float_accuracy
    )
    grad_silu = jnp.einsum(
        "inkc,npkc->ip",
        mods_all,
        modulation_low.astype(jnp.float32),
        precision=highest_float_accuracy,
    )
    (silu_near,) = route.step(Exchange([grad_silu], [(NARROW, SAME)]))
    (silu_wide,) = route.step(Exchange([jnp.sum(silu_near, 0)], [(WIDE, SAME)]))
    grad_silu = jnp.transpose(silu_wide, (1, 0, 2)).reshape(images, width)
    grad_silu = lax.dynamic_slice_in_dim(grad_silu, narrow_index * local, local, 1)
    grad_cond = jax.vjp(jax.nn.silu, cond_cols)[1](grad_silu)[0]
    features_all = sinusoid(time_all, FREQ)
    onehot_all = (labels_all[:, None] == jnp.arange(CLASSES)[None, :]).astype(jnp.float32)
    grad_condition = jnp.dot(
        jnp.concatenate([features_all, onehot_all], 1).T, grad_cond, precision=highest_float_accuracy
    )


    def totals(kind, shape):
        both = [route.met(kind, i).astype(jnp.float32) for i in range(2)]
        return jnp.stack([shape(each[0] + each[1]) for each in both])

    def by_third(g):
        thirds = [g[:, i * local : (i + 1) * local] for i in range(3)]
        return jnp.transpose(jnp.stack(thirds), (1, 0, 2))

    grads = [
        totals(IN, by_third),
        totals(OUT, lambda g: g.T),
        totals(EXPAND, lambda g: g),
        totals(CONTRACT, lambda g: g.T),
        grad_modulation,
        grad_patch_table,
        grad_condition,
    ]
    square_small = jnp.sum(grad_patch_table * grad_patch_table) + jnp.sum(
        grad_condition * grad_condition
    )
    square_local = jnp.sum(grad_modulation * grad_modulation)
    square_local = square_local + (wide_index == 0).astype(jnp.float32) * square_small
    scalars = jnp.stack([square[0, 0], nce[0, 0], square_local])
    scalars = jnp.pad(scalars[None, :], ((0, 7), (0, 125)))
    mets = [route.met(kind, i) for i in range(2) for kind in (IN, OUT, EXPAND, CONTRACT)]
    (scalars_all,) = route.step(Norm(scalars, mets))
    sums = jnp.sum(scalars_all[:, 0], 0)
    grad_norm = jnp.sqrt(sums[2])
    factor = clip_norm / jnp.maximum(grad_norm, clip_norm)
    fresh = [
        adam(params[i], grads[i], moments[i], seconds[i], averages[i], factor) for i in range(7)
    ]
    loss_parts = jnp.stack([sums[0] / count_all, sums[1] / images])
    return (loss_parts, grad_norm) + tuple(fresh[i][k] for k in range(4) for i in range(7))


def solution(mesh):
    wide, narrow = mesh.devices.shape
    planes = wide // 2
    across = max(n for n in range(1, math.isqrt(planes) + 1) if planes % n == 0)
    grid = Mesh(mesh.devices.reshape(across, planes // across, 2, narrow // 2, 2), ALL)
    image_specs = (
        P(WIDE, None, None),
        P(WIDE, None, None),
        P(WIDE, None),
        P(WIDE),
        P(WIDE),
        P(WIDE),
        P(WIDE, None),
    )
    table_specs = (
        P(None, WIDE, None, NARROW),
        P(None, NARROW, WIDE),
        P(None, WIDE, NARROW),
        P(None, NARROW, WIDE),
        P(None, WIDE, None, NARROW),
        P(None, NARROW),
        P(None, NARROW),
    )
    return jax.shard_map(
        shards,
        mesh=grid,
        in_specs=image_specs + table_specs * 4,
        out_specs=(P(), P()) + table_specs * 4,
        check_vma=False,
    )
```
